32 devices in a mesh: ctx: 8 (over z, y), head: 4 (over x, core).
Axes of the slice: x: 2, y: 2, z: 4, core: 2. Of those that a mesh axis runs over, the one named last changes fastest.
Arguments:
- query_in: bfloat16 [1024, 2048], P('ctx', 'head'), may hold values from -6 to 6
- key_in: bfloat16 [1024, 2048], P('ctx', 'head'), may hold values from -6 to 6
- value_in: bfloat16 [1024, 4096], P('ctx', 'head'), may hold values from -6 to 6
- gate_in: bfloat16 [1024, 4096], P('ctx', 'head'), may hold values from -6 to 6
- conv_query: float32 [4, 2048], P(None, 'head'), may hold values from -3 to 3
- conv_key: float32 [4, 2048], P(None, 'head'), may hold values from -3 to 3
- conv_value: float32 [4, 4096], P(None, 'head'), may hold values from -3 to 3
- decay_in: float32 [32, 1024], P('head', 'ctx'), may hold values from -14 to 0.1
- beta_in: float32 [32, 1024], P('head', 'ctx'), may hold values from -2.5 to -1.5
- norm_gain: float32 [128], replicated, may hold values from 0.5 to 1.5
- doc_lengths: int32 [16], replicated, may hold values from 1 to 256, 1024 in all
- out_weight: bfloat16 [4096, 2048], P('head'), may hold values from -0.09375 to 0.09375
Outputs:
- projected: bfloat16 [2048, 1024], P('head', 'ctx')
The draws below stay inside these ranges and needn't reach their ends.
Inputs may be any that keep to these rules, and one draw needn't show every extreme that they name: `doc_lengths`: lengths of the 16 packed documents in packing order; they sum to 1024, and the longest has exactly 256 tokens.
All inputs are finite; a program needn't handle non-finite values.
Results may differ from the reference program's by a relative error of at most 0.017.
Values may be sent and summed in bfloat16 or wider, within the bound.
No kernel may reach another device: no remote copies, remote signals or barrier semaphores. Data moves between devices by JAX's collectives and lax.ppermute only.
A program may use at most 192 MiB of HBM per device.

```python
import math
import jax
import jax.numpy as jnp
import numpy as np
from jax import lax

D = 2048
VALUE_HEAD_COUNT = 32
HK = 16
DK = 128
DV = 128
KW = 4
SPAN = 64
TOKENS_PER_SHARD = 128
PACKED_TOKENS = 1024
DOCS = 16
MOST_DOC = 256
N_HEAD = 4


def draw_decay_in(key, part):
    random_subkeys = jax.random.split(key, 5)
    slow_heads = jax.random.bernoulli(random_subkeys[0], 0.5, (VALUE_HEAD_COUNT, 1))
    block_count = PACKED_TOKENS // TOKENS_PER_SHARD
    block_scale = jnp.exp(jax.random.uniform(random_subkeys[1], (VALUE_HEAD_COUNT, block_count, 1), jnp.float32, -0.7, 0.7))
    block_scale = jnp.broadcast_to(block_scale, (VALUE_HEAD_COUNT, block_count, TOKENS_PER_SHARD)).reshape(VALUE_HEAD_COUNT, PACKED_TOKENS)
    token_scale = jnp.exp(jax.random.uniform(random_subkeys[2], (VALUE_HEAD_COUNT, PACKED_TOKENS), jnp.float32, -0.7, 0.7))
    base_rate = jnp.where(slow_heads, 0.25 / MOST_DOC, 1.0 / 40.0)
    frequency = base_rate * block_scale * token_scale
    sudden_spike = jax.random.bernoulli(random_subkeys[3], 4.0 / PACKED_TOKENS, (VALUE_HEAD_COUNT, PACKED_TOKENS))
    spike_frequency = jax.random.uniform(random_subkeys[4], (VALUE_HEAD_COUNT, PACKED_TOKENS), jnp.float32, 0.25, 0.7)
    frequency = jnp.where(sudden_spike, spike_frequency, frequency)
    return jnp.log(jnp.expm1(frequency)).astype(jnp.float32)


def draw_key_in(key, part):
    random_subkeys = jax.random.split(key, 3)
    width = HK * DK
    signs = jnp.where(jax.random.bernoulli(random_subkeys[0], 0.5, (1, width)), 1.0, -1.0)
    offset = signs * jax.random.uniform(random_subkeys[1], (1, width), jnp.float32, 0.5, 2.5)
    noise = jax.random.normal(random_subkeys[2], (PACKED_TOKENS, width), jnp.float32)
    return jnp.clip(offset + noise, -6.0, 6.0).astype(jnp.bfloat16)


def steps_of(key, extent, cuts, least, largest):
    factor_of, own = 1.0, jax.random.fold_in(key, 6)
    for position, parts in cuts:
        steps = jnp.exp(jax.random.uniform(jax.random.fold_in(own, position), (parts,), jnp.float32, least / len(cuts), largest / len(cuts)))
        factor_of = factor_of * jnp.repeat(steps, extent[position] // parts).reshape([-1 if axis == position else 1 for axis in range(len(extent))])
    return factor_of


def length_profile(amount, total, most, lean):
    portions = [(1 << 20) // math.isqrt(rank ** lean) + 1 for rank in range(2, amount + 1)]
    spare, holding = total - most - (amount - 1), [1] * (amount - 1)
    while spare > 0:
        candidates = [i for i in range(amount - 1) if holding[i] < most]
        whole, remaining = sum([portions[i] for i in candidates]), spare
        for i in candidates:
            addition = min(most - holding[i], max(1, remaining * portions[i] // whole), spare)
            holding[i] = holding[i] + addition
            spare = spare - addition
    return np.array([most] + holding)


def uneven(key, count, total, bound, lean):
    if count == 2:
        one = jax.random.randint(key, (), max(1, total - bound), min(bound, total - 1) + 1)
        return jnp.stack([one, total - one])
    tallies = jnp.asarray(length_profile(count, total, bound, lean), jnp.int32)
    twos = (count - 1) // 2
    giver, taker = tallies[1:1 + 2 * twos:2], tallies[2:2 + 2 * twos:2]
    room = jnp.minimum(giver - 1, bound - taker)
    shifted = jax.random.randint(jax.random.fold_in(key, 1), (twos,), 0, 1 << 20) % (room + 1)
    tallies = tallies.at[1:1 + 2 * twos:2].set(giver - shifted).at[2:2 + 2 * twos:2].set(taker + shifted)
    return tallies[jax.random.permutation(jax.random.fold_in(key, 2), count)]


def normal_values(own_key, dims, scale, bound, cuts=(), kind=jnp.bfloat16):
    loudness = steps_of(own_key, dims, cuts, -0.22, 0.18) if cuts else 1.0
    values = jax.random.normal(own_key, dims, jnp.float32) * scale * loudness
    return jnp.minimum(jnp.maximum(values, -bound), bound).astype(kind)


def setup_inputs(seed: int = 0) -> dict:
    key_of = jax.random.split(jax.random.key(seed), 13)
    query_in = normal_values(key_of[0], (PACKED_TOKENS, HK * DK), 1.0, 6.0, ((0, 8), (1, 4)))
    key_in = draw_key_in(jax.random.fold_in(key_of[12], 71), 0)
    value_in = normal_values(key_of[2], (PACKED_TOKENS, VALUE_HEAD_COUNT * DV), 1.0, 6.0, ((0, 8), (1, 4)))
    gate_in = normal_values(key_of[3], (PACKED_TOKENS, VALUE_HEAD_COUNT * DV), 1.0, 6.0, ((0, 8), (1, 4)))
    conv_query = normal_values(key_of[4], (KW, HK * DK), KW ** -0.5, 3.0, ((1, 4),), jnp.float32)
    conv_key = normal_values(key_of[5], (KW, HK * DK), KW ** -0.5, 3.0, ((1, 4),), jnp.float32)
    conv_value = normal_values(key_of[6], (KW, VALUE_HEAD_COUNT * DV), KW ** -0.5, 3.0, ((1, 4),), jnp.float32)
    decay_in = draw_decay_in(jax.random.fold_in(key_of[12], 71), 0)
    beta_in = jnp.clip(-2.5 + 1.0 * jax.random.uniform(key_of[8], (VALUE_HEAD_COUNT, PACKED_TOKENS), jnp.float32) ** steps_of(key_of[8], (VALUE_HEAD_COUNT, PACKED_TOKENS), ((0, 4), (1, 8)), -0.2, 0.2), -2.5, -1.5)
    norm_gain = jnp.clip(1.0 + 0.1 * jax.random.normal(key_of[9], (DV,), jnp.float32), 0.5, 1.5)
    doc_lengths = uneven(key_of[10], DOCS, PACKED_TOKENS, MOST_DOC, 2).astype(jnp.int32)
    out_weight = normal_values(key_of[11], (VALUE_HEAD_COUNT * DV, D), (VALUE_HEAD_COUNT * DV) ** -0.5, 0.09375, ((0, 4),))
    return {"query_in": query_in, "key_in": key_in, "value_in": value_in, "gate_in": gate_in, "conv_query": conv_query, "conv_key": conv_key, "conv_value": conv_value, "decay_in": decay_in, "beta_in": beta_in, "norm_gain": norm_gain, "doc_lengths": doc_lengths, "out_weight": out_weight}


PRECISE = lax.Precision.HIGHEST

def shard_conv(before, current, weight, keep_masks):
    margin = weight.shape[0] - 1
    count_rows = current.shape[0]
    padded = jnp.concatenate([before, current], axis=0).astype(jnp.float32)
    summed = jnp.zeros((count_rows, current.shape[1]), jnp.float32)
    for offset in range(margin + 1):
        summed = summed + weight[offset][None, :] * padded[offset:offset + count_rows] * keep_masks[margin - offset][:, None]
    return jax.nn.silu(summed)

def unit_heads(vectors, head_count):
    reshaped = vectors.reshape(vectors.shape[0], head_count, -1)
    return reshaped / jnp.sqrt(lax.optimization_barrier(jnp.sum(reshaped * reshaped, axis=-1, keepdims=True)) + 1e-06)

def span_terms(queries, keys_unit, values, log_gamma, beta_values, resets):
    length = resets.shape[0]
    segment = jnp.cumsum(resets).astype(jnp.int32)
    cumulative = jnp.cumsum(log_gamma, axis=-1)
    row_index = jnp.arange(length, dtype=jnp.int32)[:, None]
    col_index = jnp.arange(length, dtype=jnp.int32)[None, :]
    same_doc = (segment[:, None] == segment[None, :]) & (row_index >= col_index)
    strict = same_doc & (row_index > col_index)
    log_ratio = cumulative[:, :, None] - cumulative[:, None, :]
    decay_pairs = jnp.exp(jnp.where(same_doc[None], log_ratio, -1e+30))
    key_gram = jnp.einsum('hid,hjd->hij', keys_unit, keys_unit, precision=PRECISE)
    lower_part = jnp.where(strict[None], beta_values[:, :, None] * key_gram * decay_pairs, 0.0)
    head_start = jnp.where(segment[None, :] == 0, jnp.exp(cumulative), 0.0)
    last_segment = segment[length - 1]
    to_end = jnp.where(segment[None, :] == last_segment, jnp.exp(cumulative[:, length - 1:] - cumulative), 0.0)
    through = jnp.where(last_segment == 0, jnp.exp(cumulative[:, length - 1]), 0.0)
    values_in = lax.linalg.triangular_solve(lower_part, beta_values[:, :, None] * values, left_side=True, lower=True, unit_diagonal=True)
    keys_in = lax.linalg.triangular_solve(lower_part, (beta_values * head_start)[:, :, None] * keys_unit, left_side=True, lower=True, unit_diagonal=True)
    scores = jnp.einsum('hid,hjd->hij', queries, keys_unit, precision=PRECISE)
    inside = jnp.where(same_doc[None], scores * decay_pairs, 0.0)
    return (values_in, keys_in, inside, head_start, to_end, through)

def reference(query_in, key_in, value_in, gate_in, conv_query, conv_key, conv_value, decay_in, beta_in, norm_gain, doc_lengths, out_weight):
    margin = KW - 1
    positions = jnp.arange(PACKED_TOKENS, dtype=jnp.int32)
    doc_starts = (jnp.cumsum(doc_lengths) - doc_lengths).astype(jnp.int32)
    start_flags = jnp.any(positions[:, None] == doc_starts[None, :], axis=1).astype(jnp.int32)
    running = jnp.concatenate([jnp.zeros((margin,), jnp.int32), jnp.cumsum(start_flags).astype(jnp.int32)])
    padded_query = jnp.concatenate([jnp.zeros((margin, HK * DK), jnp.bfloat16), query_in], axis=0)
    padded_key = jnp.concatenate([jnp.zeros((margin, HK * DK), jnp.bfloat16), key_in], axis=0)
    padded_value = jnp.concatenate([jnp.zeros((margin, VALUE_HEAD_COUNT * DV), jnp.bfloat16), value_in], axis=0)
    log_gamma = -jax.nn.softplus(decay_in)
    beta_values = jax.nn.sigmoid(beta_in)
    group_ratio = VALUE_HEAD_COUNT // HK

    def span_step(carried, span_index):
        first_row = (span_index * SPAN).astype(jnp.int32)

        def window(array):
            return lax.dynamic_slice_in_dim(array, first_row, SPAN + margin, 0)
        counts_here = window(running)
        keep_masks = [(counts_here[margin:] - counts_here[margin - lag_steps:margin - lag_steps + SPAN] == 0).astype(jnp.float32) for lag_steps in range(margin + 1)]
        resets = lax.dynamic_slice_in_dim(start_flags, first_row, SPAN, 0)
        rows_query = window(padded_query)
        rows_key = window(padded_key)
        rows_value = window(padded_value)
        queries = unit_heads(shard_conv(rows_query[:margin], rows_query[margin:], conv_query, keep_masks), HK)
        keys_unit = unit_heads(shard_conv(rows_key[:margin], rows_key[margin:], conv_key, keep_masks), HK)
        values = shard_conv(rows_value[:margin], rows_value[margin:], conv_value, keep_masks).reshape(SPAN, VALUE_HEAD_COUNT, DV)
        queries = jnp.repeat(queries, group_ratio, axis=1).transpose(1, 0, 2)
        keys_unit = jnp.repeat(keys_unit, group_ratio, axis=1).transpose(1, 0, 2)
        values = values.transpose(1, 0, 2)
        gamma_part = lax.dynamic_slice_in_dim(log_gamma, first_row, SPAN, 1)
        beta_part = lax.dynamic_slice_in_dim(beta_values, first_row, SPAN, 1)
        values_in, keys_in, inside, head_start, to_end, through = span_terms(queries, keys_unit, values, gamma_part, beta_part, resets)
        fresh_values = values_in - jnp.einsum('hcd,hde->hce', keys_in, carried, precision=PRECISE)
        result = jnp.einsum('hcd,hde->hce', queries * head_start[..., None], carried, precision=PRECISE) + jnp.einsum('hij,hje->hie', inside, fresh_values, precision=PRECISE)
        carried = through[:, None, None] * carried + jnp.einsum('hcd,hce->hde', keys_unit * to_end[..., None], fresh_values, precision=PRECISE)
        heads_out = result.transpose(1, 0, 2)
        gate_values = lax.dynamic_slice_in_dim(gate_in, first_row, SPAN, 0).astype(jnp.float32).reshape(SPAN, VALUE_HEAD_COUNT, DV)
        normed = heads_out / jnp.sqrt(lax.optimization_barrier(jnp.mean(heads_out * heads_out, axis=-1, keepdims=True)) + 1e-06) * norm_gain * jax.nn.silu(gate_values)
        return (carried, normed.reshape(SPAN, VALUE_HEAD_COUNT * DV).astype(jnp.bfloat16))
    zeros_state = jnp.zeros((VALUE_HEAD_COUNT, DK, DV), jnp.float32)
    _, mixed_blocks = lax.scan(span_step, zeros_state, jnp.arange(PACKED_TOKENS // SPAN, dtype=jnp.int32))
    mixed_rows = mixed_blocks.reshape(PACKED_TOKENS, VALUE_HEAD_COUNT * DV)
    group_cols = VALUE_HEAD_COUNT * DV // N_HEAD
    summed = jnp.zeros((PACKED_TOKENS, D), jnp.float32)
    for group_index in range(N_HEAD):
        low = group_index * group_cols
        partial_value = jnp.dot(mixed_rows[:, low:low + group_cols].astype(jnp.float32), out_weight[low:low + group_cols].astype(jnp.float32), preferred_element_type=jnp.float32).astype(jnp.bfloat16)
        partial_value = lax.optimization_barrier(partial_value)
        summed = summed + partial_value.astype(jnp.float32)
    return summed.T.astype(jnp.bfloat16)
```

```python
import jax
import jax.numpy as jnp
from jax import lax
from jax.experimental import pallas as pl
from jax.experimental.pallas import tpu as pltpu
from jax.sharding import PartitionSpec as P

DK = 128
DV = 128
EDGE = 16
F32 = jnp.float32
BF16 = jnp.bfloat16
VMEM_LIMIT = 48 * 1024 * 1024


def dot(a, b):
    return jnp.dot(a.astype(BF16), b.astype(BF16), preferred_element_type=F32)


def exact_dot(a, b):
    return jnp.dot(a, b, precision=lax.Precision.HIGHEST, preferred_element_type=F32)


def where_y(flag, a, b):
    return jnp.where(flag == 1, a, b)


def three_terms(value):
    high = value.astype(BF16)
    rest = value - high.astype(F32)
    middle = rest.astype(BF16)
    low = (rest - middle.astype(F32)).astype(BF16)
    return high, middle, low


def pack_kernel(q_ref, k_ref, v_ref, g_ref, decay_ref, beta_ref, pack_ref, edge_ref, own_edge_ref, gate_ref):
    y = lax.axis_index("ctx") % 2
    rows, key_width = q_ref.shape
    value_width = v_ref.shape[1]
    hk, hv = key_width // 2, value_width // 2
    heads = decay_ref.shape[0] // 2
    parts = ((q_ref, 0, hk), (k_ref, hk, hk), (v_ref, 2 * hk, hv))
    for ref, at, width in parts:
        other = where_y(y, ref[:, :width], ref[:, width:])
        pack_ref[0:rows, at : at + width] = other
        edge_ref[:, at : at + width] = other[rows - EDGE :]
        own_edge_ref[:, at : at + width] = where_y(y, ref[rows - EDGE :, width:], ref[rows - EDGE :, :width])
    gate_ref[...] = where_y(y, g_ref[:, :hv], g_ref[:, hv:])
    pack_ref[rows : rows + EDGE, :] = jnp.zeros((EDGE, pack_ref.shape[1]), BF16)
    at = 0
    for ref in (decay_ref, beta_ref):
        for term in three_terms(where_y(y, ref[0:heads], ref[heads:])):
            pack_ref[rows : rows + heads, at : at + rows] = term
            at += rows


def document_counts(doc_ref, base, rows):
    down = lax.broadcasted_iota(jnp.int32, (rows + 8, rows), 0) + (base - 8)
    along = lax.broadcasted_iota(jnp.int32, (8, rows), 1) + base
    docs = doc_ref.shape[0]

    def one(d, carried):
        start, count_down, count_along = carried
        count_down = count_down + (down >= start).astype(jnp.int32)
        count_along = count_along + (along >= start).astype(jnp.int32)
        return start + doc_ref[d], count_down, count_along

    state = (jnp.int32(0), jnp.zeros_like(down), jnp.zeros_like(along))
    if docs <= 16:
        for d in range(docs):
            state = one(d, state)
    else:
        state = lax.fori_loop(0, docs, one, state)
    return state[1], state[2]


def conv_silu(halo, current, weight, keeps):
    rows = current.shape[0]
    padded = jnp.concatenate([halo.astype(F32)[EDGE - 8 :], current.astype(F32)], axis=0)
    margin = weight.shape[0] - 1
    summed = weight[margin : margin + 1] * padded[8:]
    for lag in range(1, margin + 1):
        summed = summed + weight[margin - lag : margin - lag + 1] * padded[8 - lag : 8 - lag + rows] * keeps[lag]
    return summed / (1.0 + jnp.exp(-summed))


def unit(vectors):
    return vectors * lax.rsqrt(jnp.sum(vectors * vectors, axis=-1, keepdims=True) + 1e-6)


def block_terms(doc_ref, base, halo, q, k, v, weights, decay, beta_raw):
    rows = decay.shape[1]
    heads = decay.shape[0]
    key_heads = heads // 2
    seg_down, seg_along = document_counts(doc_ref, base, rows)
    seg = seg_down[8:]
    keeps = [None] + [(seg_down[8 - lag : 8 - lag + rows] == seg).astype(F32) for lag in (1, 2, 3)]
    before = seg_down[7:8]
    last = seg_down[rows + 7 : rows + 8]
    row = lax.broadcasted_iota(jnp.int32, (rows, rows), 0)
    col = lax.broadcasted_iota(jnp.int32, (rows, rows), 1)
    same = (seg == seg_along[0:1]) & (row >= col)

    log_gamma = -(jnp.maximum(decay, 0.0) + jnp.log1p(jnp.exp(-jnp.abs(decay))))
    beta = 1.0 / (1.0 + jnp.exp(-beta_raw))
    padded_gamma = jnp.concatenate([log_gamma, jnp.zeros((8 - heads, rows), F32)], axis=0)
    upper = (row <= col).astype(F32)
    sums = exact_dot(padded_gamma, upper)
    stacked = jnp.concatenate([sums[:heads], beta, jnp.zeros((rows - 2 * heads, rows), F32)], axis=0)
    columns = stacked.T

    queries = [unit(conv_silu(halo(0, g), q(g), weights(0, g), keeps)) for g in range(key_heads)]
    keys = [unit(conv_silu(halo(1, g), k(g), weights(1, g), keeps)) for g in range(key_heads)]
    values = [conv_silu(halo(2, g), v(g), weights(2, g), keeps) for g in range(heads)]
    keys_t = [key.T for key in keys]
    keys_t16 = [key.astype(BF16) for key in keys_t]
    grams = [dot(key, key_t) for key, key_t in zip(keys, keys_t16)]
    scores = [dot(query, key_t) for query, key_t in zip(queries, keys_t16)]

    lower, inside, rhs, starts, ends, throughs = [], [], [], [], [], []
    for h in range(heads):
        g = h // 2
        down = jnp.broadcast_to(columns[:, h : h + 1], (rows, rows))
        beta_down = jnp.broadcast_to(columns[:, heads + h : heads + h + 1], (rows, rows))
        along = sums[h : h + 1]
        end = jnp.broadcast_to(columns[rows - 1 : rows, h : h + 1], (1, rows))
        decays = jnp.exp(jnp.where(same, down - along, -1e30))
        lower.append(jnp.where(row > col, beta_down * grams[g] * decays, 0.0))
        inside.append((scores[g] * decays).astype(BF16))
        start = jnp.where(seg == before, jnp.exp(down), 0.0)
        starts.append((queries[g] * start).astype(BF16))
        rhs.append(
            jnp.concatenate([(beta_down * values[h]).astype(BF16), (beta_down * start * keys[g]).astype(BF16)], axis=1)
        )
        ends.append((keys_t[g] * jnp.where(seg_along[0:1] == last, jnp.exp(end - along), 0.0)).astype(BF16))
        throughs.append(jnp.where(last == before, jnp.exp(end), 0.0))

    small = 16
    eye = (row == col).astype(F32)
    power = [jnp.where(row // small == col // small, -x, 0.0) for x in lower]
    inverse = [eye + x for x in power]
    power = [x.astype(BF16) for x in power]
    reach = 2
    while reach < small:
        power = [dot(x, x).astype(BF16) for x in power]
        inverse = [x + dot(x, p) for x, p in zip(inverse, power)]
        reach *= 2
    reach = small
    while reach < rows:
        here = (row // (2 * reach) == col // (2 * reach)) & (row // reach != col // reach)
        moved = [dot(jnp.where(here, x, 0.0), i) for x, i in zip(lower, inverse)]
        inverse = [i - dot(i, m) for i, m in zip(inverse, moved)]
        reach *= 2
    solved = [dot(i, r).astype(BF16) for i, r in zip(inverse, rhs)]
    ended = [dot(e, s) for e, s in zip(ends, solved)]
    states = [e[:, :DV] for e in ended]
    maps = [t * eye - e[:, DV:] for t, e in zip(throughs, ended)]
    return states, maps, inside, solved, starts


def own_kernel(doc_ref, q_ref, k_ref, v_ref, cq_ref, ck_ref, cv_ref, decay_ref, beta_ref, halo_ref,
               state_ref, map_ref, out_ref, through_ref):
    ctx = lax.axis_index("ctx")
    y = ctx % 2
    rows = q_ref.shape[0]
    heads = decay_ref.shape[0] // 2
    widths = (q_ref.shape[1] // 2, k_ref.shape[1] // 2, v_ref.shape[1] // 2)
    at = (0, widths[0], widths[0] + widths[1])

    def half(ref, which, g):
        low = slice(g * 128, g * 128 + 128)
        high = slice(widths[which] + g * 128, widths[which] + g * 128 + 128)
        return where_y(y, ref[:, high], ref[:, low])

    weight_refs = (cq_ref, ck_ref, cv_ref)
    states, maps, inside, solved, starts = block_terms(
        doc_ref,
        ctx * rows,
        lambda which, g: halo_ref[:, at[which] + g * 128 : at[which] + g * 128 + 128],
        lambda g: half(q_ref, 0, g),
        lambda g: half(k_ref, 1, g),
        lambda g: half(v_ref, 2, g),
        lambda which, g: half(weight_refs[which], which, g),
        where_y(y, decay_ref[heads:], decay_ref[:heads]),
        where_y(y, beta_ref[heads:], beta_ref[:heads]),
    )
    results = [dot(i, s) for i, s in zip(inside, solved)]
    for h in range(heads):
        state_ref[h] = states[h]
        map_ref[h] = maps[h].astype(BF16)
        out_ref[:, h * DV : h * DV + DV] = results[h][:, :DV]
        through_ref[:, h * DK : h * DK + DK] = (starts[h].astype(F32) - results[h][:, DV:]).astype(BF16)


def peer_kernel(hops, doc_ref, pack_ref, own_edge_ref, edge_ref, cq_ref, ck_ref, cv_ref, own_state_ref, own_map_ref,
                state_ref, map_ref, inside_ref, solved_ref, start_ref, end_ref, *pair_map_ref):
    ctx = lax.axis_index("ctx")
    y = ctx % 2
    rows = pack_ref.shape[0] - EDGE
    heads = own_state_ref.shape[0]
    widths = (cq_ref.shape[1] // 2, ck_ref.shape[1] // 2, cv_ref.shape[1] // 2)
    at = (0, widths[0], widths[0] + widths[1])
    weight_refs = (cq_ref, ck_ref, cv_ref)

    def columns(which, g):
        return slice(at[which] + g * 128, at[which] + g * 128 + 128)

    def weights(which, g):
        ref, low = weight_refs[which], g * 128
        return where_y(y, ref[:, widths[which] + low : widths[which] + low + 128], ref[:, low : low + 128])

    gates = [
        sum(pack_ref[rows : rows + heads, (3 * part + i) * rows : (3 * part + i + 1) * rows].astype(F32) for i in range(3))
        for part in range(2)
    ]
    states, maps, inside, solved, starts = block_terms(
        doc_ref,
        (ctx + 1 - 2 * y) * rows,
        lambda which, g: where_y(y, edge_ref[:, columns(which, g)], own_edge_ref[:, columns(which, g)]),
        lambda g: pack_ref[0:rows, columns(0, g)],
        lambda g: pack_ref[0:rows, columns(1, g)],
        lambda g: pack_ref[0:rows, columns(2, g)],
        weights,
        gates[0],
        gates[1],
    )
    for h in range(heads):
        own_state, own_map = own_state_ref[h], own_map_ref[h]
        maps16 = maps[h].astype(BF16)
        state_0, state_1 = where_y(y, states[h], own_state), where_y(y, own_state, states[h])
        map_0, map_1 = where_y(y, maps16, own_map), where_y(y, own_map, maps16)
        end_ref[h] = (state_1 + dot(map_1, state_0)).astype(BF16)
        if hops > 1:
            pair_map_ref[0][h] = dot(map_1, map_0).astype(BF16)
    for h in range(heads):
        state_ref[h] = states[h]
        map_ref[h] = maps[h].astype(BF16)
        inside_ref[h] = inside[h]
        solved_ref[h] = solved[h]
        start_ref[:, h * DK : h * DK + DK] = starts[h]


def local_kernel(own_state_ref, own_map_ref, own_out_ref, own_through_ref, state_ref, map_ref, inside_ref, solved_ref,
                 start_ref, out_ref, through_ref):
    y = lax.axis_index("ctx") % 2
    rows = own_out_ref.shape[0]
    heads = own_state_ref.shape[0]
    results = [dot(inside_ref[h], solved_ref[h]) for h in range(heads)]
    for h in range(heads):
        lanes = slice(h * DV, h * DV + DV)
        own_out, own_through = own_out_ref[:, lanes], own_through_ref[:, lanes]
        out = results[h][:, :DV]
        through = (start_ref[:, lanes].astype(F32) - results[h][:, DV:]).astype(BF16)
        state_0 = where_y(y, state_ref[h], own_state_ref[h]).astype(BF16)
        map_0 = where_y(y, map_ref[h], own_map_ref[h])
        through_1 = where_y(y, own_through, through)
        more = dot(through_1, jnp.concatenate([state_0, map_0], axis=1))
        extra, moved = more[:, :DV], more[:, DV:].astype(BF16)
        out_ref[0:rows, lanes] = own_out + where_y(y, extra, jnp.zeros_like(extra))
        out_ref[rows:, lanes] = out + where_y(y, jnp.zeros_like(extra), extra)
        through_ref[0:rows, lanes] = where_y(y, moved, own_through)
        through_ref[rows:, lanes] = where_y(y, through, moved)


def project_kernel(out_ref, through_ref, enter_ref, gate_ref, peer_gate_ref, gain_ref, weight_ref, send_ref, keep_ref,
                   weight_vmem, sems):
    y = lax.axis_index("ctx") % 2
    head = lax.axis_index("head")
    core, x = head % 2, head // 2
    heads = enter_ref.shape[0]
    rows = gate_ref.shape[0]
    depth = weight_vmem.shape[1]
    width = weight_vmem.shape[2]
    copies = []
    for i, (c, xx) in enumerate(((1 - core, x), (1 - core, 1 - x), (core, x), (core, 1 - x))):
        copies.append(
            pltpu.make_async_copy(
                weight_ref.at[
                    pl.ds(pl.multiple_of(y * depth, depth), depth),
                    pl.ds(pl.multiple_of((xx * 2 + c) * width, width), width),
                ],
                weight_vmem.at[i],
                sems.at[i],
            )
        )
    for copy in copies:
        copy.start()
    mixed = []
    for h in range(heads):
        lanes = slice(h * DV, h * DV + DV)
        high = slice(heads * DV + h * DV, heads * DV + h * DV + DV)
        o = out_ref[:, lanes] + dot(through_ref[:, lanes], enter_ref[h])
        gate = jnp.concatenate([where_y(y, gate_ref[:, high], gate_ref[:, lanes]), peer_gate_ref[:, lanes]], axis=0)
        gate = gate.astype(F32)
        scale = lax.rsqrt(jnp.mean(o * o, axis=-1, keepdims=True) + 1e-6)
        mixed.append((o * scale * gain_ref[...] * (gate / (1.0 + jnp.exp(-gate)))).astype(BF16))
    mixed = jnp.concatenate(mixed, axis=1)
    for i, copy in enumerate(copies):
        copy.wait()
        to_ref = (send_ref, keep_ref)[i // 2]
        to_ref[:, (i % 2) * width : (i % 2 + 1) * width] = jnp.dot(
            mixed, weight_vmem[i], preferred_element_type=F32
        ).astype(BF16)


def core_sum_kernel(keep_ref, got_ref, mine_ref, x_ref, y_ref, xy_ref):
    rows, width = mine_ref.shape
    for ref, r, c in ((xy_ref, 1, 1), (x_ref, 0, 1), (y_ref, 1, 0), (mine_ref, 0, 0)):
        at = (slice(r * rows, r * rows + rows), slice(c * width, c * width + width))
        ref[...] = (keep_ref[at].astype(F32) + got_ref[at].astype(F32)).astype(ref.dtype)


def last_kernel(mine_ref, x_ref, y_ref, xy_ref, out_ref):
    total = mine_ref[...] + x_ref[...].astype(F32) + (y_ref[...].astype(F32) + xy_ref[...].astype(F32))
    out_ref[...] = total.T.astype(BF16)


def call(kernel, outs, args, name, smem=0, any_space=(), scratch=(), flops=0, moved=0):
    space = [
        pl.BlockSpec(memory_space=pltpu.SMEM if i < smem else pl.ANY if i in any_space else pltpu.VMEM)
        for i in range(len(args))
    ]
    return pl.pallas_call(
        kernel,
        out_shape=[jax.ShapeDtypeStruct(shape, kind) for shape, kind in outs],
        in_specs=space,
        out_specs=[pl.BlockSpec(memory_space=pltpu.VMEM)] * len(outs),
        scratch_shapes=list(scratch),
        compiler_params=pltpu.CompilerParams(vmem_limit_bytes=VMEM_LIMIT),
        cost_estimate=pl.CostEstimate(flops=flops, bytes_accessed=moved, transcendentals=0),
        name=name,
    )(*args)


def body(
    query_in,
    key_in,
    value_in,
    gate_in,
    conv_query,
    conv_key,
    conv_value,
    decay_in,
    beta_in,
    norm_gain,
    doc_lengths,
    out_weight,
):
    rows = query_in.shape[0]
    ctx_count, head_count = lax.axis_size("ctx"), lax.axis_size("head")
    heads = decay_in.shape[0] // 2
    half_width = query_in.shape[1] + value_in.shape[1] // 2
    value_width = value_in.shape[1] // 2
    width = out_weight.shape[1] // head_count
    longest = ctx_count * rows // 4
    hops = -(-(longest - 1) // (2 * rows))

    swap = [(i, i ^ 1) for i in range(ctx_count)]
    ahead_1 = [(i, (i + 1) % ctx_count) for i in range(ctx_count)]
    ahead_2 = [(i, (i + 2) % ctx_count) for i in range(ctx_count)]

    pack, edge, own_edge, gate_out = call(
        pack_kernel,
        [((rows + EDGE, half_width), BF16), ((EDGE, half_width), BF16), ((EDGE, half_width), BF16), ((rows, value_width), BF16)],
        (query_in, key_in, value_in, gate_in, decay_in, beta_in),
        "pack",
    )
    got_edge = lax.ppermute(edge, "ctx", ahead_1)
    got_far_edge = lax.ppermute(own_edge, "ctx", ahead_2)
    got_pack = lax.ppermute(pack, "ctx", swap)

    square = (heads, DK, DV)
    own_state, own_map, own_out, own_through = call(
        own_kernel,
        [(square, F32), (square, BF16), ((rows, value_width), F32), ((rows, value_width), BF16)],
        (doc_lengths, query_in, key_in, value_in, conv_query, conv_key, conv_value, decay_in, beta_in, got_edge),
        "own_terms",
        smem=1,
        flops=2_000_000_000,
        moved=4_000_000,
    )
    peer = call(
        lambda *refs: peer_kernel(hops, *refs),
        [
            (square, F32),
            (square, BF16),
            ((heads, rows, rows), BF16),
            ((heads, rows, DK + DV), BF16),
            ((rows, value_width), BF16),
            (square, BF16),
        ]
        + ([(square, BF16)] if hops > 1 else []),
        (doc_lengths, got_pack, own_edge, got_far_edge, conv_query, conv_key, conv_value, own_state, own_map),
        "peer_terms",
        smem=1,
        flops=2_000_000_000,
        moved=4_000_000,
    )
    state, map_, inside, solved, start, end = peer[:6]
    gate_out, end = lax.optimization_barrier((gate_out, end))
    entering = lax.ppermute(end, "ctx", ahead_2)
    for _ in range(hops - 1):
        moved = jnp.einsum("hij,hjk->hik", peer[6], entering, preferred_element_type=F32)
        entering = lax.ppermute((end.astype(F32) + moved).astype(BF16), "ctx", ahead_2)
    got_gate = lax.ppermute(gate_out, "ctx", swap)
    out, through = call(
        local_kernel,
        [((2 * rows, value_width), F32), ((2 * rows, value_width), BF16)],
        (own_state, own_map, own_out, own_through, state, map_, inside, solved, start),
        "local_outputs",
        flops=1_000_000_000,
        moved=4_000_000,
    )
    send, keep = call(
        project_kernel,
        [((2 * rows, 2 * width), BF16), ((2 * rows, 2 * width), BF16)],
        (out, through, entering, gate_in, got_gate, norm_gain.reshape(1, DV), out_weight),
        "project",
        any_space=(6,),
        scratch=(pltpu.VMEM((4, value_width, width), BF16), pltpu.SemaphoreType.DMA((4,))),
    )
    got = lax.ppermute(send, "head", [(i, i ^ 1) for i in range(head_count)])
    mine, to_x, to_y, to_xy = call(
        core_sum_kernel,
        [((rows, width), F32), ((rows, width), BF16), ((rows, width), BF16), ((rows, width), BF16)],
        (keep, got),
        "core_sum",
    )
    both = [
        (c * head_count + h, (c ^ 1) * head_count + (h ^ 2)) for c in range(ctx_count) for h in range(head_count)
    ]
    got_xy = lax.ppermute(to_xy, ("ctx", "head"), both)
    got_x = lax.ppermute(to_x, "head", [(i, i ^ 2) for i in range(head_count)])
    got_y = lax.ppermute(to_y, "ctx", swap)
    (projected,) = call(
        last_kernel, [((width, rows), BF16)], (mine, got_x, got_y, got_xy), "last_sum"
    )
    return projected


def solution(mesh):
    return jax.shard_map(
        body,
        mesh=mesh,
        in_specs=(
            P("ctx", "head"),
            P("ctx", "head"),
            P("ctx", "head"),
            P("ctx", "head"),
            P(None, "head"),
            P(None, "head"),
            P(None, "head"),
            P("head", "ctx"),
            P("head", "ctx"),
            P(),
            P(),
            P("head", None),
        ),
        out_specs=P("head", "ctx"),
        check_vma=False,
    )
```

```python
import jax
import jax.numpy as jnp
from jax import lax
from jax.experimental import pallas as pl
from jax.experimental.pallas import tpu as pltpu
from jax.sharding import PartitionSpec as P

DK = 128
DV = 128
EDGE = 16
F32 = jnp.float32
BF16 = jnp.bfloat16
VMEM_LIMIT = 48 * 1024 * 1024


def dot(a, b):
    return jnp.dot(a.astype(BF16), b.astype(BF16), preferred_element_type=F32)


def exact_dot(a, b):
    return jnp.dot(a, b, precision=lax.Precision.HIGHEST, preferred_element_type=F32)


def where_y(flag, a, b):
    return jnp.where(flag == 1, a, b)


def three_terms(value):
    high = value.astype(BF16)
    rest = value - high.astype(F32)
    middle = rest.astype(BF16)
    low = (rest - middle.astype(F32)).astype(BF16)
    return high, middle, low


def pack_kernel(q_ref, k_ref, v_ref, g_ref, cq_ref, ck_ref, cv_ref, decay_ref, beta_ref,
                edge_ref, own_edge_ref, pack_ref, gate_ref, own_ref, weight_ref, gates_ref, own_gate_ref,
                raw_gates, sems):
    y = lax.axis_index("ctx") % 2
    rows = q_ref.shape[0]
    heads = decay_ref.shape[0] // 2
    started = []

    def copy(source, target):
        one = pltpu.make_async_copy(source, target, sems.at[len(started)])
        one.start()
        started.append(one)

    def columns(ref, which):
        width = ref.shape[1] // 2
        return pl.ds(pl.multiple_of(which * width, width), width)

    copy(decay_ref, raw_gates.at[0])
    copy(beta_ref, raw_gates.at[1])
    at = 0
    for ref, weights in ((q_ref, cq_ref), (k_ref, ck_ref), (v_ref, cv_ref)):
        width = ref.shape[1] // 2
        here = pl.ds(at, width)
        tail = pl.ds(rows - EDGE, EDGE)
        copy(ref.at[tail, columns(ref, 1 - y)], edge_ref.at[:, here])
        copy(ref.at[tail, columns(ref, y)], own_edge_ref.at[:, here])
        copy(ref.at[:, columns(ref, 1 - y)], pack_ref.at[pl.ds(0, rows), here])
        copy(ref.at[:, columns(ref, y)], own_ref.at[:, here])
        copy(weights.at[:, columns(ref, y)], weight_ref.at[:, here])
        at += width
    copy(g_ref.at[:, columns(g_ref, 1 - y)], gate_ref)
    copy(g_ref.at[:, columns(g_ref, y)], own_gate_ref)
    pack_ref[rows : rows + EDGE, :] = jnp.zeros((EDGE, pack_ref.shape[1]), BF16)
    started[0].wait()
    started[1].wait()
    at = 0
    for i in range(2):
        raw = raw_gates[i]
        gates_ref[i * heads : i * heads + heads] = where_y(y, raw[heads:], raw[:heads])
        for term in three_terms(where_y(y, raw[:heads], raw[heads:])):
            pack_ref[rows : rows + heads, at : at + rows] = term
            at += rows
    for one in started[2:]:
        one.wait()


def document_counts(doc_ref, base, rows):
    down = lax.broadcasted_iota(jnp.int32, (rows + 8, rows), 0) + (base - 8)
    along = lax.broadcasted_iota(jnp.int32, (8, rows), 1) + base
    docs = doc_ref.shape[0]

    def one(d, carried):
        start, count_down, count_along = carried
        count_down = count_down + (down >= start).astype(jnp.int32)
        count_along = count_along + (along >= start).astype(jnp.int32)
        return start + doc_ref[d], count_down, count_along

    state = (jnp.int32(0), jnp.zeros_like(down), jnp.zeros_like(along))
    if docs <= 16:
        for d in range(docs):
            state = one(d, state)
    else:
        state = lax.fori_loop(0, docs, one, state)
    return state[1], state[2]


def conv_silu(halo, current, weight, keeps):
    rows = current.shape[0]
    padded = jnp.concatenate([halo.astype(F32)[EDGE - 8 :], current.astype(F32)], axis=0)
    margin = weight.shape[0] - 1
    summed = weight[margin : margin + 1] * padded[8:]
    for lag in range(1, margin + 1):
        summed = summed + weight[margin - lag : margin - lag + 1] * padded[8 - lag : 8 - lag + rows] * keeps[lag]
    return summed / (1.0 + jnp.exp(-summed))


def unit(vectors):
    return vectors * lax.rsqrt(jnp.sum(vectors * vectors, axis=-1, keepdims=True) + 1e-6)


def block_terms(doc_ref, base, halo, q, k, v, weights, decay, beta_raw):
    rows = decay.shape[1]
    heads = decay.shape[0]
    key_heads = heads // 2
    seg_down, seg_along = document_counts(doc_ref, base, rows)
    seg = seg_down[8:]
    keeps = [None] + [(seg_down[8 - lag : 8 - lag + rows] == seg).astype(F32) for lag in (1, 2, 3)]
    before = seg_down[7:8]
    last = seg_down[rows + 7 : rows + 8]
    row = lax.broadcasted_iota(jnp.int32, (rows, rows), 0)
    col = lax.broadcasted_iota(jnp.int32, (rows, rows), 1)
    same = (seg == seg_along[0:1]) & (row >= col)

    log_gamma = -(jnp.maximum(decay, 0.0) + jnp.log1p(jnp.exp(-jnp.abs(decay))))
    beta = 1.0 / (1.0 + jnp.exp(-beta_raw))
    padded_gamma = jnp.concatenate([log_gamma, jnp.zeros((8 - heads, rows), F32)], axis=0)
    upper = (row <= col).astype(F32)
    sums = exact_dot(padded_gamma, upper)
    stacked = jnp.concatenate([sums[:heads], beta, jnp.zeros((rows - 2 * heads, rows), F32)], axis=0)
    columns = stacked.T

    queries = [unit(conv_silu(halo(0, g), q(g), weights(0, g), keeps)) for g in range(key_heads)]
    keys = [unit(conv_silu(halo(1, g), k(g), weights(1, g), keeps)) for g in range(key_heads)]
    values = [conv_silu(halo(2, g), v(g), weights(2, g), keeps) for g in range(heads)]
    keys_t = [key.T for key in keys]
    keys_t16 = [key.astype(BF16) for key in keys_t]
    grams = [dot(key, key_t) for key, key_t in zip(keys, keys_t16)]
    scores = [dot(query, key_t) for query, key_t in zip(queries, keys_t16)]

    lower, inside, rhs, starts, ends, throughs = [], [], [], [], [], []
    for h in range(heads):
        g = h // 2
        down = jnp.broadcast_to(columns[:, h : h + 1], (rows, rows))
        beta_down = jnp.broadcast_to(columns[:, heads + h : heads + h + 1], (rows, rows))
        along = sums[h : h + 1]
        end = jnp.broadcast_to(columns[rows - 1 : rows, h : h + 1], (1, rows))
        decays = jnp.exp(jnp.where(same, down - along, -1e30))
        lower.append(jnp.where(row > col, beta_down * grams[g] * decays, 0.0))
        inside.append((scores[g] * decays).astype(BF16))
        start = jnp.where(seg == before, jnp.exp(down), 0.0)
        starts.append((queries[g] * start).astype(BF16))
        rhs.append(
            jnp.concatenate([(beta_down * values[h]).astype(BF16), (beta_down * start * keys[g]).astype(BF16)], axis=1)
        )
        ends.append((keys_t[g] * jnp.where(seg_along[0:1] == last, jnp.exp(end - along), 0.0)).astype(BF16))
        throughs.append(jnp.where(last == before, jnp.exp(end), 0.0))

    small = 16
    eye = (row == col).astype(F32)
    power = [jnp.where(row // small == col // small, -x, 0.0) for x in lower]
    inverse = [eye + x for x in power]
    power = [x.astype(BF16) for x in power]
    reach = 2
    while reach < small:
        power = [dot(x, x).astype(BF16) for x in power]
        inverse = [x + dot(x, p) for x, p in zip(inverse, power)]
        reach *= 2
    reach = small
    while reach < rows:
        here = (row // (2 * reach) == col // (2 * reach)) & (row // reach != col // reach)
        moved = [dot(jnp.where(here, x, 0.0), i) for x, i in zip(lower, inverse)]
        inverse = [i - dot(i, m) for i, m in zip(inverse, moved)]
        reach *= 2
    solved = [dot(i, r).astype(BF16) for i, r in zip(inverse, rhs)]
    ended = [dot(e, s) for e, s in zip(ends, solved)]
    states = [e[:, :DV] for e in ended]
    maps = [t * eye - e[:, DV:] for t, e in zip(throughs, ended)]
    return states, maps, inside, solved, starts


def groups(heads):
    at = (0, heads // 2 * DK, heads * DK)
    return lambda which, g: slice(at[which] + g * 128, at[which] + g * 128 + 128)


def own_kernel(doc_hbm, own_ref, weight_ref, gates_ref, halo_ref,
               state_ref, map_ref, out_ref, through_ref, doc_ref, sem):
    copy = pltpu.make_async_copy(doc_hbm, doc_ref, sem)
    copy.start()
    copy.wait()
    rows = own_ref.shape[0]
    heads = gates_ref.shape[0] // 2
    columns = groups(heads)
    states, maps, inside, solved, starts = block_terms(
        doc_ref,
        lax.axis_index("ctx") * rows,
        lambda which, g: halo_ref[:, columns(which, g)],
        lambda g: own_ref[:, columns(0, g)],
        lambda g: own_ref[:, columns(1, g)],
        lambda g: own_ref[:, columns(2, g)],
        lambda which, g: weight_ref[:, columns(which, g)],
        gates_ref[0:heads],
        gates_ref[heads:],
    )
    results = [dot(i, s) for i, s in zip(inside, solved)]
    for h in range(heads):
        state_ref[h] = states[h]
        map_ref[h] = maps[h].astype(BF16)
        out_ref[:, h * DV : h * DV + DV] = results[h][:, :DV]
        through_ref[:, h * DK : h * DK + DK] = (starts[h].astype(F32) - results[h][:, DV:]).astype(BF16)


def peer_kernel(doc_hbm, pack_ref, own_edge_ref, edge_ref, weight_ref, own_state_ref, own_map_ref,
                state_ref, map_ref, inside_ref, solved_ref, start_ref, end_ref, *rest):
    *pair_map_ref, doc_ref, sem = rest
    copy = pltpu.make_async_copy(doc_hbm, doc_ref, sem)
    copy.start()
    copy.wait()
    ctx = lax.axis_index("ctx")
    y = ctx % 2
    rows = pack_ref.shape[0] - EDGE
    heads = own_state_ref.shape[0]
    columns = groups(heads)
    gates = [
        sum(pack_ref[rows : rows + heads, (3 * part + i) * rows : (3 * part + i + 1) * rows].astype(F32) for i in range(3))
        for part in range(2)
    ]
    states, maps, inside, solved, starts = block_terms(
        doc_ref,
        (ctx + 1 - 2 * y) * rows,
        lambda which, g: where_y(y, edge_ref[:, columns(which, g)], own_edge_ref[:, columns(which, g)]),
        lambda g: pack_ref[0:rows, columns(0, g)],
        lambda g: pack_ref[0:rows, columns(1, g)],
        lambda g: pack_ref[0:rows, columns(2, g)],
        lambda which, g: weight_ref[:, columns(which, g)],
        gates[0],
        gates[1],
    )
    for h in range(heads):
        own_state, own_map = own_state_ref[h], own_map_ref[h]
        maps16 = maps[h].astype(BF16)
        state_0, state_1 = where_y(y, states[h], own_state), where_y(y, own_state, states[h])
        map_0, map_1 = where_y(y, maps16, own_map), where_y(y, own_map, maps16)
        end_ref[h] = (state_1 + dot(map_1, state_0)).astype(BF16)
        if pair_map_ref:
            pair_map_ref[0][h] = dot(map_1, map_0).astype(BF16)
    for h in range(heads):
        state_ref[h] = states[h]
        map_ref[h] = maps[h].astype(BF16)
        inside_ref[h] = inside[h]
        solved_ref[h] = solved[h]
        start_ref[:, h * DK : h * DK + DK] = starts[h]


def local_kernel(own_state_ref, own_map_ref, own_out_ref, own_through_ref, state_ref, map_ref, inside_ref, solved_ref,
                 start_ref, weight_hbm, out_ref, through_ref, weight_ref, sems):
    y = lax.axis_index("ctx") % 2
    head = lax.axis_index("head")
    core, x = head % 2, head // 2
    depth, width = weight_ref.shape[1:]
    copies = []
    for i, (c, xx) in enumerate(((1 - core, x), (1 - core, 1 - x), (core, x), (core, 1 - x))):
        source = weight_hbm.at[
            pl.ds(pl.multiple_of(y * depth, depth), depth), pl.ds(pl.multiple_of((xx * 2 + c) * width, width), width)
        ]
        copies.append(pltpu.make_async_copy(source, weight_ref.at[i], sems.at[i]))
        copies[-1].start()
    rows = own_out_ref.shape[0]
    heads = own_state_ref.shape[0]
    results = [dot(inside_ref[h], solved_ref[h]) for h in range(heads)]
    for h in range(heads):
        lanes = slice(h * DV, h * DV + DV)
        own_out, own_through = own_out_ref[:, lanes], own_through_ref[:, lanes]
        out = results[h][:, :DV]
        through = (start_ref[:, lanes].astype(F32) - results[h][:, DV:]).astype(BF16)
        state_0 = where_y(y, state_ref[h], own_state_ref[h]).astype(BF16)
        map_0 = where_y(y, map_ref[h], own_map_ref[h])
        through_1 = where_y(y, own_through, through)
        more = dot(through_1, jnp.concatenate([state_0, map_0], axis=1))
        extra, moved = more[:, :DV], more[:, DV:].astype(BF16)
        out_ref[0:rows, lanes] = own_out + where_y(y, extra, jnp.zeros_like(extra))
        out_ref[rows:, lanes] = out + where_y(y, jnp.zeros_like(extra), extra)
        through_ref[0:rows, lanes] = where_y(y, moved, own_through)
        through_ref[rows:, lanes] = where_y(y, through, moved)
    for copy in copies:
        copy.wait()


def project_kernel(out_ref, through_ref, enter_ref, gate_ref, peer_gate_ref, gain_ref, weight_ref, send_ref, keep_ref):
    heads = enter_ref.shape[0]
    width = weight_ref.shape[2]
    mixed = []
    for h in range(heads):
        lanes = slice(h * DV, h * DV + DV)
        o = out_ref[:, lanes] + dot(through_ref[:, lanes], enter_ref[h])
        gate = jnp.concatenate([gate_ref[:, lanes], peer_gate_ref[:, lanes]], axis=0).astype(F32)
        scale = lax.rsqrt(jnp.mean(o * o, axis=-1, keepdims=True) + 1e-6)
        mixed.append((o * scale * gain_ref[...] * (gate / (1.0 + jnp.exp(-gate)))).astype(BF16))
    mixed = jnp.concatenate(mixed, axis=1)
    for i in range(4):
        to_ref = (send_ref, keep_ref)[i // 2]
        to_ref[:, (i % 2) * width : (i % 2 + 1) * width] = jnp.dot(
            mixed, weight_ref[i], preferred_element_type=F32
        ).astype(BF16)


def core_sum_kernel(keep_ref, got_ref, mine_ref, x_ref, y_ref, xy_ref):
    rows, width = mine_ref.shape
    for ref, r, c in ((xy_ref, 1, 1), (x_ref, 0, 1), (y_ref, 1, 0), (mine_ref, 0, 0)):
        at = (slice(r * rows, r * rows + rows), slice(c * width, c * width + width))
        ref[...] = (keep_ref[at].astype(F32) + got_ref[at].astype(F32)).astype(ref.dtype)


def last_kernel(mine_ref, x_ref, y_ref, xy_ref, out_ref):
    total = mine_ref[...] + x_ref[...].astype(F32) + (y_ref[...].astype(F32) + xy_ref[...].astype(F32))
    out_ref[...] = total.T.astype(BF16)


def call(kernel, outs, args, name, hbm=(), scratch=(), flops=0, moved=0):
    space = [pl.BlockSpec(memory_space=pltpu.HBM if i in hbm else pltpu.VMEM) for i in range(len(args))]
    args = [pltpu.with_memory_space_constraint(arg, pltpu.HBM) if i in hbm else arg for i, arg in enumerate(args)]
    return pl.pallas_call(
        kernel,
        out_shape=[jax.ShapeDtypeStruct(shape, kind) for shape, kind in outs],
        in_specs=space,
        out_specs=[pl.BlockSpec(memory_space=pltpu.VMEM)] * len(outs),
        scratch_shapes=list(scratch),
        compiler_params=pltpu.CompilerParams(vmem_limit_bytes=VMEM_LIMIT),
        cost_estimate=pl.CostEstimate(flops=flops, bytes_accessed=moved, transcendentals=0),
        name=name,
    )(*args)


def body(
    query_in,
    key_in,
    value_in,
    gate_in,
    conv_query,
    conv_key,
    conv_value,
    decay_in,
    beta_in,
    norm_gain,
    doc_lengths,
    out_weight,
):
    rows = query_in.shape[0]
    ctx_count, head_count = lax.axis_size("ctx"), lax.axis_size("head")
    heads = decay_in.shape[0] // 2
    half_width = query_in.shape[1] + value_in.shape[1] // 2
    value_width = value_in.shape[1] // 2
    width = out_weight.shape[1] // head_count
    longest = ctx_count * rows // 4
    hops = -(-(longest - 1) // (2 * rows))

    swap = [(i, i ^ 1) for i in range(ctx_count)]
    ahead_1 = [(i, (i + 1) % ctx_count) for i in range(ctx_count)]
    ahead_2 = [(i, (i + 2) % ctx_count) for i in range(ctx_count)]

    edge, own_edge, pack, gate_out, own, weights, gates, own_gate = call(
        pack_kernel,
        [
            ((EDGE, half_width), BF16),
            ((EDGE, half_width), BF16),
            ((rows + EDGE, half_width), BF16),
            ((rows, value_width), BF16),
            ((rows, half_width), BF16),
            ((conv_query.shape[0], half_width), F32),
            ((2 * heads, rows), F32),
            ((rows, value_width), BF16),
        ],
        (query_in, key_in, value_in, gate_in, conv_query, conv_key, conv_value, decay_in, beta_in),
        "pack",
        hbm=range(9),
        scratch=(pltpu.VMEM((2,) + decay_in.shape, F32), pltpu.SemaphoreType.DMA((19,))),
    )
    got_edge = lax.ppermute(edge, "ctx", ahead_1)
    got_far_edge = lax.ppermute(own_edge, "ctx", ahead_2)
    got_pack = lax.ppermute(pack, "ctx", swap)

    square = (heads, DK, DV)
    docs = (pltpu.SMEM(doc_lengths.shape, jnp.int32), pltpu.SemaphoreType.DMA)
    own_state, own_map, own_out, own_through = call(
        own_kernel,
        [(square, F32), (square, BF16), ((rows, value_width), F32), ((rows, value_width), BF16)],
        (doc_lengths, own, weights, gates, got_edge),
        "own_terms",
        hbm=(0,),
        scratch=docs,
        flops=2_000_000_000,
        moved=4_000_000,
    )
    peer = call(
        peer_kernel,
        [
            (square, F32),
            (square, BF16),
            ((heads, rows, rows), BF16),
            ((heads, rows, DK + DV), BF16),
            ((rows, value_width), BF16),
            (square, BF16),
        ]
        + ([(square, BF16)] if hops > 1 else []),
        (doc_lengths, got_pack, own_edge, got_far_edge, weights, own_state, own_map),
        "peer_terms",
        hbm=(0,),
        scratch=docs,
        flops=2_000_000_000,
        moved=4_000_000,
    )
    state, map_, inside, solved, start, end = peer[:6]
    gate_out, end = lax.optimization_barrier((gate_out, end))
    entering = lax.ppermute(end, "ctx", ahead_2)
    for _ in range(hops - 1):
        moved = jnp.einsum("hij,hjk->hik", peer[6], entering, preferred_element_type=F32)
        entering = lax.ppermute((end.astype(F32) + moved).astype(BF16), "ctx", ahead_2)
    got_gate = lax.ppermute(gate_out, "ctx", swap)
    out, through, weight = call(
        local_kernel,
        [((2 * rows, value_width), F32), ((2 * rows, value_width), BF16), ((4, value_width, width), BF16)],
        (own_state, own_map, own_out, own_through, state, map_, inside, solved, start, out_weight),
        "local_outputs",
        hbm=(9,),
        scratch=(pltpu.SemaphoreType.DMA((4,)),),
        flops=1_000_000_000,
        moved=4_000_000,
    )
    send, keep = call(
        project_kernel,
        [((2 * rows, 2 * width), BF16), ((2 * rows, 2 * width), BF16)],
        (out, through, entering, own_gate, got_gate, norm_gain.reshape(1, DV), weight),
        "project",
    )
    got = lax.ppermute(send, "head", [(i, i ^ 1) for i in range(head_count)])
    mine, to_x, to_y, to_xy = call(
        core_sum_kernel,
        [((rows, width), F32), ((rows, width), BF16), ((rows, width), BF16), ((rows, width), BF16)],
        (keep, got),
        "core_sum",
    )
    both = [
        (c * head_count + h, (c ^ 1) * head_count + (h ^ 2)) for c in range(ctx_count) for h in range(head_count)
    ]
    got_xy = lax.ppermute(to_xy, ("ctx", "head"), both)
    got_x = lax.ppermute(to_x, "head", [(i, i ^ 2) for i in range(head_count)])
    got_y = lax.ppermute(to_y, "ctx", swap)
    (projected,) = call(
        last_kernel, [((width, rows), BF16)], (mine, got_x, got_y, got_xy), "last_sum"
    )
    return projected


def solution(mesh):
    return jax.shard_map(
        body,
        mesh=mesh,
        in_specs=(
            P("ctx", "head"),
            P("ctx", "head"),
            P("ctx", "head"),
            P("ctx", "head"),
            P(None, "head"),
            P(None, "head"),
            P(None, "head"),
            P("head", "ctx"),
            P("head", "ctx"),
            P(),
            P(),
            P("head", None),
        ),
        out_specs=P("head", "ctx"),
        check_vma=False,
    )
```

```python
import jax
import jax.numpy as jnp
from jax import lax
from jax.experimental import pallas as pl
from jax.experimental.pallas import tpu as pltpu
from jax.sharding import PartitionSpec as P

DK = 128
DV = 128
EDGE = 16
F32 = jnp.float32
BF16 = jnp.bfloat16
VMEM_LIMIT = 48 * 1024 * 1024


def dot(a, b):
    return jnp.dot(a.astype(BF16), b.astype(BF16), preferred_element_type=F32)


def exact_dot(a, b):
    return jnp.dot(a, b, precision=lax.Precision.HIGHEST, preferred_element_type=F32)


def where_y(flag, a, b):
    return jnp.where(flag == 1, a, b)


def document_counts(doc_ref, base, rows, lanes):
    down = lax.broadcasted_iota(jnp.int32, (rows + 8, lanes), 0) + (base - 8)
    along = lax.broadcasted_iota(jnp.int32, (8, rows), 1) + base
    docs = doc_ref.shape[0]

    def one(d, carried):
        start, count_down, count_along = carried
        count_down = count_down + (down >= start).astype(jnp.int32)
        count_along = count_along + (along >= start).astype(jnp.int32)
        return start + doc_ref[d], count_down, count_along

    state = (jnp.int32(0), jnp.zeros_like(down), jnp.zeros_like(along))
    if docs <= 16:
        for d in range(docs):
            state = one(d, state)
    else:
        state = lax.fori_loop(0, docs, one, state)
    return state[1], state[2]


def three_terms(value):
    high = value.astype(BF16)
    rest = value - high.astype(F32)
    middle = rest.astype(BF16)
    low = (rest - middle.astype(F32)).astype(BF16)
    return high, middle, low


class Copies:
    def __init__(self, sems):
        self.sems, self.started = sems, []

    def start(self, source, target):
        self.started.append(pltpu.make_async_copy(source, target, self.sems.at[len(self.started)]))
        self.started[-1].start()

    def wait(self, first=0, last=None):
        for one in self.started[first:last]:
            one.wait()


def half_columns(ref, which):
    width = ref.shape[1] // 2
    return pl.ds(pl.multiple_of(which * width, width), width)


def pack_kernel(q_ref, k_ref, v_ref, decay_ref, beta_ref, edge_ref, pack_ref, gates_ref, raw_gates, sems):
    other = 1 - lax.axis_index("ctx") % 2
    rows = q_ref.shape[0]
    heads = decay_ref.shape[0] // 2
    copies = Copies(sems)
    copies.start(decay_ref, raw_gates.at[0])
    copies.start(beta_ref, raw_gates.at[1])
    at = 0
    for ref in (q_ref, k_ref, v_ref):
        width = ref.shape[1] // 2
        copies.start(ref.at[pl.ds(rows - EDGE, EDGE), half_columns(ref, other)], edge_ref.at[:, pl.ds(at, width)])
        at += width
    at = 0
    for ref in (k_ref, v_ref):
        width = ref.shape[1] // 2
        copies.start(ref.at[:, half_columns(ref, other)], pack_ref.at[pl.ds(0, rows), pl.ds(at, width)])
        at += width
    pack_ref[rows : rows + EDGE, :] = jnp.zeros((EDGE, pack_ref.shape[1]), BF16)
    copies.wait(0, 2)
    decay = raw_gates[0]
    log_gamma = -(jnp.maximum(decay, 0.0) + jnp.log1p(jnp.exp(-jnp.abs(decay))))
    upper = lax.broadcasted_iota(jnp.int32, (rows, rows), 0) <= lax.broadcasted_iota(jnp.int32, (rows, rows), 1)
    sums = exact_dot(log_gamma, upper.astype(F32))
    beta = 1.0 / (1.0 + jnp.exp(-raw_gates[1]))
    at = 0
    for i, value in enumerate((sums, beta)):
        gates_ref[i * heads : i * heads + heads] = where_y(other, value[:heads], value[heads:])
        for term in three_terms(where_y(other, value[heads:], value[:heads])):
            pack_ref[rows : rows + heads, at : at + rows] = term
            at += rows
    copies.wait(2)


def early_kernel(q_ref, k_ref, v_ref, g_ref, cq_ref, ck_ref, cv_ref, doc_hbm,
                 own_edge_ref, late_ref, own_ref, weight_ref, own_gate_ref, down_ref, along_ref, doc_ref, sems):
    ctx = lax.axis_index("ctx")
    y = ctx % 2
    rows = q_ref.shape[0]
    copies = Copies(sems)
    copies.start(doc_hbm, doc_ref)
    at = 0
    for ref, weights in ((q_ref, cq_ref), (k_ref, ck_ref), (v_ref, cv_ref)):
        width = ref.shape[1] // 2
        here = pl.ds(at, width)
        copies.start(ref.at[pl.ds(rows - EDGE, EDGE), half_columns(ref, y)], own_edge_ref.at[:, here])
        copies.start(ref.at[:, half_columns(ref, y)], own_ref.at[:, here])
        copies.start(weights.at[:, half_columns(ref, y)], weight_ref.at[:, here])
        at += width
    key_width = q_ref.shape[1] // 2
    copies.start(q_ref.at[:, half_columns(q_ref, 1 - y)], late_ref.at[:, pl.ds(0, key_width)])
    copies.start(g_ref.at[:, half_columns(g_ref, 1 - y)], late_ref.at[:, pl.ds(key_width, g_ref.shape[1] // 2)])
    copies.start(g_ref.at[:, half_columns(g_ref, y)], own_gate_ref)
    copies.wait(0, 1)
    down_ref[...], along_ref[...] = document_counts(doc_ref, (ctx - y) * rows, 2 * rows, 128)
    copies.wait(1)


def conv_silu(halo, current, weight, keeps):
    rows = current.shape[0]
    padded = jnp.concatenate([halo.astype(F32)[EDGE - 8 :], current.astype(F32)], axis=0)
    margin = weight.shape[0] - 1
    summed = weight[margin : margin + 1] * padded[8:]
    for lag in range(1, margin + 1):
        summed = summed + weight[margin - lag : margin - lag + 1] * padded[8 - lag : 8 - lag + rows] * keeps[lag]
    return summed / (1.0 + jnp.exp(-summed))


def unit(vectors):
    return vectors * lax.rsqrt(jnp.sum(vectors * vectors, axis=-1, keepdims=True) + 1e-6)


def odd_blocks(value, reach):
    return jnp.concatenate([value[at : at + reach] for at in range(reach, value.shape[0], 2 * reach)], axis=0)


def at_odd_blocks(value, reach):
    parts = []
    for at in range(0, value.shape[0], reach):
        parts += [jnp.zeros((reach, value.shape[1]), value.dtype), value[at : at + reach]]
    return jnp.concatenate(parts, axis=0)


def keep_masks(seg_down):
    seg = seg_down[8:]
    return [None] + [(seg_down[8 - lag : 8 - lag + seg.shape[0]] == seg).astype(F32) for lag in (1, 2, 3)]


def state_terms(seg_down, seg_along, halo, k, v, weights, sums, beta):
    heads, rows = sums.shape
    key_heads = heads // 2
    seg = seg_down[8:]
    keeps = keep_masks(seg_down)
    before = seg_down[7:8]
    last = seg_down[rows + 7 : rows + 8]
    row = lax.broadcasted_iota(jnp.int32, (rows, rows), 0)
    col = lax.broadcasted_iota(jnp.int32, (rows, rows), 1)
    same = (seg == seg_along[0:1]) & (row >= col)
    stacked = jnp.concatenate([sums, beta, jnp.zeros((rows - 2 * heads, rows), F32)], axis=0)
    columns = stacked.T

    keys = [unit(conv_silu(halo(1, g), k(g), weights(1, g), keeps)) for g in range(key_heads)]
    values = [conv_silu(halo(2, g), v(g), weights(2, g), keeps) for g in range(heads)]
    keys_t = [key.T for key in keys]
    keys_t16 = [key.astype(BF16) for key in keys_t]
    grams = [dot(key, key_t) for key, key_t in zip(keys, keys_t16)]

    lower, decays, rhs, starts, ends, throughs = [], [], [], [], [], []
    for h in range(heads):
        g = h // 2
        down = jnp.broadcast_to(columns[:, h : h + 1], (rows, rows))
        beta_down = jnp.broadcast_to(columns[:, heads + h : heads + h + 1], (rows, rows))
        along = sums[h : h + 1]
        end = jnp.broadcast_to(columns[rows - 1 : rows, h : h + 1], (1, rows))
        decay = jnp.exp(jnp.where(same, down - along, -1e30))
        decays.append(decay)
        lower.append(jnp.where(row > col, beta_down * grams[g] * decay, 0.0))
        start = jnp.where(seg == before, jnp.exp(down), 0.0)
        starts.append(start)
        rhs.append(
            jnp.concatenate([(beta_down * values[h]).astype(BF16), (beta_down * start * keys[g]).astype(BF16)], axis=1)
        )
        ends.append((keys_t[g] * jnp.where(seg_along[0:1] == last, jnp.exp(end - along), 0.0)).astype(BF16))
        throughs.append(jnp.where(last == before, jnp.exp(end), 0.0))

    small = 16
    eye = (row == col).astype(F32)
    power = [jnp.where(row // small == col // small, -x, 0.0) for x in lower]
    inverse = [eye + x for x in power]
    power = [x.astype(BF16) for x in power]
    reach = 2
    while reach < small:
        power = [dot(x, x).astype(BF16) for x in power]
        inverse = [x + dot(x, p) for x, p in zip(inverse, power)]
        reach *= 2
    reach = small
    while reach < rows:
        here = (row // (2 * reach) == col // (2 * reach)) & (row // reach != col // reach)
        moved = [dot(odd_blocks(jnp.where(here, x, 0.0), reach), i) for x, i in zip(lower, inverse)]
        moved = [dot(odd_blocks(i, reach), at_odd_blocks(m, reach)) for i, m in zip(inverse, moved)]
        inverse = [i - at_odd_blocks(m, reach) for i, m in zip(inverse, moved)]
        reach *= 2
    solved = [dot(i, r).astype(BF16) for i, r in zip(inverse, rhs)]
    ended = [dot(e, s) for e, s in zip(ends, solved)]
    states = [e[:, :DV] for e in ended]
    maps = [t * eye - e[:, DV:] for t, e in zip(throughs, ended)]
    return states, maps, solved, decays, starts, keys_t16


def query_terms(seg_down, halo, q, weights, solved, decays, starts, keys_t):
    keeps = keep_masks(seg_down)
    queries = [unit(conv_silu(halo(0, g), q(g), weights(0, g), keeps)) for g in range(len(keys_t))]
    scores = [dot(query, key_t) for query, key_t in zip(queries, keys_t)]
    results = [dot(scores[h // 2] * decays[h], solved[h]) for h in range(len(solved))]
    outs = [result[:, :DV] for result in results]
    throughs = [(queries[h // 2] * starts[h] - results[h][:, DV:]).astype(BF16) for h in range(len(solved))]
    return outs, throughs


def groups(heads):
    at = (0, heads // 2 * DK, heads * DK)
    return lambda which, g: slice(at[which] + g * 128, at[which] + g * 128 + 128)


def counts(down_ref, along_ref, block, rows):
    at = pl.multiple_of(block * rows, rows)
    return down_ref[pl.ds(at, rows + 8), :], along_ref[:, pl.ds(at, rows)]


def own_kernel(down_ref, along_ref, own_ref, weight_ref, gates_ref, halo_ref,
               state_ref, map_ref, out_ref, through_ref):
    rows = own_ref.shape[0]
    heads = gates_ref.shape[0] // 2
    columns = groups(heads)
    seg_down, seg_along = counts(down_ref, along_ref, lax.axis_index("ctx") % 2, rows)

    def halo(which, g):
        return halo_ref[:, columns(which, g)]

    def weights(which, g):
        return weight_ref[:, columns(which, g)]

    states, maps, solved, decays, starts, keys_t = state_terms(
        seg_down,
        seg_along,
        halo,
        lambda g: own_ref[:, columns(1, g)],
        lambda g: own_ref[:, columns(2, g)],
        weights,
        gates_ref[0:heads],
        gates_ref[heads:],
    )
    outs, throughs = query_terms(
        seg_down, halo, lambda g: own_ref[:, columns(0, g)], weights, solved, decays, starts, keys_t
    )
    for h in range(heads):
        state_ref[h] = states[h]
        map_ref[h] = maps[h].astype(BF16)
        out_ref[:, h * DV : h * DV + DV] = outs[h]
        through_ref[:, h * DK : h * DK + DK] = throughs[h]


def peer_halo(own_edge_ref, edge_ref, columns):
    y = lax.axis_index("ctx") % 2
    return lambda which, g: where_y(y, edge_ref[:, columns(which, g)], own_edge_ref[:, columns(which, g)])


def peer_kernel(down_ref, along_ref, pack_ref, own_edge_ref, edge_ref, weight_ref, own_state_ref, own_map_ref,
                state_ref, map_ref, solved_ref, decay_ref, start_ref, key_ref, end_ref, *pair_map_ref):
    y = lax.axis_index("ctx") % 2
    rows = pack_ref.shape[0] - EDGE
    heads = own_state_ref.shape[0]
    columns = groups(heads)
    key_width = heads // 2 * DK
    gates = [
        sum(pack_ref[rows : rows + heads, (3 * part + i) * rows : (3 * part + i + 1) * rows].astype(F32) for i in range(3))
        for part in range(2)
    ]
    states, maps, solved, decays, starts, keys_t = state_terms(
        *counts(down_ref, along_ref, 1 - y, rows),
        peer_halo(own_edge_ref, edge_ref, columns),
        lambda g: pack_ref[0:rows, g * DK : g * DK + DK],
        lambda g: pack_ref[0:rows, key_width + g * DV : key_width + g * DV + DV],
        lambda which, g: weight_ref[:, columns(which, g)],
        gates[0],
        gates[1],
    )
    for h in range(heads):
        own_state, own_map = own_state_ref[h], own_map_ref[h]
        maps16 = maps[h].astype(BF16)
        state_0, state_1 = where_y(y, states[h], own_state), where_y(y, own_state, states[h])
        map_0, map_1 = where_y(y, maps16, own_map), where_y(y, own_map, maps16)
        end_ref[h] = (state_1 + dot(map_1, state_0)).astype(BF16)
        if pair_map_ref:
            pair_map_ref[0][h] = dot(map_1, map_0).astype(BF16)
    for h in range(heads):
        state_ref[h] = states[h]
        map_ref[h] = maps[h].astype(BF16)
        solved_ref[h] = solved[h]
        decay_ref[h] = decays[h]
        start_ref[h] = starts[h]
    for g in range(heads // 2):
        key_ref[g] = keys_t[g]


def local_kernel(own_state_ref, own_map_ref, own_out_ref, own_through_ref, state_ref, map_ref, solved_ref, decay_ref,
                 start_ref, key_ref, down_ref, along_ref, late_ref, own_edge_ref, edge_ref, conv_ref, weight_hbm,
                 out_ref, through_ref, weight_ref, sems):
    y = lax.axis_index("ctx") % 2
    head = lax.axis_index("head")
    core, x = head % 2, head // 2
    depth, width = weight_ref.shape[1:]
    copies = []
    for i, (c, xx) in enumerate(((1 - core, x), (1 - core, 1 - x), (core, x), (core, 1 - x))):
        source = weight_hbm.at[
            pl.ds(pl.multiple_of(y * depth, depth), depth), pl.ds(pl.multiple_of((xx * 2 + c) * width, width), width)
        ]
        copies.append(pltpu.make_async_copy(source, weight_ref.at[i], sems.at[i]))
        copies[-1].start()
    rows = own_out_ref.shape[0]
    heads = own_state_ref.shape[0]
    columns = groups(heads)
    outs, throughs = query_terms(
        counts(down_ref, along_ref, 1 - y, rows)[0],
        peer_halo(own_edge_ref, edge_ref, columns),
        lambda g: late_ref[:, g * DK : g * DK + DK],
        lambda which, g: conv_ref[:, columns(which, g)],
        [solved_ref[h] for h in range(heads)],
        [decay_ref[h] for h in range(heads)],
        [start_ref[h] for h in range(heads)],
        [key_ref[g] for g in range(heads // 2)],
    )
    for h in range(heads):
        lanes = slice(h * DV, h * DV + DV)
        own_out, own_through = own_out_ref[:, lanes], own_through_ref[:, lanes]
        out, through = outs[h], throughs[h]
        state_0 = where_y(y, state_ref[h], own_state_ref[h]).astype(BF16)
        map_0 = where_y(y, map_ref[h], own_map_ref[h])
        through_1 = where_y(y, own_through, through)
        more = dot(through_1, jnp.concatenate([state_0, map_0], axis=1))
        extra, moved = more[:, :DV], more[:, DV:].astype(BF16)
        out_ref[0:rows, lanes] = own_out + where_y(y, extra, jnp.zeros_like(extra))
        out_ref[rows:, lanes] = out + where_y(y, jnp.zeros_like(extra), extra)
        through_ref[0:rows, lanes] = where_y(y, moved, own_through)
        through_ref[rows:, lanes] = where_y(y, through, moved)
    for copy in copies:
        copy.wait()


def project_kernel(out_ref, through_ref, enter_ref, gate_ref, late_ref, gain_ref, weight_ref, send_ref, keep_ref):
    heads = enter_ref.shape[0]
    key_width = late_ref.shape[1] - heads * DV
    width = weight_ref.shape[2]
    mixed = []
    for h in range(heads):
        lanes = slice(h * DV, h * DV + DV)
        o = out_ref[:, lanes] + dot(through_ref[:, lanes], enter_ref[h])
        gate = jnp.concatenate([gate_ref[:, lanes], late_ref[:, key_width + h * DV : key_width + h * DV + DV]], axis=0).astype(F32)
        scale = lax.rsqrt(jnp.mean(o * o, axis=-1, keepdims=True) + 1e-6)
        mixed.append((o * scale * gain_ref[...] * (gate / (1.0 + jnp.exp(-gate)))).astype(BF16))
    mixed = jnp.concatenate(mixed, axis=1)
    for i in range(4):
        to_ref = (send_ref, keep_ref)[i // 2]
        to_ref[:, (i % 2) * width : (i % 2 + 1) * width] = jnp.dot(
            mixed, weight_ref[i], preferred_element_type=F32
        ).astype(BF16)


def core_sum_kernel(keep_ref, got_ref, mine_ref, x_ref, y_ref, xy_ref):
    rows, width = mine_ref.shape
    for ref, r, c in ((xy_ref, 1, 1), (x_ref, 0, 1), (y_ref, 1, 0), (mine_ref, 0, 0)):
        at = (slice(r * rows, r * rows + rows), slice(c * width, c * width + width))
        ref[...] = (keep_ref[at].astype(F32) + got_ref[at].astype(F32)).astype(ref.dtype)


def last_kernel(mine_ref, x_ref, y_ref, xy_ref, out_ref):
    total = mine_ref[...] + x_ref[...].astype(F32) + (y_ref[...].astype(F32) + xy_ref[...].astype(F32))
    out_ref[...] = total.T.astype(BF16)


def call(kernel, outs, args, name, hbm=(), scratch=(), flops=0, moved=0):
    space = [pl.BlockSpec(memory_space=pltpu.HBM if i in hbm else pltpu.VMEM) for i in range(len(args))]
    args = [pltpu.with_memory_space_constraint(arg, pltpu.HBM) if i in hbm else arg for i, arg in enumerate(args)]
    return pl.pallas_call(
        kernel,
        out_shape=[jax.ShapeDtypeStruct(shape, kind) for shape, kind in outs],
        in_specs=space,
        out_specs=[pl.BlockSpec(memory_space=pltpu.VMEM)] * len(outs),
        scratch_shapes=list(scratch),
        compiler_params=pltpu.CompilerParams(vmem_limit_bytes=VMEM_LIMIT),
        cost_estimate=pl.CostEstimate(flops=flops, bytes_accessed=moved, transcendentals=0),
        name=name,
    )(*args)


def body(
    query_in,
    key_in,
    value_in,
    gate_in,
    conv_query,
    conv_key,
    conv_value,
    decay_in,
    beta_in,
    norm_gain,
    doc_lengths,
    out_weight,
):
    rows = query_in.shape[0]
    ctx_count, head_count = lax.axis_size("ctx"), lax.axis_size("head")
    heads = decay_in.shape[0] // 2
    key_width, value_width = key_in.shape[1] // 2, value_in.shape[1] // 2
    half_width = 2 * key_width + value_width
    width = out_weight.shape[1] // head_count
    longest = ctx_count * rows // 4
    hops = -(-(longest - 1) // (2 * rows))

    swap = [(i, i ^ 1) for i in range(ctx_count)]
    ahead_1 = [(i, (i + 1) % ctx_count) for i in range(ctx_count)]
    ahead_2 = [(i, (i + 2) % ctx_count) for i in range(ctx_count)]

    edge, pack, gates = call(
        pack_kernel,
        [((EDGE, half_width), BF16), ((rows + EDGE, key_width + value_width), BF16), ((2 * heads, rows), F32)],
        (query_in, key_in, value_in, decay_in, beta_in),
        "pack",
        hbm=range(5),
        scratch=(pltpu.VMEM((2,) + decay_in.shape, F32), pltpu.SemaphoreType.DMA((7,))),
    )
    own_edge, late, own, weights, own_gate, down, along = call(
        early_kernel,
        [
            ((EDGE, half_width), BF16),
            ((rows, key_width + value_width), BF16),
            ((rows, half_width), BF16),
            ((conv_query.shape[0], half_width), F32),
            ((rows, value_width), BF16),
            ((2 * rows + 8, 128), jnp.int32),
            ((8, 2 * rows), jnp.int32),
        ],
        (query_in, key_in, value_in, gate_in, conv_query, conv_key, conv_value, doc_lengths),
        "early",
        hbm=range(8),
        scratch=(pltpu.SMEM(doc_lengths.shape, jnp.int32), pltpu.SemaphoreType.DMA((13,))),
        flops=10_000_000_000,
        moved=2_000_000,
    )
    got_edge = lax.ppermute(edge, "ctx", ahead_1)
    got_pack = lax.ppermute(pack, "ctx", swap)
    got_far_edge = lax.ppermute(own_edge, "ctx", ahead_2)
    got_late = lax.ppermute(late, "ctx", swap)

    square = (heads, DK, DV)
    own_state, own_map, own_out, own_through = call(
        own_kernel,
        [(square, F32), (square, BF16), ((rows, value_width), F32), ((rows, value_width), BF16)],
        (down, along, own, weights, gates, got_edge),
        "own_terms",
        flops=20_000_000_000,
        moved=4_000_000,
    )
    peer = call(
        peer_kernel,
        [
            (square, F32),
            (square, BF16),
            ((heads, rows, DK + DV), BF16),
            ((heads, rows, rows), F32),
            ((heads, rows, DK), F32),
            ((heads // 2, DK, rows), BF16),
            (square, BF16),
        ]
        + ([(square, BF16)] if hops > 1 else []),
        (down, along, got_pack, own_edge, got_far_edge, weights, own_state, own_map),
        "peer_terms",
        flops=2_000_000_000,
        moved=4_000_000,
    )
    state, map_, solved, decay, start, key, end = peer[:7]
    entering = lax.ppermute(end, "ctx", ahead_2)
    for _ in range(hops - 1):
        moved = jnp.einsum("hij,hjk->hik", peer[7], entering, preferred_element_type=F32)
        entering = lax.ppermute((end.astype(F32) + moved).astype(BF16), "ctx", ahead_2)
    out, through, weight = call(
        local_kernel,
        [((2 * rows, value_width), F32), ((2 * rows, value_width), BF16), ((4, value_width, width), BF16)],
        (own_state, own_map, own_out, own_through, state, map_, solved, decay, start, key, down, along, got_late, own_edge,
         got_far_edge, weights, out_weight),
        "local_outputs",
        hbm=(16,),
        scratch=(pltpu.SemaphoreType.DMA((4,)),),
        flops=1_000_000_000,
        moved=4_000_000,
    )
    send, keep = call(
        project_kernel,
        [((2 * rows, 2 * width), BF16), ((2 * rows, 2 * width), BF16)],
        (out, through, entering, own_gate, got_late, norm_gain.reshape(1, DV), weight),
        "project",
    )
    got = lax.ppermute(send, "head", [(i, i ^ 1) for i in range(head_count)])
    mine, to_x, to_y, to_xy = call(
        core_sum_kernel,
        [((rows, width), F32), ((rows, width), BF16), ((rows, width), BF16), ((rows, width), BF16)],
        (keep, got),
        "core_sum",
    )
    both = [
        (c * head_count + h, (c ^ 1) * head_count + (h ^ 2)) for c in range(ctx_count) for h in range(head_count)
    ]
    got_xy = lax.ppermute(to_xy, ("ctx", "head"), both)
    got_x = lax.ppermute(to_x, "head", [(i, i ^ 2) for i in range(head_count)])
    got_y = lax.ppermute(to_y, "ctx", swap)
    (projected,) = call(
        last_kernel, [((width, rows), BF16)], (mine, got_x, got_y, got_xy), "last_sum"
    )
    return projected


def solution(mesh):
    return jax.shard_map(
        body,
        mesh=mesh,
        in_specs=(
            P("ctx", "head"),
            P("ctx", "head"),
            P("ctx", "head"),
            P("ctx", "head"),
            P(None, "head"),
            P(None, "head"),
            P(None, "head"),
            P("head", "ctx"),
            P("head", "ctx"),
            P(),
            P(),
            P("head", None),
        ),
        out_specs=P("head", "ctx"),
        check_vma=False,
    )
```

```python
import jax
import jax.numpy as jnp
from jax import lax
from jax.experimental import pallas as pl
from jax.experimental.pallas import tpu as pltpu
from jax.sharding import PartitionSpec as P

DK = 128
DV = 128
EDGE = 16
F32 = jnp.float32
BF16 = jnp.bfloat16
VMEM_LIMIT = 48 * 1024 * 1024


def dot(a, b):
    return jnp.dot(a.astype(BF16), b.astype(BF16), preferred_element_type=F32)


def exact_dot(a, b):
    return jnp.dot(a, b, precision=lax.Precision.HIGHEST, preferred_element_type=F32)


def where_y(flag, a, b):
    return jnp.where(flag == 1, a, b)


def document_counts(doc_ref, base, rows, lanes):
    down = lax.broadcasted_iota(jnp.int32, (rows + 8, lanes), 0) + (base - 8)
    along = lax.broadcasted_iota(jnp.int32, (8, rows), 1) + base
    docs = doc_ref.shape[0]

    def one(d, carried):
        start, count_down, count_along = carried
        count_down = count_down + (down >= start).astype(jnp.int32)
        count_along = count_along + (along >= start).astype(jnp.int32)
        return start + doc_ref[d], count_down, count_along

    state = (jnp.int32(0), jnp.zeros_like(down), jnp.zeros_like(along))
    if docs <= 16:
        for d in range(docs):
            state = one(d, state)
    else:
        state = lax.fori_loop(0, docs, one, state)
    return state[1], state[2]


def three_terms(value):
    high = value.astype(BF16)
    rest = value - high.astype(F32)
    middle = rest.astype(BF16)
    low = (rest - middle.astype(F32)).astype(BF16)
    return high, middle, low


class Copies:
    def __init__(self, sems):
        self.sems, self.started = sems, []

    def start(self, source, target):
        self.started.append(pltpu.make_async_copy(source, target, self.sems.at[len(self.started)]))
        self.started[-1].start()

    def wait(self, first=0, last=None):
        for one in self.started[first:last]:
            one.wait()


def half_columns(ref, which):
    width = ref.shape[1] // 2
    return pl.ds(pl.multiple_of(which * width, width), width)


def pack_kernel(q_ref, k_ref, v_ref, decay_ref, beta_ref, edge_ref, pack_ref, gates_ref, raw_gates, sems):
    other = 1 - lax.axis_index("ctx") % 2
    rows = q_ref.shape[0]
    heads = decay_ref.shape[0] // 2
    copies = Copies(sems)
    copies.start(decay_ref, raw_gates.at[0])
    copies.start(beta_ref, raw_gates.at[1])
    at = 0
    for ref in (q_ref, k_ref, v_ref):
        width = ref.shape[1] // 2
        copies.start(ref.at[pl.ds(rows - EDGE, EDGE), half_columns(ref, other)], edge_ref.at[:, pl.ds(at, width)])
        at += width
    at = 0
    for ref in (k_ref, v_ref):
        width = ref.shape[1] // 2
        copies.start(ref.at[:, half_columns(ref, other)], pack_ref.at[pl.ds(0, rows), pl.ds(at, width)])
        at += width
    pack_ref[rows : rows + EDGE, :] = jnp.zeros((EDGE, pack_ref.shape[1]), BF16)
    copies.wait(0, 2)
    decay = raw_gates[0]
    log_gamma = -(jnp.maximum(decay, 0.0) + jnp.log1p(jnp.exp(-jnp.abs(decay))))
    upper = lax.broadcasted_iota(jnp.int32, (rows, rows), 0) <= lax.broadcasted_iota(jnp.int32, (rows, rows), 1)
    sums = exact_dot(log_gamma, upper.astype(F32))
    beta = 1.0 / (1.0 + jnp.exp(-raw_gates[1]))
    at = 0
    for i, value in enumerate((sums, beta)):
        gates_ref[i * heads : i * heads + heads] = where_y(other, value[:heads], value[heads:])
        for term in three_terms(where_y(other, value[heads:], value[:heads])):
            pack_ref[rows : rows + heads, at : at + rows] = term
            at += rows
    copies.wait(2)


def early_kernel(q_ref, k_ref, v_ref, g_ref, cq_ref, ck_ref, cv_ref, doc_hbm,
                 own_edge_ref, late_ref, own_ref, weight_ref, own_gate_ref, down_ref, along_ref, doc_ref, sems):
    ctx = lax.axis_index("ctx")
    y = ctx % 2
    rows = q_ref.shape[0]
    copies = Copies(sems)
    copies.start(doc_hbm, doc_ref)
    at = 0
    for ref, weights in ((q_ref, cq_ref), (k_ref, ck_ref), (v_ref, cv_ref)):
        width = ref.shape[1] // 2
        here = pl.ds(at, width)
        copies.start(ref.at[pl.ds(rows - EDGE, EDGE), half_columns(ref, y)], own_edge_ref.at[:, here])
        copies.start(ref.at[:, half_columns(ref, y)], own_ref.at[:, here])
        copies.start(weights.at[:, half_columns(ref, y)], weight_ref.at[:, here])
        at += width
    key_width = q_ref.shape[1] // 2
    copies.start(q_ref.at[:, half_columns(q_ref, 1 - y)], late_ref.at[:, pl.ds(0, key_width)])
    copies.start(g_ref.at[:, half_columns(g_ref, 1 - y)], late_ref.at[:, pl.ds(key_width, g_ref.shape[1] // 2)])
    copies.start(g_ref.at[:, half_columns(g_ref, y)], own_gate_ref)
    copies.wait(0, 1)
    down_ref[...], along_ref[...] = document_counts(doc_ref, (ctx - y) * rows, 2 * rows, 128)
    copies.wait(1)


def conv_silu(halo, current, weight, keeps):
    rows = current.shape[0]
    padded = jnp.concatenate([halo.astype(F32)[EDGE - 8 :], current.astype(F32)], axis=0)
    margin = weight.shape[0] - 1
    summed = weight[margin : margin + 1] * padded[8:]
    for lag in range(1, margin + 1):
        summed = summed + weight[margin - lag : margin - lag + 1] * padded[8 - lag : 8 - lag + rows] * keeps[lag]
    return summed / (1.0 + jnp.exp(-summed))


def unit(vectors):
    return vectors * lax.rsqrt(jnp.sum(vectors * vectors, axis=-1, keepdims=True) + 1e-6)


def odd_blocks(value, reach):
    return jnp.concatenate([value[at : at + reach] for at in range(reach, value.shape[0], 2 * reach)], axis=0)


def at_odd_blocks(value, reach):
    parts = []
    for at in range(0, value.shape[0], reach):
        parts += [jnp.zeros((reach, value.shape[1]), value.dtype), value[at : at + reach]]
    return jnp.concatenate(parts, axis=0)


def keep_masks(seg_down):
    seg = seg_down[8:]
    return [None] + [(seg_down[8 - lag : 8 - lag + seg.shape[0]] == seg).astype(F32) for lag in (1, 2, 3)]


def state_terms(seg_down, seg_along, halo, k, v, weights, sums, beta):
    heads, rows = sums.shape
    key_heads = heads // 2
    seg = seg_down[8:]
    keeps = keep_masks(seg_down)
    before = seg_down[7:8]
    last = seg_down[rows + 7 : rows + 8]
    row = lax.broadcasted_iota(jnp.int32, (rows, rows), 0)
    col = lax.broadcasted_iota(jnp.int32, (rows, rows), 1)
    same = (seg == seg_along[0:1]) & (row >= col)
    stacked = jnp.concatenate([sums, beta, jnp.zeros((rows - 2 * heads, rows), F32)], axis=0)
    columns = stacked.T

    keys = [unit(conv_silu(halo(1, g), k(g), weights(1, g), keeps)) for g in range(key_heads)]
    values = [conv_silu(halo(2, g), v(g), weights(2, g), keeps) for g in range(heads)]
    keys_t = [key.T for key in keys]
    keys_t16 = [key.astype(BF16) for key in keys_t]
    grams = [dot(key, key_t) for key, key_t in zip(keys, keys_t16)]

    lower, decays, rhs, starts, ends, throughs = [], [], [], [], [], []
    for h in range(heads):
        g = h // 2
        down = jnp.broadcast_to(columns[:, h : h + 1], (rows, rows))
        beta_down = jnp.broadcast_to(columns[:, heads + h : heads + h + 1], (rows, rows))
        along = sums[h : h + 1]
        end = jnp.broadcast_to(columns[rows - 1 : rows, h : h + 1], (1, rows))
        decay = jnp.exp(jnp.where(same, down - along, -1e30))
        decays.append(decay)
        lower.append(jnp.where(row > col, beta_down * grams[g] * decay, 0.0))
        start = jnp.where(seg == before, jnp.exp(down), 0.0)
        starts.append(start)
        rhs.append(
            jnp.concatenate([(beta_down * values[h]).astype(BF16), (beta_down * start * keys[g]).astype(BF16)], axis=1)
        )
        ends.append((keys_t[g] * jnp.where(seg_along[0:1] == last, jnp.exp(end - along), 0.0)).astype(BF16))
        throughs.append(jnp.where(last == before, jnp.exp(end), 0.0))

    small = 16
    eye = (row == col).astype(F32)
    power = [jnp.where(row // small == col // small, -x, 0.0) for x in lower]
    inverse = [eye + x for x in power]
    power = [x.astype(BF16) for x in power]
    reach = 2
    while reach < small:
        power = [dot(x, x).astype(BF16) for x in power]
        inverse = [x + dot(x, p) for x, p in zip(inverse, power)]
        reach *= 2
    reach = small
    while reach < rows:
        here = (row // (2 * reach) == col // (2 * reach)) & (row // reach != col // reach)
        moved = [dot(odd_blocks(jnp.where(here, x, 0.0), reach), i) for x, i in zip(lower, inverse)]
        moved = [dot(odd_blocks(i, reach), at_odd_blocks(m, reach)) for i, m in zip(inverse, moved)]
        inverse = [i - at_odd_blocks(m, reach) for i, m in zip(inverse, moved)]
        reach *= 2
    solved = [dot(i, r).astype(BF16) for i, r in zip(inverse, rhs)]
    ended = [dot(e, s) for e, s in zip(ends, solved)]
    states = [e[:, :DV] for e in ended]
    maps = [t * eye - e[:, DV:] for t, e in zip(throughs, ended)]
    return states, maps, solved, decays, starts, keys_t16


def query_terms(seg_down, halo, q, weights, solved, decays, starts, keys_t):
    keeps = keep_masks(seg_down)
    queries = [unit(conv_silu(halo(0, g), q(g), weights(0, g), keeps)) for g in range(len(keys_t))]
    scores = [dot(query, key_t) for query, key_t in zip(queries, keys_t)]
    results = [dot(scores[h // 2] * decays[h], solved[h]) for h in range(len(solved))]
    outs = [result[:, :DV] for result in results]
    throughs = [(queries[h // 2] * starts[h] - results[h][:, DV:]).astype(BF16) for h in range(len(solved))]
    return outs, throughs


def groups(heads):
    at = (0, heads // 2 * DK, heads * DK)
    return lambda which, g: slice(at[which] + g * 128, at[which] + g * 128 + 128)


def counts(down_ref, along_ref, block, rows):
    at = pl.multiple_of(block * rows, rows)
    return down_ref[pl.ds(at, rows + 8), :], along_ref[:, pl.ds(at, rows)]


def own_kernel(down_ref, along_ref, own_ref, weight_ref, gates_ref, halo_ref,
               state_ref, map_ref, out_ref, through_ref):
    rows = own_ref.shape[0]
    heads = gates_ref.shape[0] // 2
    columns = groups(heads)
    seg_down, seg_along = counts(down_ref, along_ref, lax.axis_index("ctx") % 2, rows)

    def halo(which, g):
        return halo_ref[:, columns(which, g)]

    def weights(which, g):
        return weight_ref[:, columns(which, g)]

    states, maps, solved, decays, starts, keys_t = state_terms(
        seg_down,
        seg_along,
        halo,
        lambda g: own_ref[:, columns(1, g)],
        lambda g: own_ref[:, columns(2, g)],
        weights,
        gates_ref[0:heads],
        gates_ref[heads:],
    )
    outs, throughs = query_terms(
        seg_down, halo, lambda g: own_ref[:, columns(0, g)], weights, solved, decays, starts, keys_t
    )
    for h in range(heads):
        state_ref[h] = states[h]
        map_ref[h] = maps[h].astype(BF16)
        out_ref[:, h * DV : h * DV + DV] = outs[h]
        through_ref[:, h * DK : h * DK + DK] = throughs[h]


def peer_halo(own_edge_ref, edge_ref, columns):
    y = lax.axis_index("ctx") % 2
    return lambda which, g: where_y(y, edge_ref[:, columns(which, g)], own_edge_ref[:, columns(which, g)])


def peer_kernel(down_ref, along_ref, pack_ref, own_edge_ref, edge_ref, weight_ref, own_state_ref, own_map_ref,
                state_ref, map_ref, solved_ref, decay_ref, start_ref, key_ref, end_ref, *pair_map_ref):
    y = lax.axis_index("ctx") % 2
    rows = pack_ref.shape[0] - EDGE
    heads = own_state_ref.shape[0]
    columns = groups(heads)
    key_width = heads // 2 * DK
    gates = [
        sum(pack_ref[rows : rows + heads, (3 * part + i) * rows : (3 * part + i + 1) * rows].astype(F32) for i in range(3))
        for part in range(2)
    ]
    states, maps, solved, decays, starts, keys_t = state_terms(
        *counts(down_ref, along_ref, 1 - y, rows),
        peer_halo(own_edge_ref, edge_ref, columns),
        lambda g: pack_ref[0:rows, g * DK : g * DK + DK],
        lambda g: pack_ref[0:rows, key_width + g * DV : key_width + g * DV + DV],
        lambda which, g: weight_ref[:, columns(which, g)],
        gates[0],
        gates[1],
    )
    for h in range(heads):
        own_state, own_map = own_state_ref[h], own_map_ref[h]
        maps16 = maps[h].astype(BF16)
        state_0, state_1 = where_y(y, states[h], own_state), where_y(y, own_state, states[h])
        map_0, map_1 = where_y(y, maps16, own_map), where_y(y, own_map, maps16)
        end_ref[h] = (state_1 + dot(map_1, state_0)).astype(BF16)
        if pair_map_ref:
            pair_map_ref[0][h] = dot(map_1, map_0).astype(BF16)
    for h in range(heads):
        state_ref[h] = states[h]
        map_ref[h] = maps[h].astype(BF16)
        solved_ref[h] = solved[h]
        decay_ref[h] = decays[h]
        start_ref[h] = starts[h]
    for g in range(heads // 2):
        key_ref[g] = keys_t[g]


def local_kernel(own_state_ref, own_map_ref, own_out_ref, own_through_ref, state_ref, map_ref, solved_ref, decay_ref,
                 start_ref, key_ref, down_ref, along_ref, late_ref, own_edge_ref, edge_ref, conv_ref, weight_hbm,
                 out_ref, through_ref, weight_ref, sems):
    y = lax.axis_index("ctx") % 2
    head = lax.axis_index("head")
    core, x = head % 2, head // 2
    depth, width = weight_ref.shape[1:]
    copies = []
    for i, (c, xx) in enumerate(((1 - core, x), (1 - core, 1 - x), (core, x), (core, 1 - x))):
        source = weight_hbm.at[
            pl.ds(pl.multiple_of(y * depth, depth), depth), pl.ds(pl.multiple_of((xx * 2 + c) * width, width), width)
        ]
        copies.append(pltpu.make_async_copy(source, weight_ref.at[i], sems.at[i]))
        copies[-1].start()
    rows = own_out_ref.shape[0]
    heads = own_state_ref.shape[0]
    columns = groups(heads)
    outs, throughs = query_terms(
        counts(down_ref, along_ref, 1 - y, rows)[0],
        peer_halo(own_edge_ref, edge_ref, columns),
        lambda g: late_ref[:, g * DK : g * DK + DK],
        lambda which, g: conv_ref[:, columns(which, g)],
        [solved_ref[h] for h in range(heads)],
        [decay_ref[h] for h in range(heads)],
        [start_ref[h] for h in range(heads)],
        [key_ref[g] for g in range(heads // 2)],
    )
    for h in range(heads):
        lanes = slice(h * DV, h * DV + DV)
        own_out, own_through = own_out_ref[:, lanes], own_through_ref[:, lanes]
        out, through = outs[h], throughs[h]
        state_0 = where_y(y, state_ref[h], own_state_ref[h]).astype(BF16)
        map_0 = where_y(y, map_ref[h], own_map_ref[h])
        through_1 = where_y(y, own_through, through)
        more = dot(through_1, jnp.concatenate([state_0, map_0], axis=1))
        extra, moved = more[:, :DV], more[:, DV:].astype(BF16)
        out_ref[0:rows, lanes] = own_out + where_y(y, extra, jnp.zeros_like(extra))
        out_ref[rows:, lanes] = out + where_y(y, jnp.zeros_like(extra), extra)
        through_ref[0:rows, lanes] = where_y(y, moved, own_through)
        through_ref[rows:, lanes] = where_y(y, through, moved)
    for copy in copies:
        copy.wait()


def project_kernel(out_ref, through_ref, enter_ref, gate_ref, late_ref, gain_ref, weight_ref, send_ref, keep_ref):
    heads = enter_ref.shape[0]
    key_width = late_ref.shape[1] - heads * DV
    width = weight_ref.shape[2]
    mixed = []
    for h in range(heads):
        lanes = slice(h * DV, h * DV + DV)
        o = out_ref[:, lanes] + dot(through_ref[:, lanes], enter_ref[h])
        gate = jnp.concatenate([gate_ref[:, lanes], late_ref[:, key_width + h * DV : key_width + h * DV + DV]], axis=0).astype(F32)
        scale = lax.rsqrt(jnp.mean(o * o, axis=-1, keepdims=True) + 1e-6)
        mixed.append((o * scale * gain_ref[...] * (gate / (1.0 + jnp.exp(-gate)))).astype(BF16))
    mixed = jnp.concatenate(mixed, axis=1)
    for i in range(4):
        to_ref = (send_ref, keep_ref)[i // 2]
        to_ref[:, (i % 2) * width : (i % 2 + 1) * width] = jnp.dot(
            mixed, weight_ref[i], preferred_element_type=F32
        ).astype(BF16)


def core_sum_kernel(keep_ref, got_ref, xy_ref):
    rows, width = xy_ref.shape
    at = (slice(rows, 2 * rows), slice(width, 2 * width))
    xy_ref[...] = (keep_ref[at].astype(F32) + got_ref[at].astype(F32)).astype(BF16)


def core_sums_kernel(keep_ref, got_ref, mine_ref, x_ref, y_ref):
    rows, width = mine_ref.shape
    for ref, r, c in ((x_ref, 0, 1), (y_ref, 1, 0), (mine_ref, 0, 0)):
        at = (slice(r * rows, r * rows + rows), slice(c * width, c * width + width))
        ref[...] = (keep_ref[at].astype(F32) + got_ref[at].astype(F32)).astype(ref.dtype)


def last_kernel(mine_ref, x_ref, y_ref, xy_ref, out_ref):
    total = mine_ref[...] + x_ref[...].astype(F32) + (y_ref[...].astype(F32) + xy_ref[...].astype(F32))
    out_ref[...] = total.T.astype(BF16)


def call(kernel, outs, args, name, hbm=(), scratch=(), flops=0, moved=0):
    space = [pl.BlockSpec(memory_space=pltpu.HBM if i in hbm else pltpu.VMEM) for i in range(len(args))]
    args = [pltpu.with_memory_space_constraint(arg, pltpu.HBM) if i in hbm else arg for i, arg in enumerate(args)]
    return pl.pallas_call(
        kernel,
        out_shape=[jax.ShapeDtypeStruct(shape, kind) for shape, kind in outs],
        in_specs=space,
        out_specs=[pl.BlockSpec(memory_space=pltpu.VMEM)] * len(outs),
        scratch_shapes=list(scratch),
        compiler_params=pltpu.CompilerParams(vmem_limit_bytes=VMEM_LIMIT),
        cost_estimate=pl.CostEstimate(flops=flops, bytes_accessed=moved, transcendentals=0),
        name=name,
    )(*args)


def body(
    query_in,
    key_in,
    value_in,
    gate_in,
    conv_query,
    conv_key,
    conv_value,
    decay_in,
    beta_in,
    norm_gain,
    doc_lengths,
    out_weight,
):
    rows = query_in.shape[0]
    ctx_count, head_count = lax.axis_size("ctx"), lax.axis_size("head")
    heads = decay_in.shape[0] // 2
    key_width, value_width = key_in.shape[1] // 2, value_in.shape[1] // 2
    half_width = 2 * key_width + value_width
    width = out_weight.shape[1] // head_count
    longest = ctx_count * rows // 4
    hops = -(-(longest - 1) // (2 * rows))

    swap = [(i, i ^ 1) for i in range(ctx_count)]
    ahead_1 = [(i, (i + 1) % ctx_count) for i in range(ctx_count)]
    pair_ahead = [(i, i + 2) for i in range(ctx_count - 2)]
    ring = [1 + 2 * p for p in range(ctx_count // 2)] + [2 * p for p in reversed(range(ctx_count // 2))]
    along_ring = [(ring[i], ring[(i + 1) % ctx_count]) for i in range(ctx_count)]

    edge, pack, gates = call(
        pack_kernel,
        [((EDGE, half_width), BF16), ((rows + EDGE, key_width + value_width), BF16), ((2 * heads, rows), F32)],
        (query_in, key_in, value_in, decay_in, beta_in),
        "pack",
        hbm=range(5),
        scratch=(pltpu.VMEM((2,) + decay_in.shape, F32), pltpu.SemaphoreType.DMA((7,))),
    )
    own_edge, late, own, weights, own_gate, down, along = call(
        early_kernel,
        [
            ((EDGE, half_width), BF16),
            ((rows, key_width + value_width), BF16),
            ((rows, half_width), BF16),
            ((conv_query.shape[0], half_width), F32),
            ((rows, value_width), BF16),
            ((2 * rows + 8, 128), jnp.int32),
            ((8, 2 * rows), jnp.int32),
        ],
        (query_in, key_in, value_in, gate_in, conv_query, conv_key, conv_value, doc_lengths),
        "early",
        hbm=range(8),
        scratch=(pltpu.SMEM(doc_lengths.shape, jnp.int32), pltpu.SemaphoreType.DMA((13,))),
        flops=10_000_000_000,
        moved=2_000_000,
    )
    got_edge = lax.ppermute(edge, "ctx", ahead_1)
    got_pack = lax.ppermute(pack, "ctx", swap)
    got_far_edge = lax.ppermute(own_edge, "ctx", along_ring)

    square = (heads, DK, DV)
    own_state, own_map, own_out, own_through = call(
        own_kernel,
        [(square, F32), (square, BF16), ((rows, value_width), F32), ((rows, value_width), BF16)],
        (down, along, own, weights, gates, got_edge),
        "own_terms",
        flops=20_000_000_000,
        moved=4_000_000,
    )
    late, own_map = lax.optimization_barrier((late, own_map))
    got_late = lax.ppermute(late, "ctx", swap)
    peer = call(
        peer_kernel,
        [
            (square, F32),
            (square, BF16),
            ((heads, rows, DK + DV), BF16),
            ((heads, rows, rows), F32),
            ((heads, rows, DK), F32),
            ((heads // 2, DK, rows), BF16),
            (square, BF16),
        ]
        + ([(square, BF16)] if hops > 1 else []),
        (down, along, got_pack, own_edge, got_far_edge, weights, own_state, own_map),
        "peer_terms",
        flops=2_000_000_000,
        moved=4_000_000,
    )
    state, map_, solved, decay, start, key, end = peer[:7]
    entering = lax.ppermute(end, "ctx", pair_ahead)
    for _ in range(hops - 1):
        moved = jnp.einsum("hij,hjk->hik", peer[7], entering, preferred_element_type=F32)
        entering = lax.ppermute((end.astype(F32) + moved).astype(BF16), "ctx", pair_ahead)
    out, through, weight = call(
        local_kernel,
        [((2 * rows, value_width), F32), ((2 * rows, value_width), BF16), ((4, value_width, width), BF16)],
        (own_state, own_map, own_out, own_through, state, map_, solved, decay, start, key, down, along, got_late, own_edge,
         got_far_edge, weights, out_weight),
        "local_outputs",
        hbm=(16,),
        scratch=(pltpu.SemaphoreType.DMA((4,)),),
        flops=1_000_000_000,
        moved=4_000_000,
    )
    send, keep = call(
        project_kernel,
        [((2 * rows, 2 * width), BF16), ((2 * rows, 2 * width), BF16)],
        (out, through, entering, own_gate, got_late, norm_gain.reshape(1, DV), weight),
        "project",
    )
    got = lax.ppermute(send, "head", [(i, i ^ 1) for i in range(head_count)])
    (to_xy,) = call(core_sum_kernel, [((rows, width), BF16)], (keep, got), "core_sum_xy")
    mine, to_x, to_y = call(
        core_sums_kernel,
        [((rows, width), F32), ((rows, width), BF16), ((rows, width), BF16)],
        (keep, got),
        "core_sums",
        flops=2_000_000_000,
        moved=1_000_000,
    )
    both = [
        (c * head_count + h, (c ^ 1) * head_count + (h ^ 2)) for c in range(ctx_count) for h in range(head_count)
    ]
    got_xy = lax.ppermute(to_xy, ("ctx", "head"), both)
    got_x = lax.ppermute(to_x, "head", [(i, i ^ 2) for i in range(head_count)])
    got_y = lax.ppermute(to_y, "ctx", swap)
    (projected,) = call(
        last_kernel, [((width, rows), BF16)], (mine, got_x, got_y, got_xy), "last_sum"
    )
    return projected


def solution(mesh):
    return jax.shard_map(
        body,
        mesh=mesh,
        in_specs=(
            P("ctx", "head"),
            P("ctx", "head"),
            P("ctx", "head"),
            P("ctx", "head"),
            P(None, "head"),
            P(None, "head"),
            P(None, "head"),
            P("head", "ctx"),
            P("head", "ctx"),
            P(),
            P(),
            P("head", None),
        ),
        out_specs=P("head", "ctx"),
        check_vma=False,
    )
```

```python
import jax
import jax.numpy as jnp
from jax import lax
from jax.experimental import pallas as pl
from jax.experimental.pallas import tpu as pltpu
from jax.sharding import PartitionSpec as P

DK = 128
DV = 128
EDGE = 16
F32 = jnp.float32
BF16 = jnp.bfloat16
VMEM_LIMIT = 48 * 1024 * 1024


def dot(a, b):
    return jnp.dot(a.astype(BF16), b.astype(BF16), preferred_element_type=F32)


def exact_dot(a, b):
    return jnp.dot(a, b, precision=lax.Precision.HIGHEST, preferred_element_type=F32)


def where_y(flag, a, b):
    return jnp.where(flag == 1, a, b)


def document_counts(doc_ref, base, rows, lanes):
    down = lax.broadcasted_iota(jnp.int32, (rows + 8, lanes), 0) + (base - 8)
    along = lax.broadcasted_iota(jnp.int32, (8, rows), 1) + base
    docs = doc_ref.shape[0]

    def one(d, carried):
        start, count_down, count_along = carried
        count_down = count_down + (down >= start).astype(jnp.int32)
        count_along = count_along + (along >= start).astype(jnp.int32)
        return start + doc_ref[d], count_down, count_along

    state = (jnp.int32(0), jnp.zeros_like(down), jnp.zeros_like(along))
    if docs <= 16:
        for d in range(docs):
            state = one(d, state)
    else:
        state = lax.fori_loop(0, docs, one, state)
    return state[1], state[2]


def three_terms(value):
    high = value.astype(BF16)
    rest = value - high.astype(F32)
    middle = rest.astype(BF16)
    low = (rest - middle.astype(F32)).astype(BF16)
    return high, middle, low


class Copies:
    def __init__(self, sems):
        self.sems, self.started = sems, []

    def start(self, source, target):
        self.started.append(pltpu.make_async_copy(source, target, self.sems.at[len(self.started)]))
        self.started[-1].start()

    def wait(self, first=0, last=None):
        for one in self.started[first:last]:
            one.wait()


def half_columns(ref, which):
    width = ref.shape[1] // 2
    return pl.ds(pl.multiple_of(which * width, width), width)


def pack_kernel(q_ref, k_ref, v_ref, decay_ref, beta_ref, edge_ref, pack_ref, gates_ref, raw_gates, sems):
    other = 1 - lax.axis_index("ctx") % 2
    rows = q_ref.shape[0]
    heads = decay_ref.shape[0] // 2
    copies = Copies(sems)
    copies.start(decay_ref, raw_gates.at[0])
    copies.start(beta_ref, raw_gates.at[1])
    at = 0
    for ref in (q_ref, k_ref, v_ref):
        width = ref.shape[1] // 2
        copies.start(ref.at[pl.ds(rows - EDGE, EDGE), half_columns(ref, other)], edge_ref.at[:, pl.ds(at, width)])
        at += width
    at = 0
    for ref in (k_ref, v_ref):
        width = ref.shape[1] // 2
        copies.start(ref.at[:, half_columns(ref, other)], pack_ref.at[pl.ds(0, rows), pl.ds(at, width)])
        at += width
    pack_ref[rows : rows + EDGE, :] = jnp.zeros((EDGE, pack_ref.shape[1]), BF16)
    copies.wait(0, 2)
    decay = raw_gates[0]
    log_gamma = -(jnp.maximum(decay, 0.0) + jnp.log1p(jnp.exp(-jnp.abs(decay))))
    upper = lax.broadcasted_iota(jnp.int32, (rows, rows), 0) <= lax.broadcasted_iota(jnp.int32, (rows, rows), 1)
    sums = exact_dot(log_gamma, upper.astype(F32))
    beta = 1.0 / (1.0 + jnp.exp(-raw_gates[1]))
    at = 0
    for i, value in enumerate((sums, beta)):
        gates_ref[i * heads : i * heads + heads] = where_y(other, value[:heads], value[heads:])
        for term in three_terms(where_y(other, value[heads:], value[:heads])):
            pack_ref[rows : rows + heads, at : at + rows] = term
            at += rows
    copies.wait(2)


def early_kernel(q_ref, k_ref, v_ref, g_ref, cq_ref, ck_ref, cv_ref, doc_hbm,
                 own_edge_ref, late_ref, own_ref, weight_ref, own_gate_ref, down_ref, along_ref, doc_ref, sems):
    ctx = lax.axis_index("ctx")
    y = ctx % 2
    rows = q_ref.shape[0]
    copies = Copies(sems)
    copies.start(doc_hbm, doc_ref)
    at = 0
    for ref, weights in ((q_ref, cq_ref), (k_ref, ck_ref), (v_ref, cv_ref)):
        width = ref.shape[1] // 2
        here = pl.ds(at, width)
        copies.start(ref.at[pl.ds(rows - EDGE, EDGE), half_columns(ref, y)], own_edge_ref.at[:, here])
        copies.start(ref.at[:, half_columns(ref, y)], own_ref.at[:, here])
        copies.start(weights.at[:, half_columns(ref, y)], weight_ref.at[:, here])
        at += width
    key_width = q_ref.shape[1] // 2
    copies.start(q_ref.at[:, half_columns(q_ref, 1 - y)], late_ref.at[:, pl.ds(0, key_width)])
    copies.start(g_ref.at[:, half_columns(g_ref, 1 - y)], late_ref.at[:, pl.ds(key_width, g_ref.shape[1] // 2)])
    copies.start(g_ref.at[:, half_columns(g_ref, y)], own_gate_ref)
    copies.wait(0, 1)
    down_ref[...], along_ref[...] = document_counts(doc_ref, (ctx - y) * rows, 2 * rows, 128)
    copies.wait(1)


def conv_silu(halo, current, weight, keeps):
    rows = current.shape[0]
    padded = jnp.concatenate([halo.astype(F32)[EDGE - 8 :], current.astype(F32)], axis=0)
    margin = weight.shape[0] - 1
    summed = weight[margin : margin + 1] * padded[8:]
    for lag in range(1, margin + 1):
        summed = summed + weight[margin - lag : margin - lag + 1] * padded[8 - lag : 8 - lag + rows] * keeps[lag]
    return summed / (1.0 + jnp.exp(-summed))


def unit(vectors):
    return vectors * lax.rsqrt(jnp.sum(vectors * vectors, axis=-1, keepdims=True) + 1e-6)


def odd_blocks(value, reach):
    return jnp.concatenate([value[at : at + reach] for at in range(reach, value.shape[0], 2 * reach)], axis=0)


def at_odd_blocks(value, reach):
    parts = []
    for at in range(0, value.shape[0], reach):
        parts += [jnp.zeros((reach, value.shape[1]), value.dtype), value[at : at + reach]]
    return jnp.concatenate(parts, axis=0)


def keep_masks(seg_down):
    seg = seg_down[8:]
    return [None] + [(seg_down[8 - lag : 8 - lag + seg.shape[0]] == seg).astype(F32) for lag in (1, 2, 3)]


def solve_terms(lower):
    rows = lower[0].shape[0]
    small, large = rows // 8, rows // 4
    row = lax.broadcasted_iota(jnp.int32, (rows, rows), 0)
    col = lax.broadcasted_iota(jnp.int32, (rows, rows), 1)
    power = [jnp.where(row // small == col // small, -x, 0.0) for x in lower]
    eye = (row == col).astype(F32)
    inverse = [eye + x for x in power]
    power = [x.astype(BF16) for x in power]
    reach = 2
    while reach < small:
        power = [dot(x, x).astype(BF16) for x in power]
        inverse = [x + dot(x, p) for x, p in zip(inverse, power)]
        reach *= 2
    here = (row // large == col // large) & (row // small != col // small)
    moved = [dot(odd_blocks(jnp.where(here, x, 0.0), small), i) for x, i in zip(lower, inverse)]
    moved = [dot(odd_blocks(i, small), at_odd_blocks(m, small)) for i, m in zip(inverse, moved)]
    inverse = [(i - at_odd_blocks(m, small)).astype(BF16) for i, m in zip(inverse, moved)]
    rest = [jnp.where(row // large == col // large, 0.0, -x) for x in lower]
    once = [dot(i, r).astype(BF16) for i, r in zip(inverse, rest)]
    twice = [dot(m, m).astype(BF16) for m in once]
    return inverse, once, twice


def state_terms(seg_down, seg_along, halo, k, v, weights, sums, beta):
    heads, rows = sums.shape
    key_heads = heads // 2
    seg = seg_down[8:]
    keeps = keep_masks(seg_down)
    before = seg_down[7:8]
    last = seg_down[rows + 7 : rows + 8]
    row = lax.broadcasted_iota(jnp.int32, (rows, rows), 0)
    col = lax.broadcasted_iota(jnp.int32, (rows, rows), 1)
    same = (seg == seg_along[0:1]) & (row >= col)
    stacked = jnp.concatenate([sums, beta, jnp.zeros((rows - 2 * heads, rows), F32)], axis=0)
    columns = stacked.T

    keys = [unit(conv_silu(halo(1, g), k(g), weights(1, g), keeps)) for g in range(key_heads)]
    values = [conv_silu(halo(2, g), v(g), weights(2, g), keeps) for g in range(heads)]
    keys_t = [key.T for key in keys]
    keys_t16 = [key.astype(BF16) for key in keys_t]
    grams = [dot(key, key_t) for key, key_t in zip(keys, keys_t16)]

    lower, decays, rhs, starts, ends, throughs = [], [], [], [], [], []
    for h in range(heads):
        g = h // 2
        down = jnp.broadcast_to(columns[:, h : h + 1], (rows, rows))
        beta_down = jnp.broadcast_to(columns[:, heads + h : heads + h + 1], (rows, rows))
        along = sums[h : h + 1]
        end = jnp.broadcast_to(columns[rows - 1 : rows, h : h + 1], (1, rows))
        decay = jnp.exp(jnp.where(same, down - along, -1e30))
        decays.append(decay)
        lower.append(jnp.where(row > col, beta_down * grams[g] * decay, 0.0))
        start = jnp.where(seg == before, jnp.exp(down), 0.0)
        starts.append(start)
        rhs.append(
            jnp.concatenate([(beta_down * values[h]).astype(BF16), (beta_down * start * keys[g]).astype(BF16)], axis=1)
        )
        ends.append((keys_t[g] * jnp.where(seg_along[0:1] == last, jnp.exp(end - along), 0.0)).astype(BF16))
        throughs.append(jnp.where(last == before, jnp.exp(end), 0.0))

    inverse, once, twice = solve_terms(lower)
    solved = [dot(i, r) for i, r in zip(inverse, rhs)]
    solved = [s + dot(m, s) for m, s in zip(once, solved)]
    solved = [(s + dot(m, s)).astype(BF16) for m, s in zip(twice, solved)]
    eye = (row == col).astype(F32)
    ended = [dot(e, s) for e, s in zip(ends, solved)]
    states = [e[:, :DV] for e in ended]
    maps = [t * eye - e[:, DV:] for t, e in zip(throughs, ended)]
    return states, maps, solved, decays, starts, keys_t16


def query_terms(seg_down, halo, q, weights, solved, decays, starts, keys_t):
    keeps = keep_masks(seg_down)
    queries = [unit(conv_silu(halo(0, g), q(g), weights(0, g), keeps)) for g in range(len(keys_t))]
    scores = [dot(query, key_t) for query, key_t in zip(queries, keys_t)]
    results = [dot(scores[h // 2] * decays[h], solved[h]) for h in range(len(solved))]
    outs = [result[:, :DV] for result in results]
    throughs = [(queries[h // 2] * starts[h] - results[h][:, DV:]).astype(BF16) for h in range(len(solved))]
    return outs, throughs


def groups(heads):
    at = (0, heads // 2 * DK, heads * DK)
    return lambda which, g: slice(at[which] + g * 128, at[which] + g * 128 + 128)


def counts(down_ref, along_ref, block, rows):
    at = pl.multiple_of(block * rows, rows)
    return down_ref[pl.ds(at, rows + 8), :], along_ref[:, pl.ds(at, rows)]


def own_kernel(down_ref, along_ref, own_ref, weight_ref, gates_ref, halo_ref,
               state_ref, map_ref, out_ref, through_ref):
    rows = own_ref.shape[0]
    heads = gates_ref.shape[0] // 2
    columns = groups(heads)
    seg_down, seg_along = counts(down_ref, along_ref, lax.axis_index("ctx") % 2, rows)

    def halo(which, g):
        return halo_ref[:, columns(which, g)]

    def weights(which, g):
        return weight_ref[:, columns(which, g)]

    states, maps, solved, decays, starts, keys_t = state_terms(
        seg_down,
        seg_along,
        halo,
        lambda g: own_ref[:, columns(1, g)],
        lambda g: own_ref[:, columns(2, g)],
        weights,
        gates_ref[0:heads],
        gates_ref[heads:],
    )
    outs, throughs = query_terms(
        seg_down, halo, lambda g: own_ref[:, columns(0, g)], weights, solved, decays, starts, keys_t
    )
    for h in range(heads):
        state_ref[h] = states[h]
        map_ref[h] = maps[h].astype(BF16)
        out_ref[:, h * DV : h * DV + DV] = outs[h]
        through_ref[:, h * DK : h * DK + DK] = throughs[h]


def peer_halo(own_edge_ref, edge_ref, columns):
    y = lax.axis_index("ctx") % 2
    return lambda which, g: where_y(y, edge_ref[:, columns(which, g)], own_edge_ref[:, columns(which, g)])


def peer_kernel(down_ref, along_ref, pack_ref, own_edge_ref, edge_ref, weight_ref, own_state_ref, own_map_ref,
                state_ref, map_ref, solved_ref, decay_ref, start_ref, key_ref, end_ref, *pair_map_ref):
    y = lax.axis_index("ctx") % 2
    rows = pack_ref.shape[0] - EDGE
    heads = own_state_ref.shape[0]
    columns = groups(heads)
    key_width = heads // 2 * DK
    gates = [
        sum(pack_ref[rows : rows + heads, (3 * part + i) * rows : (3 * part + i + 1) * rows].astype(F32) for i in range(3))
        for part in range(2)
    ]
    states, maps, solved, decays, starts, keys_t = state_terms(
        *counts(down_ref, along_ref, 1 - y, rows),
        peer_halo(own_edge_ref, edge_ref, columns),
        lambda g: pack_ref[0:rows, g * DK : g * DK + DK],
        lambda g: pack_ref[0:rows, key_width + g * DV : key_width + g * DV + DV],
        lambda which, g: weight_ref[:, columns(which, g)],
        gates[0],
        gates[1],
    )
    for h in range(heads):
        own_state, own_map = own_state_ref[h], own_map_ref[h]
        maps16 = maps[h].astype(BF16)
        state_0, state_1 = where_y(y, states[h], own_state), where_y(y, own_state, states[h])
        map_0, map_1 = where_y(y, maps16, own_map), where_y(y, own_map, maps16)
        end_ref[h] = (state_1 + dot(map_1, state_0)).astype(BF16)
        if pair_map_ref:
            pair_map_ref[0][h] = dot(map_1, map_0).astype(BF16)
    for h in range(heads):
        state_ref[h] = states[h]
        map_ref[h] = maps[h].astype(BF16)
        solved_ref[h] = solved[h]
        decay_ref[h] = decays[h]
        start_ref[h] = starts[h]
    for g in range(heads // 2):
        key_ref[g] = keys_t[g]


def local_kernel(own_state_ref, own_map_ref, own_out_ref, own_through_ref, state_ref, map_ref, solved_ref, decay_ref,
                 start_ref, key_ref, down_ref, along_ref, late_ref, own_edge_ref, edge_ref, conv_ref, weight_hbm,
                 out_ref, through_ref, weight_ref, sems):
    y = lax.axis_index("ctx") % 2
    head = lax.axis_index("head")
    core, x = head % 2, head // 2
    depth, width = weight_ref.shape[1:]
    copies = []
    for i, (c, xx) in enumerate(((1 - core, x), (1 - core, 1 - x), (core, x), (core, 1 - x))):
        source = weight_hbm.at[
            pl.ds(pl.multiple_of(y * depth, depth), depth), pl.ds(pl.multiple_of((xx * 2 + c) * width, width), width)
        ]
        copies.append(pltpu.make_async_copy(source, weight_ref.at[i], sems.at[i]))
        copies[-1].start()
    rows = own_out_ref.shape[0]
    heads = own_state_ref.shape[0]
    columns = groups(heads)
    outs, throughs = query_terms(
        counts(down_ref, along_ref, 1 - y, rows)[0],
        peer_halo(own_edge_ref, edge_ref, columns),
        lambda g: late_ref[:, g * DK : g * DK + DK],
        lambda which, g: conv_ref[:, columns(which, g)],
        [solved_ref[h] for h in range(heads)],
        [decay_ref[h] for h in range(heads)],
        [start_ref[h] for h in range(heads)],
        [key_ref[g] for g in range(heads // 2)],
    )
    for h in range(heads):
        lanes = slice(h * DV, h * DV + DV)
        own_out, own_through = own_out_ref[:, lanes], own_through_ref[:, lanes]
        out, through = outs[h], throughs[h]
        state_0 = where_y(y, state_ref[h], own_state_ref[h]).astype(BF16)
        map_0 = where_y(y, map_ref[h], own_map_ref[h])
        through_1 = where_y(y, own_through, through)
        more = dot(through_1, jnp.concatenate([state_0, map_0], axis=1))
        extra, moved = more[:, :DV], more[:, DV:].astype(BF16)
        out_ref[0:rows, lanes] = own_out + where_y(y, extra, jnp.zeros_like(extra))
        out_ref[rows:, lanes] = out + where_y(y, jnp.zeros_like(extra), extra)
        through_ref[0:rows, lanes] = where_y(y, moved, own_through)
        through_ref[rows:, lanes] = where_y(y, through, moved)
    for copy in copies:
        copy.wait()


def mix_kernel(out_ref, through_ref, even_ref, odd_ref, gate_ref, late_ref, gain_ref, weight_ref, mixed_ref, send_ref, keep_ref):
    from_even = lax.axis_index("ctx") // 2 % 2
    heads = even_ref.shape[0]
    rows = gate_ref.shape[0]
    key_width = late_ref.shape[1] - heads * DV
    for h in range(heads):
        lanes = slice(h * DV, h * DV + DV)
        o = out_ref[:, lanes] + dot(through_ref[:, lanes], where_y(from_even, even_ref[h], odd_ref[h]))
        gate = jnp.concatenate([gate_ref[:, lanes], late_ref[:, key_width + h * DV : key_width + h * DV + DV]], axis=0)
        gate = gate.astype(F32)
        scale = lax.rsqrt(jnp.mean(o * o, axis=-1, keepdims=True) + 1e-6)
        mixed_ref[:, lanes] = (o * scale * gain_ref[...] * (gate / (1.0 + jnp.exp(-gate)))).astype(BF16)
    send_ref[...] = jnp.dot(mixed_ref[rows:, :], weight_ref[1], preferred_element_type=F32).astype(BF16)
    keep_ref[...] = jnp.dot(mixed_ref[rows:, :], weight_ref[3], preferred_element_type=F32).astype(BF16)


QUARTERS = ((0, 0), (0, 1), (1, 0))


def project_kernel(mixed_ref, weight_ref, send_ref, keep_ref):
    rows = send_ref.shape[1]
    for c, to_ref in ((0, send_ref), (1, keep_ref)):
        for i, (peer, far) in enumerate(QUARTERS):
            product = jnp.dot(mixed_ref[peer * rows : peer * rows + rows, :], weight_ref[2 * c + far], preferred_element_type=F32)
            to_ref[i] = product.astype(BF16)


def core_sum_kernel(keep_ref, got_ref, xy_ref):
    xy_ref[...] = (keep_ref[...].astype(F32) + got_ref[...].astype(F32)).astype(BF16)


def core_sums_kernel(keep_ref, got_ref, mine_ref, x_ref, y_ref):
    for i, ref in enumerate((mine_ref, x_ref, y_ref)):
        ref[...] = (keep_ref[i].astype(F32) + got_ref[i].astype(F32)).astype(ref.dtype)


def last_kernel(mine_ref, x_ref, y_ref, xy_ref, out_ref):
    total = mine_ref[...] + x_ref[...].astype(F32) + (y_ref[...].astype(F32) + xy_ref[...].astype(F32))
    out_ref[...] = total.T.astype(BF16)


def call(kernel, outs, args, name, hbm=(), scratch=(), flops=0, moved=0):
    space = [pl.BlockSpec(memory_space=pltpu.HBM if i in hbm else pltpu.VMEM) for i in range(len(args))]
    args = [pltpu.with_memory_space_constraint(arg, pltpu.HBM) if i in hbm else arg for i, arg in enumerate(args)]
    return pl.pallas_call(
        kernel,
        out_shape=[jax.ShapeDtypeStruct(shape, kind) for shape, kind in outs],
        in_specs=space,
        out_specs=[pl.BlockSpec(memory_space=pltpu.VMEM)] * len(outs),
        scratch_shapes=list(scratch),
        compiler_params=pltpu.CompilerParams(vmem_limit_bytes=VMEM_LIMIT),
        cost_estimate=pl.CostEstimate(flops=flops, bytes_accessed=moved, transcendentals=0),
        name=name,
    )(*args)


def body(
    query_in,
    key_in,
    value_in,
    gate_in,
    conv_query,
    conv_key,
    conv_value,
    decay_in,
    beta_in,
    norm_gain,
    doc_lengths,
    out_weight,
):
    rows = query_in.shape[0]
    ctx_count, head_count = lax.axis_size("ctx"), lax.axis_size("head")
    heads = decay_in.shape[0] // 2
    key_width, value_width = key_in.shape[1] // 2, value_in.shape[1] // 2
    half_width = 2 * key_width + value_width
    width = out_weight.shape[1] // head_count
    longest = ctx_count * rows // 4
    hops = -(-(longest - 1) // (2 * rows))

    swap = [(i, i ^ 1) for i in range(ctx_count)]
    ahead_1 = [(i, (i + 1) % ctx_count) for i in range(ctx_count)]
    even_swap = [(i, i ^ 2) for i in range(ctx_count)]
    odd_swap = [
        (c * head_count + h, (((c + 2) ^ 2) - 2) * head_count + h if 2 <= c < ctx_count - 2 else c * head_count + (h ^ 1))
        for c in range(ctx_count)
        for h in range(head_count)
    ]
    ring = [1 + 2 * p for p in range(ctx_count // 2)] + [2 * p for p in reversed(range(ctx_count // 2))]
    along_ring = [(ring[i], ring[(i + 1) % ctx_count]) for i in range(ctx_count)]

    edge, pack, gates = call(
        pack_kernel,
        [((EDGE, half_width), BF16), ((rows + EDGE, key_width + value_width), BF16), ((2 * heads, rows), F32)],
        (query_in, key_in, value_in, decay_in, beta_in),
        "pack",
        hbm=range(5),
        scratch=(pltpu.VMEM((2,) + decay_in.shape, F32), pltpu.SemaphoreType.DMA((7,))),
    )
    own_edge, late, own, weights, own_gate, down, along = call(
        early_kernel,
        [
            ((EDGE, half_width), BF16),
            ((rows, key_width + value_width), BF16),
            ((rows, half_width), BF16),
            ((conv_query.shape[0], half_width), F32),
            ((rows, value_width), BF16),
            ((2 * rows + 8, 128), jnp.int32),
            ((8, 2 * rows), jnp.int32),
        ],
        (query_in, key_in, value_in, gate_in, conv_query, conv_key, conv_value, doc_lengths),
        "early",
        hbm=range(8),
        scratch=(pltpu.SMEM(doc_lengths.shape, jnp.int32), pltpu.SemaphoreType.DMA((13,))),
        flops=10_000_000_000,
        moved=2_000_000,
    )
    got_edge = lax.ppermute(edge, "ctx", ahead_1)
    got_pack = lax.ppermute(pack, "ctx", swap)
    got_far_edge = lax.ppermute(own_edge, "ctx", along_ring)

    square = (heads, DK, DV)
    own_state, own_map, own_out, own_through = call(
        own_kernel,
        [(square, F32), (square, BF16), ((rows, value_width), F32), ((rows, value_width), BF16)],
        (down, along, own, weights, gates, got_edge),
        "own_terms",
        flops=1_000_000,
        moved=4_000_000,
    )
    late, own_map = lax.optimization_barrier((late, own_map))
    got_late = lax.ppermute(late, "ctx", swap)
    peer = call(
        peer_kernel,
        [
            (square, F32),
            (square, BF16),
            ((heads, rows, DK + DV), BF16),
            ((heads, rows, rows), F32),
            ((heads, rows, DK), F32),
            ((heads // 2, DK, rows), BF16),
            (square, BF16),
        ]
        + ([(square, BF16)] if hops > 1 else []),
        (down, along, got_pack, own_edge, got_far_edge, weights, own_state, own_map),
        "peer_terms",
        flops=2_000_000_000,
        moved=4_000_000,
    )
    state, map_, solved, decay, start, key, end = peer[:7]
    def from_earlier(value):
        return lax.ppermute(value, "ctx", even_swap), lax.ppermute(value, ("ctx", "head"), odd_swap)

    entering = from_earlier(end)
    for _ in range(hops - 1):
        earlier = jnp.where(lax.axis_index("ctx") // 2 % 2 == 1, *entering)
        moved = jnp.einsum("hij,hjk->hik", peer[7], earlier, preferred_element_type=F32)
        moved = jnp.where(lax.axis_index("ctx") < 2, 0.0, moved)
        entering = from_earlier((end.astype(F32) + moved).astype(BF16))
    out, through, weight = call(
        local_kernel,
        [((2 * rows, value_width), F32), ((2 * rows, value_width), BF16), ((4, value_width, width), BF16)],
        (own_state, own_map, own_out, own_through, state, map_, solved, decay, start, key, down, along, got_late, own_edge,
         got_far_edge, weights, out_weight),
        "local_outputs",
        hbm=(16,),
        scratch=(pltpu.SemaphoreType.DMA((4,)),),
        flops=1_000_000_000,
        moved=4_000_000,
    )
    cores = [(i, i ^ 1) for i in range(head_count)]
    mixed, send_far, keep_far = call(
        mix_kernel,
        [((2 * rows, value_width), BF16), ((rows, width), BF16), ((rows, width), BF16)],
        (out, through, *entering, own_gate, got_late, norm_gain.reshape(1, DV), weight),
        "mix",
    )
    got_far = lax.ppermute(send_far, "head", cores)
    send, keep = call(
        project_kernel,
        [((3, rows, width), BF16), ((3, rows, width), BF16)],
        (mixed, weight),
        "project",
        flops=2_000_000_000,
        moved=4_000_000,
    )
    send, got_far = lax.optimization_barrier((send, got_far))
    got = lax.ppermute(send, "head", cores)
    (to_xy,) = call(core_sum_kernel, [((rows, width), BF16)], (keep_far, got_far), "core_sum_xy")
    mine, to_x, to_y = call(
        core_sums_kernel,
        [((rows, width), F32), ((rows, width), BF16), ((rows, width), BF16)],
        (keep, got),
        "core_sums",
    )
    both = [
        (c * head_count + h, (c ^ 1) * head_count + (h ^ 2)) for c in range(ctx_count) for h in range(head_count)
    ]
    got_xy = lax.ppermute(to_xy, ("ctx", "head"), both)
    got_x = lax.ppermute(to_x, "head", [(i, i ^ 2) for i in range(head_count)])
    got_y = lax.ppermute(to_y, "ctx", swap)
    (projected,) = call(
        last_kernel, [((width, rows), BF16)], (mine, got_x, got_y, got_xy), "last_sum"
    )
    return projected


def solution(mesh):
    return jax.shard_map(
        body,
        mesh=mesh,
        in_specs=(
            P("ctx", "head"),
            P("ctx", "head"),
            P("ctx", "head"),
            P("ctx", "head"),
            P(None, "head"),
            P(None, "head"),
            P(None, "head"),
            P("head", "ctx"),
            P("head", "ctx"),
            P(),
            P(),
            P("head", None),
        ),
        out_specs=P("head", "ctx"),
        check_vma=False,
    )
```

```python
import jax
import jax.numpy as jnp
from jax import lax
from jax.experimental import pallas as pl
from jax.experimental.pallas import tpu as pltpu
from jax.sharding import PartitionSpec as P

DK = 128
DV = 128
EDGE = 16
PARTS = 8
F32 = jnp.float32
BF16 = jnp.bfloat16
VMEM_LIMIT = 48 * 1024 * 1024


def dot(a, b):
    return jnp.dot(a.astype(BF16), b.astype(BF16), preferred_element_type=F32)


def dot_nt(a, b):
    dims = (((1,), (1,)), ((), ()))
    return lax.dot_general(a.astype(BF16), b.astype(BF16), dims, preferred_element_type=F32)


def exact_dot(a, b):
    return jnp.dot(a, b, precision=lax.Precision.HIGHEST, preferred_element_type=F32)


def where_y(flag, a, b):
    return jnp.where(flag == 1, a, b)


def document_counts(doc_ref, base, rows, lanes):
    down = lax.broadcasted_iota(jnp.int32, (rows + 8, lanes), 0) + (base - 8)
    along = lax.broadcasted_iota(jnp.int32, (8, rows), 1) + base
    docs = doc_ref.shape[0]

    def one(d, carried):
        start, count_down, count_along = carried
        count_down = count_down + (down >= start).astype(jnp.int32)
        count_along = count_along + (along >= start).astype(jnp.int32)
        return start + doc_ref[d], count_down, count_along

    state = (jnp.int32(0), jnp.zeros_like(down), jnp.zeros_like(along))
    if docs <= 16:
        for d in range(docs):
            state = one(d, state)
    else:
        state = lax.fori_loop(0, docs, one, state)
    return state[1], state[2]


def three_terms(value):
    high = value.astype(BF16)
    rest = value - high.astype(F32)
    middle = rest.astype(BF16)
    low = (rest - middle.astype(F32)).astype(BF16)
    return high, middle, low


class Copies:
    def __init__(self, sems):
        self.sems, self.started = sems, []

    def start(self, source, target):
        self.started.append(pltpu.make_async_copy(source, target, self.sems.at[len(self.started)]))
        self.started[-1].start()

    def wait(self, first=0, last=None):
        for one in self.started[first:last]:
            one.wait()


def half_columns(ref, which):
    width = ref.shape[1] // 2
    return pl.ds(pl.multiple_of(which * width, width), width)


def pack_kernel(q_ref, k_ref, v_ref, decay_ref, beta_ref, edge_ref, pack_ref, gates_ref, raw_gates, sems):
    other = 1 - lax.axis_index("ctx") % 2
    rows = q_ref.shape[0]
    heads = decay_ref.shape[0] // 2
    copies = Copies(sems)
    copies.start(decay_ref, raw_gates.at[0])
    copies.start(beta_ref, raw_gates.at[1])
    at = 0
    for ref in (q_ref, k_ref, v_ref):
        width = ref.shape[1] // 2
        copies.start(ref.at[pl.ds(rows - EDGE, EDGE), half_columns(ref, other)], edge_ref.at[:, pl.ds(at, width)])
        at += width
    at = 0
    for ref in (k_ref, v_ref):
        width = ref.shape[1] // 2
        copies.start(ref.at[:, half_columns(ref, other)], pack_ref.at[pl.ds(0, rows), pl.ds(at, width)])
        at += width
    pack_ref[rows : rows + EDGE, :] = jnp.zeros((EDGE, pack_ref.shape[1]), BF16)
    copies.wait(0, 2)
    decay = raw_gates[0]
    log_gamma = -(jnp.maximum(decay, 0.0) + jnp.log1p(jnp.exp(-jnp.abs(decay))))
    upper = lax.broadcasted_iota(jnp.int32, (rows, rows), 0) <= lax.broadcasted_iota(jnp.int32, (rows, rows), 1)
    sums = exact_dot(log_gamma, upper.astype(F32))
    beta = 1.0 / (1.0 + jnp.exp(-raw_gates[1]))
    at = 0
    for i, value in enumerate((sums, beta)):
        gates_ref[i * heads : i * heads + heads] = where_y(other, value[:heads], value[heads:])
        for term in three_terms(where_y(other, value[heads:], value[:heads])):
            pack_ref[rows : rows + heads, at : at + rows] = term
            at += rows
    copies.wait(2)


def early_kernel(q_ref, k_ref, v_ref, g_ref, cq_ref, ck_ref, cv_ref, doc_hbm,
                 own_edge_ref, late_ref, own_ref, weight_ref, own_gate_ref, down_ref, along_ref, doc_ref, sems):
    ctx = lax.axis_index("ctx")
    y = ctx % 2
    rows = q_ref.shape[0]
    copies = Copies(sems)
    copies.start(doc_hbm, doc_ref)
    at = 0
    for ref, weights in ((q_ref, cq_ref), (k_ref, ck_ref), (v_ref, cv_ref)):
        width = ref.shape[1] // 2
        here = pl.ds(at, width)
        copies.start(ref.at[pl.ds(rows - EDGE, EDGE), half_columns(ref, y)], own_edge_ref.at[:, here])
        copies.start(ref.at[:, half_columns(ref, y)], own_ref.at[:, here])
        copies.start(weights.at[:, half_columns(ref, y)], weight_ref.at[:, here])
        at += width
    key_width = q_ref.shape[1] // 2
    copies.start(q_ref.at[:, half_columns(q_ref, 1 - y)], late_ref.at[:, pl.ds(0, key_width)])
    copies.start(g_ref.at[:, half_columns(g_ref, 1 - y)], late_ref.at[:, pl.ds(key_width, g_ref.shape[1] // 2)])
    copies.start(g_ref.at[:, half_columns(g_ref, y)], own_gate_ref)
    copies.wait(0, 1)
    down_ref[...], along_ref[...] = document_counts(doc_ref, (ctx - y) * rows, 2 * rows, 128)
    copies.wait(1)


def conv_silu(halo, current, weight, keeps):
    rows = current.shape[0]
    padded = jnp.concatenate([halo.astype(F32)[EDGE - 8 :], current.astype(F32)], axis=0)
    margin = weight.shape[0] - 1
    summed = weight[margin : margin + 1] * padded[8:]
    for lag in range(1, margin + 1):
        summed = summed + weight[margin - lag : margin - lag + 1] * padded[8 - lag : 8 - lag + rows] * keeps[lag]
    return summed / (1.0 + jnp.exp(-summed))


def inverse_norms(vectors, axis):
    return lax.rsqrt(jnp.sum(vectors * vectors, axis=axis, keepdims=True) + 1e-6)


def odd_blocks(value, reach):
    return jnp.concatenate([value[at : at + reach] for at in range(reach, value.shape[0], 2 * reach)], axis=0)


def at_odd_blocks(value, reach):
    parts = []
    for at in range(0, value.shape[0], reach):
        parts += [jnp.zeros((reach, value.shape[1]), value.dtype), value[at : at + reach]]
    return jnp.concatenate(parts, axis=0)


def keep_masks(seg_down):
    seg = seg_down[8:]
    return [None] + [(seg_down[8 - lag : 8 - lag + seg.shape[0]] == seg).astype(F32) for lag in (1, 2, 3)]


def solve_terms(lower):
    rows = lower[0].shape[0]
    small, large = rows // 8, rows // 4
    row = lax.broadcasted_iota(jnp.int32, (rows, rows), 0)
    col = lax.broadcasted_iota(jnp.int32, (rows, rows), 1)
    power = [jnp.where(row // small == col // small, -x, 0.0) for x in lower]
    eye = (row == col).astype(F32)
    inverse = [eye + x for x in power]
    power = [x.astype(BF16) for x in power]
    reach = 2
    while reach < small:
        power = [dot(x, x).astype(BF16) for x in power]
        inverse = [x + dot(x, p) for x, p in zip(inverse, power)]
        reach *= 2
    here = (row // large == col // large) & (row // small != col // small)
    moved = [dot(odd_blocks(jnp.where(here, x, 0.0), small), i) for x, i in zip(lower, inverse)]
    moved = [dot(odd_blocks(i, small), at_odd_blocks(m, small)) for i, m in zip(inverse, moved)]
    inverse = [(i - at_odd_blocks(m, small)).astype(BF16) for i, m in zip(inverse, moved)]
    rest = [jnp.where(row // large == col // large, 0.0, -x) for x in lower]
    once = [dot(i, r).astype(BF16) for i, r in zip(inverse, rest)]
    twice = [dot(m, m).astype(BF16) for m in once]
    return inverse, once, twice


def state_terms(seg_down, seg_along, halo, k, v, weights, sums, beta):
    heads, rows = sums.shape
    key_heads = heads // 2
    seg = seg_down[8:]
    keeps = keep_masks(seg_down)
    before = seg_down[7:8]
    last = seg_down[rows + 7 : rows + 8]
    row = lax.broadcasted_iota(jnp.int32, (rows, rows), 0)
    col = lax.broadcasted_iota(jnp.int32, (rows, rows), 1)
    same = (seg == seg_along[0:1]) & (row >= col)
    stacked = jnp.concatenate([sums, beta, jnp.zeros((rows - 2 * heads, rows), F32)], axis=0)
    columns = stacked.T

    raw = [conv_silu(halo(1, g), k(g), weights(1, g), keeps) for g in range(key_heads)]
    grams = [dot_nt(key, key) for key in raw]
    raw_t = [key.T for key in raw]
    norms = [inverse_norms(key, 1) for key in raw]
    norms_t = [inverse_norms(key, 0) for key in raw_t]
    keys = [key * norm for key, norm in zip(raw, norms)]
    keys_t = [key * norm for key, norm in zip(raw_t, norms_t)]
    values = [conv_silu(halo(2, g), v(g), weights(2, g), keeps) for g in range(heads)]
    keys_t16 = [key.astype(BF16) for key in keys_t]

    lower, decays, rhs, starts, ends, throughs = [], [], [], [], [], []
    for h in range(heads):
        g = h // 2
        down = jnp.broadcast_to(columns[:, h : h + 1], (rows, rows))
        beta_down = jnp.broadcast_to(columns[:, heads + h : heads + h + 1], (rows, rows))
        along = sums[h : h + 1]
        end = jnp.broadcast_to(columns[rows - 1 : rows, h : h + 1], (1, rows))
        decay = jnp.exp(jnp.where(same, down - along, -1e30))
        decays.append(decay)
        factor = jnp.where(row > col, beta_down * norms[g] * decay * norms_t[g], 0.0)
        lower.append(factor * grams[g])
        start = jnp.where(seg == before, jnp.exp(down), 0.0)
        starts.append(start)
        rhs.append(
            jnp.concatenate([(beta_down * values[h]).astype(BF16), (beta_down * start * keys[g]).astype(BF16)], axis=1)
        )
        ends.append((keys_t[g] * jnp.where(seg_along[0:1] == last, jnp.exp(end - along), 0.0)).astype(BF16))
        throughs.append(jnp.where(last == before, jnp.exp(end), 0.0))

    inverse, once, twice = solve_terms(lower)
    solved = [dot(i, r) for i, r in zip(inverse, rhs)]
    solved = [s + dot(m, s) for m, s in zip(once, solved)]
    solved = [(s + dot(m, s)).astype(BF16) for m, s in zip(twice, solved)]
    eye = (row == col).astype(F32)
    ended = [dot(e, s) for e, s in zip(ends, solved)]
    states = [e[:, :DV] for e in ended]
    maps = [t * eye - e[:, DV:] for t, e in zip(throughs, ended)]
    return states, maps, solved, decays, starts, keys_t16


def query_terms(seg_down, halo, q, weights, solved, decays, starts, keys_t):
    keeps = keep_masks(seg_down)
    queries = [conv_silu(halo(0, g), q(g), weights(0, g), keeps) for g in range(len(keys_t))]
    scores = [dot(query, key_t) for query, key_t in zip(queries, keys_t)]
    norms = [inverse_norms(query, 1) for query in queries]
    queries = [query * norm for query, norm in zip(queries, norms)]
    results = [dot(scores[h // 2] * (norms[h // 2] * decays[h]), solved[h]) for h in range(len(solved))]
    outs = [result[:, :DV] for result in results]
    throughs = [(queries[h // 2] * starts[h] - results[h][:, DV:]).astype(BF16) for h in range(len(solved))]
    return outs, throughs


def groups(heads):
    at = (0, heads // 2 * DK, heads * DK)
    return lambda which, g: slice(at[which] + g * 128, at[which] + g * 128 + 128)


def counts(down_ref, along_ref, block, rows):
    at = pl.multiple_of(block * rows, rows)
    return down_ref[pl.ds(at, rows + 8), :], along_ref[:, pl.ds(at, rows)]


def own_kernel(down_ref, along_ref, own_ref, weight_ref, gates_ref, halo_ref,
               state_ref, map_ref, out_ref, through_ref):
    rows = own_ref.shape[0]
    heads = gates_ref.shape[0] // 2
    columns = groups(heads)
    seg_down, seg_along = counts(down_ref, along_ref, lax.axis_index("ctx") % 2, rows)

    def halo(which, g):
        return halo_ref[:, columns(which, g)]

    def weights(which, g):
        return weight_ref[:, columns(which, g)]

    states, maps, solved, decays, starts, keys_t = state_terms(
        seg_down,
        seg_along,
        halo,
        lambda g: own_ref[:, columns(1, g)],
        lambda g: own_ref[:, columns(2, g)],
        weights,
        gates_ref[0:heads],
        gates_ref[heads:],
    )
    outs, throughs = query_terms(
        seg_down, halo, lambda g: own_ref[:, columns(0, g)], weights, solved, decays, starts, keys_t
    )
    for h in range(heads):
        state_ref[h] = states[h]
        map_ref[h] = maps[h].astype(BF16)
        out_ref[:, h * DV : h * DV + DV] = outs[h]
        through_ref[:, h * DK : h * DK + DK] = throughs[h]


def peer_halo(own_edge_ref, edge_ref, columns):
    y = lax.axis_index("ctx") % 2
    return lambda which, g: where_y(y, edge_ref[:, columns(which, g)], own_edge_ref[:, columns(which, g)])


def peer_kernel(down_ref, along_ref, pack_ref, own_edge_ref, edge_ref, weight_ref, own_state_ref, own_map_ref,
                state_ref, map_ref, solved_ref, decay_ref, start_ref, key_ref, end_ref, *pair_map_ref):
    y = lax.axis_index("ctx") % 2
    rows = pack_ref.shape[0] - EDGE
    heads = own_state_ref.shape[0]
    columns = groups(heads)
    key_width = heads // 2 * DK
    gates = [
        sum(pack_ref[rows : rows + heads, (3 * part + i) * rows : (3 * part + i + 1) * rows].astype(F32) for i in range(3))
        for part in range(2)
    ]
    states, maps, solved, decays, starts, keys_t = state_terms(
        *counts(down_ref, along_ref, 1 - y, rows),
        peer_halo(own_edge_ref, edge_ref, columns),
        lambda g: pack_ref[0:rows, g * DK : g * DK + DK],
        lambda g: pack_ref[0:rows, key_width + g * DV : key_width + g * DV + DV],
        lambda which, g: weight_ref[:, columns(which, g)],
        gates[0],
        gates[1],
    )
    for h in range(heads):
        own_state, own_map = own_state_ref[h], own_map_ref[h]
        maps16 = maps[h].astype(BF16)
        state_0, state_1 = where_y(y, states[h], own_state), where_y(y, own_state, states[h])
        map_0, map_1 = where_y(y, maps16, own_map), where_y(y, own_map, maps16)
        end_ref[h] = (state_1 + dot(map_1, state_0)).astype(BF16)
        if pair_map_ref:
            pair_map_ref[0][h] = dot(map_1, map_0).astype(BF16)
    for h in range(heads):
        state_ref[h] = states[h]
        map_ref[h] = maps[h].astype(BF16)
        solved_ref[h] = solved[h]
        decay_ref[h] = decays[h]
        start_ref[h] = starts[h]
    for g in range(heads // 2):
        key_ref[g] = keys_t[g]


def local_kernel(own_state_ref, own_map_ref, own_out_ref, own_through_ref, state_ref, map_ref, solved_ref, decay_ref,
                 start_ref, key_ref, down_ref, along_ref, late_ref, own_edge_ref, edge_ref, conv_ref, weight_hbm,
                 out_ref, through_ref, weight_ref, sems):
    y = lax.axis_index("ctx") % 2
    depth = weight_ref.shape[0]
    copies = Copies(sems)
    part = depth // PARTS
    for i in range(PARTS):
        from_row = pl.multiple_of(y * depth + i * part, part)
        copies.start(weight_hbm.at[pl.ds(from_row, part), :], weight_ref.at[pl.ds(i * part, part), :])
    rows = own_out_ref.shape[0]
    heads = own_state_ref.shape[0]
    columns = groups(heads)
    outs, throughs = query_terms(
        counts(down_ref, along_ref, 1 - y, rows)[0],
        peer_halo(own_edge_ref, edge_ref, columns),
        lambda g: late_ref[:, g * DK : g * DK + DK],
        lambda which, g: conv_ref[:, columns(which, g)],
        [solved_ref[h] for h in range(heads)],
        [decay_ref[h] for h in range(heads)],
        [start_ref[h] for h in range(heads)],
        [key_ref[g] for g in range(heads // 2)],
    )
    for h in range(heads):
        lanes = slice(h * DV, h * DV + DV)
        own_out, own_through = own_out_ref[:, lanes], own_through_ref[:, lanes]
        out, through = outs[h], throughs[h]
        state_0 = where_y(y, state_ref[h], own_state_ref[h]).astype(BF16)
        map_0 = where_y(y, map_ref[h], own_map_ref[h])
        through_1 = where_y(y, own_through, through)
        more = dot(through_1, jnp.concatenate([state_0, map_0], axis=1))
        extra, moved = more[:, :DV], more[:, DV:].astype(BF16)
        out_ref[0:rows, lanes] = own_out + where_y(y, extra, jnp.zeros_like(extra))
        out_ref[rows:, lanes] = out + where_y(y, jnp.zeros_like(extra), extra)
        through_ref[0:rows, lanes] = where_y(y, moved, own_through)
        through_ref[rows:, lanes] = where_y(y, through, moved)
    copies.wait()


def feature_columns(weight_ref, other_core, other_x):
    head = lax.axis_index("head")
    core, x = head % 2, head // 2
    block = (x + other_x - 2 * x * other_x) * 2 + core + other_core - 2 * core * other_core
    width = weight_ref.shape[1] // lax.axis_size("head")
    return weight_ref[:, pl.ds(pl.multiple_of(block * width, width), width)]


def mix_kernel(out_ref, through_ref, even_ref, odd_ref, gate_ref, late_ref, gain_ref, weight_ref, mixed_ref, send_ref, keep_ref):
    from_even = lax.axis_index("ctx") // 2 % 2
    heads = even_ref.shape[0]
    rows = gate_ref.shape[0]
    key_width = late_ref.shape[1] - heads * DV
    for h in range(heads):
        lanes = slice(h * DV, h * DV + DV)
        o = out_ref[:, lanes] + dot(through_ref[:, lanes], where_y(from_even, even_ref[h], odd_ref[h]))
        gate = jnp.concatenate([gate_ref[:, lanes], late_ref[:, key_width + h * DV : key_width + h * DV + DV]], axis=0)
        gate = gate.astype(F32)
        scale = lax.rsqrt(jnp.mean(o * o, axis=-1, keepdims=True) + 1e-6)
        mixed_ref[:, lanes] = (o * scale * gain_ref[...] * (gate / (1.0 + jnp.exp(-gate)))).astype(BF16)
    send_ref[...] = jnp.dot(mixed_ref[rows:, :], feature_columns(weight_ref, 1, 1), preferred_element_type=F32).astype(BF16)
    keep_ref[...] = jnp.dot(mixed_ref[rows:, :], feature_columns(weight_ref, 0, 1), preferred_element_type=F32).astype(BF16)


QUARTERS = ((0, 0), (0, 1), (1, 0))


def project_kernel(mixed_ref, weight_ref, send_ref, keep_ref):
    rows = send_ref.shape[1]
    for c, to_ref in ((0, send_ref), (1, keep_ref)):
        for i, (peer, far) in enumerate(QUARTERS):
            weights = feature_columns(weight_ref, 1 - c, far)
            product = jnp.dot(mixed_ref[peer * rows : peer * rows + rows, :], weights, preferred_element_type=F32)
            to_ref[i] = product.astype(BF16)


def core_sum_kernel(keep_ref, got_ref, xy_ref):
    xy_ref[...] = (keep_ref[...].astype(F32) + got_ref[...].astype(F32)).astype(BF16)


def core_sums_kernel(keep_ref, got_ref, mine_ref, x_ref, y_ref):
    for i, ref in enumerate((mine_ref, x_ref, y_ref)):
        ref[...] = (keep_ref[i].astype(F32) + got_ref[i].astype(F32)).astype(ref.dtype)


def last_kernel(mine_ref, x_ref, y_ref, xy_ref, out_ref):
    total = mine_ref[...] + x_ref[...].astype(F32) + (y_ref[...].astype(F32) + xy_ref[...].astype(F32))
    out_ref[...] = total.T.astype(BF16)


def call(kernel, outs, args, name, hbm=(), scratch=(), flops=0, moved=0):
    space = [pl.BlockSpec(memory_space=pltpu.HBM if i in hbm else pltpu.VMEM) for i in range(len(args))]
    args = [pltpu.with_memory_space_constraint(arg, pltpu.HBM) if i in hbm else arg for i, arg in enumerate(args)]
    return pl.pallas_call(
        kernel,
        out_shape=[jax.ShapeDtypeStruct(shape, kind) for shape, kind in outs],
        in_specs=space,
        out_specs=[pl.BlockSpec(memory_space=pltpu.VMEM)] * len(outs),
        scratch_shapes=list(scratch),
        compiler_params=pltpu.CompilerParams(vmem_limit_bytes=VMEM_LIMIT),
        cost_estimate=pl.CostEstimate(flops=flops, bytes_accessed=moved, transcendentals=0),
        name=name,
    )(*args)


def body(
    query_in,
    key_in,
    value_in,
    gate_in,
    conv_query,
    conv_key,
    conv_value,
    decay_in,
    beta_in,
    norm_gain,
    doc_lengths,
    out_weight,
):
    rows = query_in.shape[0]
    ctx_count, head_count = lax.axis_size("ctx"), lax.axis_size("head")
    heads = decay_in.shape[0] // 2
    key_width, value_width = key_in.shape[1] // 2, value_in.shape[1] // 2
    half_width = 2 * key_width + value_width
    width = out_weight.shape[1] // head_count
    longest = ctx_count * rows // 4
    hops = -(-(longest - 1) // (2 * rows))

    swap = [(i, i ^ 1) for i in range(ctx_count)]
    ahead_1 = [(i, (i + 1) % ctx_count) for i in range(ctx_count)]
    even_swap = [(i, i ^ 2) for i in range(ctx_count)]
    odd_swap = [
        (c * head_count + h, (((c + 2) ^ 2) - 2) * head_count + h if 2 <= c < ctx_count - 2 else c * head_count + (h ^ 1))
        for c in range(ctx_count)
        for h in range(head_count)
    ]
    far_ahead = [
        (c * head_count + h, (c + 2) % ctx_count * head_count + h if c % 2 else c * head_count + (h ^ 1))
        for c in range(ctx_count)
        for h in range(head_count)
    ]


    edge, pack, gates = call(
        pack_kernel,
        [((EDGE, half_width), BF16), ((rows + EDGE, key_width + value_width), BF16), ((2 * heads, rows), F32)],
        (query_in, key_in, value_in, decay_in, beta_in),
        "pack",
        hbm=range(5),
        scratch=(pltpu.VMEM((2,) + decay_in.shape, F32), pltpu.SemaphoreType.DMA((7,))),
    )
    own_edge, late, own, weights, own_gate, down, along = call(
        early_kernel,
        [
            ((EDGE, half_width), BF16),
            ((rows, key_width + value_width), BF16),
            ((rows, half_width), BF16),
            ((conv_query.shape[0], half_width), F32),
            ((rows, value_width), BF16),
            ((2 * rows + 8, 128), jnp.int32),
            ((8, 2 * rows), jnp.int32),
        ],
        (query_in, key_in, value_in, gate_in, conv_query, conv_key, conv_value, doc_lengths),
        "early",
        hbm=range(8),
        scratch=(pltpu.SMEM(doc_lengths.shape, jnp.int32), pltpu.SemaphoreType.DMA((13,))),
        flops=10_000_000_000,
        moved=2_000_000,
    )
    got_edge = lax.ppermute(edge, "ctx", ahead_1)
    got_pack = lax.ppermute(pack, "ctx", swap)
    got_far_edge = lax.ppermute(own_edge, ("ctx", "head"), far_ahead)

    square = (heads, DK, DV)
    own_state, own_map, own_out, own_through = call(
        own_kernel,
        [(square, F32), (square, BF16), ((rows, value_width), F32), ((rows, value_width), BF16)],
        (down, along, own, weights, gates, got_edge),
        "own_terms",
        flops=1_000_000,
        moved=4_000_000,
    )
    late, own_map = lax.optimization_barrier((late, own_map))
    got_late = lax.ppermute(late, "ctx", swap)
    peer = call(
        peer_kernel,
        [
            (square, F32),
            (square, BF16),
            ((heads, rows, DK + DV), BF16),
            ((heads, rows, rows), F32),
            ((heads, rows, DK), F32),
            ((heads // 2, DK, rows), BF16),
            (square, BF16),
        ]
        + ([(square, BF16)] if hops > 1 else []),
        (down, along, got_pack, own_edge, got_far_edge, weights, own_state, own_map),
        "peer_terms",
        flops=2_000_000_000,
        moved=4_000_000,
    )
    state, map_, solved, decay, start, key, end = peer[:7]
    def from_earlier(value):
        return lax.ppermute(value, "ctx", even_swap), lax.ppermute(value, ("ctx", "head"), odd_swap)

    entering = from_earlier(end)
    for _ in range(hops - 1):
        earlier = jnp.where(lax.axis_index("ctx") // 2 % 2 == 1, *entering)
        moved = jnp.einsum("hij,hjk->hik", peer[7], earlier, preferred_element_type=F32)
        moved = jnp.where(lax.axis_index("ctx") < 2, 0.0, moved)
        entering = from_earlier((end.astype(F32) + moved).astype(BF16))
    out, through, weight = call(
        local_kernel,
        [((2 * rows, value_width), F32), ((2 * rows, value_width), BF16), ((value_width, out_weight.shape[1]), BF16)],
        (own_state, own_map, own_out, own_through, state, map_, solved, decay, start, key, down, along, got_late, own_edge,
         got_far_edge, weights, out_weight),
        "local_outputs",
        hbm=(16,),
        scratch=(pltpu.SemaphoreType.DMA((PARTS,)),),
        flops=1_000_000_000,
        moved=4_000_000,
    )
    cores = [(i, i ^ 1) for i in range(head_count)]
    mixed, send_far, keep_far = call(
        mix_kernel,
        [((2 * rows, value_width), BF16), ((rows, width), BF16), ((rows, width), BF16)],
        (out, through, *entering, own_gate, got_late, norm_gain.reshape(1, DV), weight),
        "mix",
    )
    got_far = lax.ppermute(send_far, "head", cores)
    send, keep = call(
        project_kernel,
        [((3, rows, width), BF16), ((3, rows, width), BF16)],
        (mixed, weight),
        "project",
        flops=2_000_000_000,
        moved=4_000_000,
    )
    send, got_far = lax.optimization_barrier((send, got_far))
    got = lax.ppermute(send, "head", cores)
    (to_xy,) = call(core_sum_kernel, [((rows, width), BF16)], (keep_far, got_far), "core_sum_xy")
    mine, to_x, to_y = call(
        core_sums_kernel,
        [((rows, width), F32), ((rows, width), BF16), ((rows, width), BF16)],
        (keep, got),
        "core_sums",
    )
    both = [
        (c * head_count + h, (c ^ 1) * head_count + (h ^ 2)) for c in range(ctx_count) for h in range(head_count)
    ]
    got_xy = lax.ppermute(to_xy, ("ctx", "head"), both)
    got_x = lax.ppermute(to_x, "head", [(i, i ^ 2) for i in range(head_count)])
    got_y = lax.ppermute(to_y, "ctx", swap)
    (projected,) = call(
        last_kernel, [((width, rows), BF16)], (mine, got_x, got_y, got_xy), "last_sum"
    )
    return projected


def solution(mesh):
    return jax.shard_map(
        body,
        mesh=mesh,
        in_specs=(
            P("ctx", "head"),
            P("ctx", "head"),
            P("ctx", "head"),
            P("ctx", "head"),
            P(None, "head"),
            P(None, "head"),
            P(None, "head"),
            P("head", "ctx"),
            P("head", "ctx"),
            P(),
            P(),
            P("head", None),
        ),
        out_specs=P("head", "ctx"),
        check_vma=False,
    )
```

```python
import jax
import jax.numpy as jnp
from jax import lax
from jax.experimental import pallas as pl
from jax.experimental.pallas import tpu as pltpu
from jax.sharding import PartitionSpec as P

DK = 128
DV = 128
EDGE = 16
PARTS = 8
F32 = jnp.float32
BF16 = jnp.bfloat16
VMEM_LIMIT = 48 * 1024 * 1024


def dot(a, b):
    return jnp.dot(a.astype(BF16), b.astype(BF16), preferred_element_type=F32)


def dot_nt(a, b):
    dims = (((1,), (1,)), ((), ()))
    return lax.dot_general(a.astype(BF16), b.astype(BF16), dims, preferred_element_type=F32)


def exact_dot(a, b):
    return jnp.dot(a, b, precision=lax.Precision.HIGHEST, preferred_element_type=F32)


def where_y(flag, a, b):
    return jnp.where(flag == 1, a, b)


def document_counts(doc_ref, base, rows, lanes):
    down = lax.broadcasted_iota(jnp.int32, (rows + 8, lanes), 0) + (base - 8)
    along = lax.broadcasted_iota(jnp.int32, (8, rows), 1) + base
    docs = doc_ref.shape[0]

    def one(d, carried):
        start, count_down, count_along = carried
        count_down = count_down + (down >= start).astype(jnp.int32)
        count_along = count_along + (along >= start).astype(jnp.int32)
        return start + doc_ref[d], count_down, count_along

    state = (jnp.int32(0), jnp.zeros_like(down), jnp.zeros_like(along))
    if docs <= 16:
        for d in range(docs):
            state = one(d, state)
    else:
        state = lax.fori_loop(0, docs, one, state)
    return state[1], state[2]


def three_terms(value):
    high = value.astype(BF16)
    rest = value - high.astype(F32)
    middle = rest.astype(BF16)
    low = (rest - middle.astype(F32)).astype(BF16)
    return high, middle, low


class Copies:
    def __init__(self, sems):
        self.sems, self.started = sems, []

    def start(self, source, target):
        self.started.append(pltpu.make_async_copy(source, target, self.sems.at[len(self.started)]))
        self.started[-1].start()

    def wait(self, first=0, last=None):
        for one in self.started[first:last]:
            one.wait()


def half_columns(ref, which):
    width = ref.shape[1] // 2
    return pl.ds(pl.multiple_of(which * width, width), width)


def pack_kernel(q_ref, k_ref, v_ref, decay_ref, beta_ref, edge_ref, pack_ref, gates_ref, raw_gates, sems):
    other = 1 - lax.axis_index("ctx") % 2
    rows = q_ref.shape[0]
    heads = decay_ref.shape[0] // 2
    copies = Copies(sems)
    copies.start(decay_ref, raw_gates.at[0])
    copies.start(beta_ref, raw_gates.at[1])
    at = 0
    for ref in (q_ref, k_ref, v_ref):
        width = ref.shape[1] // 2
        copies.start(ref.at[pl.ds(rows - EDGE, EDGE), half_columns(ref, other)], edge_ref.at[:, pl.ds(at, width)])
        at += width
    at = 0
    for ref in (k_ref, v_ref):
        width = ref.shape[1] // 2
        copies.start(ref.at[:, half_columns(ref, other)], pack_ref.at[pl.ds(0, rows), pl.ds(at, width)])
        at += width
    pack_ref[rows : rows + EDGE, :] = jnp.zeros((EDGE, pack_ref.shape[1]), BF16)
    copies.wait(0, 2)
    decay = raw_gates[0]
    log_gamma = -(jnp.maximum(decay, 0.0) + jnp.log1p(jnp.exp(-jnp.abs(decay))))
    upper = lax.broadcasted_iota(jnp.int32, (rows, rows), 0) <= lax.broadcasted_iota(jnp.int32, (rows, rows), 1)
    sums = exact_dot(log_gamma, upper.astype(F32))
    beta = 1.0 / (1.0 + jnp.exp(-raw_gates[1]))
    at = 0
    for i, value in enumerate((sums, beta)):
        gates_ref[i * heads : i * heads + heads] = where_y(other, value[:heads], value[heads:])
        for term in three_terms(where_y(other, value[heads:], value[:heads])):
            pack_ref[rows : rows + heads, at : at + rows] = term
            at += rows
    copies.wait(2)


def early_kernel(q_ref, k_ref, v_ref, g_ref, cq_ref, ck_ref, cv_ref, doc_hbm,
                 own_edge_ref, late_ref, own_ref, weight_ref, own_gate_ref, down_ref, along_ref, doc_ref, sems):
    ctx = lax.axis_index("ctx")
    y = ctx % 2
    rows = q_ref.shape[0]
    copies = Copies(sems)
    copies.start(doc_hbm, doc_ref)
    at = 0
    for ref, weights in ((q_ref, cq_ref), (k_ref, ck_ref), (v_ref, cv_ref)):
        width = ref.shape[1] // 2
        here = pl.ds(at, width)
        copies.start(ref.at[pl.ds(rows - EDGE, EDGE), half_columns(ref, y)], own_edge_ref.at[:, here])
        copies.start(ref.at[:, half_columns(ref, y)], own_ref.at[:, here])
        copies.start(weights.at[:, half_columns(ref, y)], weight_ref.at[:, here])
        at += width
    key_width = q_ref.shape[1] // 2
    copies.start(q_ref.at[:, half_columns(q_ref, 1 - y)], late_ref.at[:, pl.ds(0, key_width)])
    copies.start(g_ref.at[:, half_columns(g_ref, 1 - y)], late_ref.at[:, pl.ds(key_width, g_ref.shape[1] // 2)])
    copies.start(g_ref.at[:, half_columns(g_ref, y)], own_gate_ref)
    copies.wait(0, 1)
    down_ref[...], along_ref[...] = document_counts(doc_ref, (ctx - y) * rows, 2 * rows, 128)
    copies.wait(1)


def conv_silu(halo, current, weight, keeps):
    rows = current.shape[0]
    padded = jnp.concatenate([halo.astype(F32)[EDGE - 8 :], current.astype(F32)], axis=0)
    margin = weight.shape[0] - 1
    summed = weight[margin : margin + 1] * padded[8:]
    for lag in range(1, margin + 1):
        summed = summed + weight[margin - lag : margin - lag + 1] * padded[8 - lag : 8 - lag + rows] * keeps[lag]
    return summed / (1.0 + jnp.exp(-summed))


def inverse_norms(vectors, axis):
    return lax.rsqrt(jnp.sum(vectors * vectors, axis=axis, keepdims=True) + 1e-6)


def odd_blocks(value, reach):
    return jnp.concatenate([value[at : at + reach] for at in range(reach, value.shape[0], 2 * reach)], axis=0)


def at_odd_blocks(value, reach):
    parts = []
    for at in range(0, value.shape[0], reach):
        parts += [jnp.zeros((reach, value.shape[1]), value.dtype), value[at : at + reach]]
    return jnp.concatenate(parts, axis=0)


def keep_masks(seg_down):
    seg = seg_down[8:]
    return [None] + [(seg_down[8 - lag : 8 - lag + seg.shape[0]] == seg).astype(F32) for lag in (1, 2, 3)]


def solve_terms(lower):
    rows = lower[0].shape[0]
    small, large = rows // 8, rows // 4
    row = lax.broadcasted_iota(jnp.int32, (rows, rows), 0)
    col = lax.broadcasted_iota(jnp.int32, (rows, rows), 1)
    power = [jnp.where(row // small == col // small, -x, 0.0) for x in lower]
    eye = (row == col).astype(F32)
    inverse = [eye + x for x in power]
    power = [x.astype(BF16) for x in power]
    power = [dot(x, x).astype(BF16) for x in power]
    reach = 4
    while reach < small:
        following = [dot(x, x).astype(BF16) for x in power]
        inverse = [x + dot(x, p) for x, p in zip(inverse, power)]
        power = following
        reach *= 2
    inverse = [x + dot(x, p) for x, p in zip(inverse, power)]
    here = (row // large == col // large) & (row // small != col // small)
    moved = [dot(odd_blocks(jnp.where(here, x, 0.0), small), i) for x, i in zip(lower, inverse)]
    moved = [dot(odd_blocks(i, small), at_odd_blocks(m, small)) for i, m in zip(inverse, moved)]
    inverse = [(i - at_odd_blocks(m, small)).astype(BF16) for i, m in zip(inverse, moved)]
    rest = [jnp.where(row // large == col // large, 0.0, -x) for x in lower]
    once = [dot(i, r).astype(BF16) for i, r in zip(inverse, rest)]
    return inverse, once


def block_terms(seg_down, seg_along, halo, k, v, weights, sums, beta):
    heads, rows = sums.shape
    key_heads = heads // 2
    seg = seg_down[8:]
    keeps = keep_masks(seg_down)
    before = seg_down[7:8]
    last = seg_down[rows + 7 : rows + 8]
    row = lax.broadcasted_iota(jnp.int32, (rows, rows), 0)
    col = lax.broadcasted_iota(jnp.int32, (rows, rows), 1)
    same = (seg == seg_along[0:1]) & (row >= col)
    stacked = jnp.concatenate([sums, beta, jnp.zeros((rows - 2 * heads, rows), F32)], axis=0)
    columns = stacked.T

    raw = [conv_silu(halo(1, g), k(g), weights(1, g), keeps) for g in range(key_heads)]
    grams = [dot_nt(key, key) for key in raw]
    raw_t = [key.T for key in raw]
    norms = [inverse_norms(key, 1) for key in raw]
    norms_t = [inverse_norms(key, 0) for key in raw_t]
    keys = [key * norm for key, norm in zip(raw, norms)]
    keys_t = [key * norm for key, norm in zip(raw_t, norms_t)]
    values = [conv_silu(halo(2, g), v(g), weights(2, g), keeps) for g in range(heads)]
    keys_t16 = [key.astype(BF16) for key in keys_t]

    lower, decays, right, start_keys, starts, ends, throughs = [], [], [], [], [], [], []
    for h in range(heads):
        g = h // 2
        down = jnp.broadcast_to(columns[:, h : h + 1], (rows, rows))
        beta_down = jnp.broadcast_to(columns[:, heads + h : heads + h + 1], (rows, rows))
        along = sums[h : h + 1]
        end = jnp.broadcast_to(columns[rows - 1 : rows, h : h + 1], (1, rows))
        decay = jnp.exp(jnp.where(same, down - along, -1e30))
        decays.append(decay)
        factor = jnp.where(row > col, beta_down * norms[g] * decay * norms_t[g], 0.0)
        lower.append(factor * grams[g])
        start = jnp.where(seg == before, jnp.exp(down), 0.0)
        starts.append(start)
        right.append(beta_down * values[h])
        start_keys.append((beta_down * start * keys[g]).astype(BF16))
        ends.append((keys_t[g] * jnp.where(seg_along[0:1] == last, jnp.exp(end - along), 0.0)).astype(BF16))
        throughs.append(jnp.where(last == before, jnp.exp(end), 0.0))

    return lower, right, start_keys, ends, throughs, decays, starts, keys_t16


def solved_with(inverse, once, right):
    result = [dot(i, r) for i, r in zip(inverse, right)]
    twice = [dot(m, m).astype(BF16) for m in once]
    result = [r + dot(m, r) for m, r in zip(once, result)]
    return [(r + dot(m, r)).astype(BF16) for m, r in zip(twice, result)], twice


def scaled_eye(scale):
    row = lax.broadcasted_iota(jnp.int32, (DK, DK), 0)
    col = lax.broadcasted_iota(jnp.int32, (DK, DK), 1)
    return jnp.where(row == col, scale, 0.0)


def query_terms(seg_down, halo, q, weights, decays, starts, keys_t):
    keeps = keep_masks(seg_down)
    queries = [conv_silu(halo(0, g), q(g), weights(0, g), keeps) for g in range(len(keys_t))]
    scores = [dot(query, key_t) for query, key_t in zip(queries, keys_t)]
    norms = [inverse_norms(query, 1) for query in queries]
    queries = [query * norm for query, norm in zip(queries, norms)]
    inside = [(scores[h // 2] * (norms[h // 2] * decays[h])).astype(BF16) for h in range(len(decays))]
    return inside, [queries[h // 2] * starts[h] for h in range(len(decays))]


def groups(heads):
    at = (0, heads // 2 * DK, heads * DK)
    return lambda which, g: slice(at[which] + g * 128, at[which] + g * 128 + 128)


def counts(down_ref, along_ref, block, rows):
    at = pl.multiple_of(block * rows, rows)
    return down_ref[pl.ds(at, rows + 8), :], along_ref[:, pl.ds(at, rows)]


def own_kernel(down_ref, along_ref, own_ref, weight_ref, gates_ref, halo_ref,
               state_ref, map_ref, out_ref, through_ref):
    rows = own_ref.shape[0]
    heads = gates_ref.shape[0] // 2
    columns = groups(heads)
    seg_down, seg_along = counts(down_ref, along_ref, lax.axis_index("ctx") % 2, rows)

    def halo(which, g):
        return halo_ref[:, columns(which, g)]

    def weights(which, g):
        return weight_ref[:, columns(which, g)]

    lower, right, start_keys, ends, throughs, decays, starts, keys_t = block_terms(
        seg_down,
        seg_along,
        halo,
        lambda g: own_ref[:, columns(1, g)],
        lambda g: own_ref[:, columns(2, g)],
        weights,
        gates_ref[0:heads],
        gates_ref[heads:],
    )
    inverse, once = solve_terms(lower)
    inside, start_queries = query_terms(
        seg_down, halo, lambda g: own_ref[:, columns(0, g)], weights, decays, starts, keys_t
    )
    both = [jnp.concatenate([r.astype(BF16), k], axis=1) for r, k in zip(right, start_keys)]
    solved, _ = solved_with(inverse, once, both)
    ended = [dot(e, s) for e, s in zip(ends, solved)]
    result = [dot(i, s) for i, s in zip(inside, solved)]
    for h in range(heads):
        state_ref[h] = ended[h][:, :DV]
        map_ref[h] = (scaled_eye(throughs[h]) - ended[h][:, DV:]).astype(BF16)
        out_ref[:, h * DV : h * DV + DV] = result[h][:, :DV]
        through_ref[:, h * DK : h * DK + DK] = (start_queries[h] - result[h][:, DV:]).astype(BF16)


def peer_halo(own_edge_ref, edge_ref, columns):
    y = lax.axis_index("ctx") % 2
    return lambda which, g: where_y(y, edge_ref[:, columns(which, g)], own_edge_ref[:, columns(which, g)])


def peer_kernel(down_ref, along_ref, pack_ref, own_edge_ref, edge_ref, weight_ref, own_state_ref, own_map_ref,
                state_ref, solved_ref, solver_ref, start_key_ref, ended_ref, passing_ref, decay_ref, start_ref, key_ref,
                pair_state_ref, *pair_map_ref):
    y = lax.axis_index("ctx") % 2
    rows = pack_ref.shape[0] - EDGE
    heads = own_state_ref.shape[0]
    columns = groups(heads)
    key_width = heads // 2 * DK
    gates = [
        sum(pack_ref[rows : rows + heads, (3 * part + i) * rows : (3 * part + i + 1) * rows].astype(F32) for i in range(3))
        for part in range(2)
    ]
    lower, right, start_keys, ends, throughs, decays, starts, keys_t = block_terms(
        *counts(down_ref, along_ref, 1 - y, rows),
        peer_halo(own_edge_ref, edge_ref, columns),
        lambda g: pack_ref[0:rows, g * DK : g * DK + DK],
        lambda g: pack_ref[0:rows, key_width + g * DV : key_width + g * DV + DV],
        lambda which, g: weight_ref[:, columns(which, g)],
        gates[0],
        gates[1],
    )
    entering = [where_y(y, jnp.zeros((DK, DV), F32), own_state_ref[h]) for h in range(heads)]
    right = [r - dot(k, e) for r, k, e in zip(right, start_keys, entering)]
    inverse, once = solve_terms(lower)
    solved, twice = solved_with(inverse, once, right)
    ended = [dot(e, s) for e, s in zip(ends, solved)]
    states = [t * e + s for t, e, s in zip(throughs, entering, ended)]
    moved = [dot(own_map_ref[h], states[h]) for h in range(heads)]
    for h in range(heads):
        pair_state_ref[h] = where_y(y, own_state_ref[h] + moved[h], states[h]).astype(BF16)
        state_ref[h] = states[h].astype(BF16)
    if pair_map_ref:
        solved_keys, _ = solved_with(inverse, once, start_keys)
        for h in range(heads):
            own_map = own_map_ref[h]
            peer_map = scaled_eye(throughs[h]) - dot(ends[h], solved_keys[h])
            pair_map_ref[0][h] = where_y(y, dot(own_map, peer_map), dot(peer_map, own_map)).astype(BF16)
    solver = (inverse, once, twice)
    for h in range(heads):
        solved_ref[h] = solved[h]
        for i in range(3):
            solver_ref[i * heads + h] = solver[i][h]
        start_key_ref[h] = start_keys[h]
        ended_ref[h] = ends[h]
        passing_ref[h : h + 1] = throughs[h]
        decay_ref[h] = decays[h]
        start_ref[h] = starts[h]
    for g in range(heads // 2):
        key_ref[g] = keys_t[g]


def passing_kernel(solver_ref, start_key_ref, ended_ref, passing_ref, weight_hbm, solved_ref, map_ref, weight_ref, sems):
    depth = weight_ref.shape[0]
    copies = Copies(sems)
    part = depth // PARTS
    for i in range(PARTS):
        from_row = pl.multiple_of(lax.axis_index("ctx") % 2 * depth + i * part, part)
        copies.start(weight_hbm.at[pl.ds(from_row, part), :], weight_ref.at[pl.ds(i * part, part), :])
    heads = start_key_ref.shape[0]
    every = range(heads)
    inverse, once, twice = ([solver_ref[i * heads + h] for h in every] for i in range(3))
    solved = [dot(inverse[h], start_key_ref[h]) for h in every]
    solved = [k + dot(m, k) for m, k in zip(once, solved)]
    solved = [(k + dot(m, k)).astype(BF16) for m, k in zip(twice, solved)]
    ended = [dot(ended_ref[h], solved[h]) for h in every]
    for h in every:
        solved_ref[h] = solved[h]
        map_ref[h] = (scaled_eye(passing_ref[h : h + 1]) - ended[h]).astype(BF16)
    copies.wait()


def local_kernel(own_state_ref, own_map_ref, own_out_ref, own_through_ref, state_ref, map_ref, solved_ref, solved_key_ref,
                 decay_ref, start_ref, key_ref, down_ref, along_ref, late_ref, own_edge_ref, edge_ref, conv_ref,
                 out_ref, through_ref):
    y = lax.axis_index("ctx") % 2
    rows = own_out_ref.shape[0]
    heads = own_state_ref.shape[0]
    columns = groups(heads)
    inside, start_queries = query_terms(
        counts(down_ref, along_ref, 1 - y, rows)[0],
        peer_halo(own_edge_ref, edge_ref, columns),
        lambda g: late_ref[:, g * DK : g * DK + DK],
        lambda which, g: conv_ref[:, columns(which, g)],
        [decay_ref[h] for h in range(heads)],
        [start_ref[h] for h in range(heads)],
        [key_ref[g] for g in range(heads // 2)],
    )
    every = range(heads)
    outs = [dot(inside[h], solved_ref[h]) for h in every]
    passed = [dot(inside[h], solved_key_ref[h]) for h in every]
    state_0 = [where_y(y, state_ref[h], own_state_ref[h].astype(BF16)) for h in every]
    own_throughs = [own_through_ref[:, h * DK : h * DK + DK] for h in every]
    extra = [dot(where_y(y, own_throughs[h], start_queries[h].astype(BF16)), state_0[h]) for h in every]
    throughs = [(start_queries[h] - passed[h]).astype(BF16) for h in every]
    moved = [
        dot(where_y(y, own_throughs[h], throughs[h]), where_y(y, map_ref[h], own_map_ref[h])).astype(BF16) for h in every
    ]
    for h in every:
        lanes = slice(h * DV, h * DV + DV)
        out_ref[0:rows, lanes] = own_out_ref[:, lanes] + where_y(y, extra[h], jnp.zeros_like(extra[h]))
        out_ref[rows:, lanes] = outs[h] + where_y(y, jnp.zeros_like(extra[h]), extra[h])
        through_ref[0:rows, lanes] = where_y(y, moved[h], own_throughs[h])
        through_ref[rows:, lanes] = where_y(y, throughs[h], moved[h])


def feature_columns(weight_ref, other_core, other_x):
    head = lax.axis_index("head")
    core, x = head % 2, head // 2
    block = (x + other_x - 2 * x * other_x) * 2 + core + other_core - 2 * core * other_core
    width = weight_ref.shape[1] // lax.axis_size("head")
    return weight_ref[:, pl.ds(pl.multiple_of(block * width, width), width)]


def mix_kernel(out_ref, through_ref, even_ref, odd_ref, gate_ref, late_ref, gain_ref, weight_ref, mixed_ref, send_ref, keep_ref):
    from_even = lax.axis_index("ctx") // 2 % 2
    heads = even_ref.shape[0]
    rows = gate_ref.shape[0]
    key_width = late_ref.shape[1] - heads * DV
    for h in range(heads):
        lanes = slice(h * DV, h * DV + DV)
        o = out_ref[:, lanes] + dot(through_ref[:, lanes], where_y(from_even, even_ref[h], odd_ref[h]))
        gate = jnp.concatenate([gate_ref[:, lanes], late_ref[:, key_width + h * DV : key_width + h * DV + DV]], axis=0)
        gate = gate.astype(F32)
        scale = lax.rsqrt(jnp.mean(o * o, axis=-1, keepdims=True) + 1e-6)
        mixed_ref[:, lanes] = (o * scale * gain_ref[...] * (gate / (1.0 + jnp.exp(-gate)))).astype(BF16)
    send_ref[...] = jnp.dot(mixed_ref[rows:, :], feature_columns(weight_ref, 1, 1), preferred_element_type=F32).astype(BF16)
    keep_ref[...] = jnp.dot(mixed_ref[rows:, :], feature_columns(weight_ref, 0, 1), preferred_element_type=F32).astype(BF16)


QUARTERS = ((0, 0), (0, 1), (1, 0))


def project_kernel(mixed_ref, weight_ref, send_ref, keep_ref):
    rows = send_ref.shape[1]
    for c, to_ref in ((0, send_ref), (1, keep_ref)):
        for i, (peer, far) in enumerate(QUARTERS):
            weights = feature_columns(weight_ref, 1 - c, far)
            product = jnp.dot(mixed_ref[peer * rows : peer * rows + rows, :], weights, preferred_element_type=F32)
            to_ref[i] = product.astype(BF16)


def core_sum_kernel(keep_ref, got_ref, xy_ref):
    xy_ref[...] = (keep_ref[...].astype(F32) + got_ref[...].astype(F32)).astype(BF16)


def core_sums_kernel(keep_ref, got_ref, mine_ref, x_ref, y_ref):
    for i, ref in enumerate((mine_ref, x_ref, y_ref)):
        ref[...] = (keep_ref[i].astype(F32) + got_ref[i].astype(F32)).astype(ref.dtype)


def last_kernel(mine_ref, x_ref, y_ref, xy_ref, out_ref):
    total = mine_ref[...] + x_ref[...].astype(F32) + (y_ref[...].astype(F32) + xy_ref[...].astype(F32))
    out_ref[...] = total.T.astype(BF16)


def call(kernel, outs, args, name, hbm=(), scratch=(), flops=0, moved=0):
    space = [pl.BlockSpec(memory_space=pltpu.HBM if i in hbm else pltpu.VMEM) for i in range(len(args))]
    args = [pltpu.with_memory_space_constraint(arg, pltpu.HBM) if i in hbm else arg for i, arg in enumerate(args)]
    return pl.pallas_call(
        kernel,
        out_shape=[jax.ShapeDtypeStruct(shape, kind) for shape, kind in outs],
        in_specs=space,
        out_specs=[pl.BlockSpec(memory_space=pltpu.VMEM)] * len(outs),
        scratch_shapes=list(scratch),
        compiler_params=pltpu.CompilerParams(vmem_limit_bytes=VMEM_LIMIT),
        cost_estimate=pl.CostEstimate(flops=flops, bytes_accessed=moved, transcendentals=0),
        name=name,
    )(*args)


def body(
    query_in,
    key_in,
    value_in,
    gate_in,
    conv_query,
    conv_key,
    conv_value,
    decay_in,
    beta_in,
    norm_gain,
    doc_lengths,
    out_weight,
):
    rows = query_in.shape[0]
    ctx_count, head_count = lax.axis_size("ctx"), lax.axis_size("head")
    heads = decay_in.shape[0] // 2
    key_width, value_width = key_in.shape[1] // 2, value_in.shape[1] // 2
    half_width = 2 * key_width + value_width
    width = out_weight.shape[1] // head_count
    longest = ctx_count * rows // 4
    hops = -(-(longest - 1) // (2 * rows))

    swap = [(i, i ^ 1) for i in range(ctx_count)]
    ahead_1 = [(i, (i + 1) % ctx_count) for i in range(ctx_count)]
    even_swap = [(i, i ^ 2) for i in range(ctx_count)]
    odd_swap = [
        (c * head_count + h, (((c + 2) ^ 2) - 2) * head_count + h if 2 <= c < ctx_count - 2 else c * head_count + (h ^ 1))
        for c in range(ctx_count)
        for h in range(head_count)
    ]
    far_ahead = [
        (c * head_count + h, (c + 2) % ctx_count * head_count + h if c % 2 else c * head_count + (h ^ 1))
        for c in range(ctx_count)
        for h in range(head_count)
    ]


    edge, pack, gates = call(
        pack_kernel,
        [((EDGE, half_width), BF16), ((rows + EDGE, key_width + value_width), BF16), ((2 * heads, rows), F32)],
        (query_in, key_in, value_in, decay_in, beta_in),
        "pack",
        hbm=range(5),
        scratch=(pltpu.VMEM((2,) + decay_in.shape, F32), pltpu.SemaphoreType.DMA((7,))),
    )
    own_edge, late, own, weights, own_gate, down, along = call(
        early_kernel,
        [
            ((EDGE, half_width), BF16),
            ((rows, key_width + value_width), BF16),
            ((rows, half_width), BF16),
            ((conv_query.shape[0], half_width), F32),
            ((rows, value_width), BF16),
            ((2 * rows + 8, 128), jnp.int32),
            ((8, 2 * rows), jnp.int32),
        ],
        (query_in, key_in, value_in, gate_in, conv_query, conv_key, conv_value, doc_lengths),
        "early",
        hbm=range(8),
        scratch=(pltpu.SMEM(doc_lengths.shape, jnp.int32), pltpu.SemaphoreType.DMA((13,))),
        flops=10_000_000_000,
        moved=2_000_000,
    )
    got_edge = lax.ppermute(edge, "ctx", ahead_1)
    got_pack = lax.ppermute(pack, "ctx", swap)
    got_far_edge = lax.ppermute(own_edge, ("ctx", "head"), far_ahead)

    square = (heads, DK, DV)
    own_state, own_map, own_out, own_through = call(
        own_kernel,
        [(square, F32), (square, BF16), ((rows, value_width), F32), ((rows, value_width), BF16)],
        (down, along, own, weights, gates, got_edge),
        "own_terms",
        flops=1_000_000,
        moved=4_000_000,
    )
    late, own_map = lax.optimization_barrier((late, own_map))
    got_late = lax.ppermute(late, "ctx", swap)
    peer = call(
        peer_kernel,
        [
            (square, BF16),
            ((heads, rows, DV), BF16),
            ((3 * heads, rows, rows), BF16),
            ((heads, rows, DK), BF16),
            ((heads, DK, rows), BF16),
            ((heads, rows), F32),
            ((heads, rows, rows), F32),
            ((heads, rows, DK), F32),
            ((heads // 2, DK, rows), BF16),
            (square, BF16),
        ]
        + ([(square, BF16)] if hops > 1 else []),
        (down, along, got_pack, own_edge, got_far_edge, weights, own_state, own_map),
        "peer_terms",
        flops=2_000_000_000,
        moved=4_000_000,
    )
    end = peer[9]
    def from_earlier(value):
        return lax.ppermute(value, "ctx", even_swap), lax.ppermute(value, ("ctx", "head"), odd_swap)

    entering = from_earlier(end)
    for _ in range(hops - 1):
        earlier = jnp.where(lax.axis_index("ctx") // 2 % 2 == 1, *entering)
        moved = jnp.einsum("hij,hjk->hik", peer[10], earlier, preferred_element_type=F32)
        moved = jnp.where(lax.axis_index("ctx") < 2, 0.0, moved)
        entering = from_earlier((end.astype(F32) + moved).astype(BF16))
    state, solved, solver, start_key, ended, passing, decay, start, key = peer[:9]
    solved_key, map_, weight = call(
        passing_kernel,
        [(square, BF16), (square, BF16), ((value_width, out_weight.shape[1]), BF16)],
        (solver, start_key, ended, passing, out_weight),
        "passing",
        hbm=(4,),
        scratch=(pltpu.SemaphoreType.DMA((PARTS,)),),
        flops=1_000_000_000,
        moved=4_000_000,
    )
    out, through = call(
        local_kernel,
        [((2 * rows, value_width), F32), ((2 * rows, value_width), BF16)],
        (own_state, own_map, own_out, own_through, state, map_, solved, solved_key, decay, start, key, down, along, got_late,
         own_edge, got_far_edge, weights),
        "local_outputs",
        flops=1_000_000_000,
        moved=4_000_000,
    )
    cores = [(i, i ^ 1) for i in range(head_count)]
    mixed, send_far, keep_far = call(
        mix_kernel,
        [((2 * rows, value_width), BF16), ((rows, width), BF16), ((rows, width), BF16)],
        (out, through, *entering, own_gate, got_late, norm_gain.reshape(1, DV), weight),
        "mix",
    )
    got_far = lax.ppermute(send_far, "head", cores)
    send, keep = call(
        project_kernel,
        [((3, rows, width), BF16), ((3, rows, width), BF16)],
        (mixed, weight),
        "project",
        flops=2_000_000_000,
        moved=4_000_000,
    )
    send, got_far = lax.optimization_barrier((send, got_far))
    got = lax.ppermute(send, "head", cores)
    (to_xy,) = call(core_sum_kernel, [((rows, width), BF16)], (keep_far, got_far), "core_sum_xy")
    mine, to_x, to_y = call(
        core_sums_kernel,
        [((rows, width), F32), ((rows, width), BF16), ((rows, width), BF16)],
        (keep, got),
        "core_sums",
    )
    both = [
        (c * head_count + h, (c ^ 1) * head_count + (h ^ 2)) for c in range(ctx_count) for h in range(head_count)
    ]
    got_xy = lax.ppermute(to_xy, ("ctx", "head"), both)
    got_x = lax.ppermute(to_x, "head", [(i, i ^ 2) for i in range(head_count)])
    got_y = lax.ppermute(to_y, "ctx", swap)
    (projected,) = call(
        last_kernel, [((width, rows), BF16)], (mine, got_x, got_y, got_xy), "last_sum"
    )
    return projected


def solution(mesh):
    return jax.shard_map(
        body,
        mesh=mesh,
        in_specs=(
            P("ctx", "head"),
            P("ctx", "head"),
            P("ctx", "head"),
            P("ctx", "head"),
            P(None, "head"),
            P(None, "head"),
            P(None, "head"),
            P("head", "ctx"),
            P("head", "ctx"),
            P(),
            P(),
            P("head", None),
        ),
        out_specs=P("head", "ctx"),
        check_vma=False,
    )
```

```python
import jax
import jax.numpy as jnp
from jax import lax
from jax.experimental import pallas as pl
from jax.experimental.pallas import tpu as pltpu
from jax.sharding import PartitionSpec as P

DK = 128
DV = 128
EDGE = 16
PARTS = 8
F32 = jnp.float32
BF16 = jnp.bfloat16
VMEM_LIMIT = 48 * 1024 * 1024


def dot(a, b):
    return jnp.dot(a.astype(BF16), b.astype(BF16), preferred_element_type=F32)


def dot_nt(a, b):
    dims = (((1,), (1,)), ((), ()))
    return lax.dot_general(a.astype(BF16), b.astype(BF16), dims, preferred_element_type=F32)


def exact_dot(a, b):
    return jnp.dot(a, b, precision=lax.Precision.HIGHEST, preferred_element_type=F32)


def where_y(flag, a, b):
    return jnp.where(flag == 1, a, b)


def document_counts(doc_ref, base, rows, lanes):
    down = lax.broadcasted_iota(jnp.int32, (rows + 8, lanes), 0) + (base - 8)
    along = lax.broadcasted_iota(jnp.int32, (8, rows), 1) + base
    docs = doc_ref.shape[0]

    def one(d, carried):
        start, count_down, count_along = carried
        count_down = count_down + (down >= start).astype(jnp.int32)
        count_along = count_along + (along >= start).astype(jnp.int32)
        return start + doc_ref[d], count_down, count_along

    state = (jnp.int32(0), jnp.zeros_like(down), jnp.zeros_like(along))
    if docs <= 16:
        for d in range(docs):
            state = one(d, state)
    else:
        state = lax.fori_loop(0, docs, one, state)
    return state[1], state[2]


def three_terms(value):
    high = value.astype(BF16)
    rest = value - high.astype(F32)
    middle = rest.astype(BF16)
    low = (rest - middle.astype(F32)).astype(BF16)
    return high, middle, low


class Copies:
    def __init__(self, sems):
        self.sems, self.started = sems, []

    def start(self, source, target):
        self.started.append(pltpu.make_async_copy(source, target, self.sems.at[len(self.started)]))
        self.started[-1].start()

    def wait(self, first=0, last=None):
        for one in self.started[first:last]:
            one.wait()


def half_columns(ref, which):
    width = ref.shape[1] // 2
    return pl.ds(pl.multiple_of(which * width, width), width)


def pack_kernel(q_ref, k_ref, v_ref, decay_ref, beta_ref, edge_ref, pack_ref, gates_ref, raw_gates, sems):
    other = 1 - lax.axis_index("ctx") % 2
    rows = q_ref.shape[0]
    heads = decay_ref.shape[0] // 2
    copies = Copies(sems)
    copies.start(decay_ref, raw_gates.at[0])
    copies.start(beta_ref, raw_gates.at[1])
    at = 0
    for ref in (q_ref, k_ref, v_ref):
        width = ref.shape[1] // 2
        copies.start(ref.at[pl.ds(rows - EDGE, EDGE), half_columns(ref, other)], edge_ref.at[:, pl.ds(at, width)])
        at += width
    at = 0
    for ref in (k_ref, v_ref):
        width = ref.shape[1] // 2
        copies.start(ref.at[:, half_columns(ref, other)], pack_ref.at[pl.ds(0, rows), pl.ds(at, width)])
        at += width
    pack_ref[rows : rows + EDGE, :] = jnp.zeros((EDGE, pack_ref.shape[1]), BF16)
    copies.wait(0, 2)
    decay = raw_gates[0]
    log_gamma = -(jnp.maximum(decay, 0.0) + jnp.log1p(jnp.exp(-jnp.abs(decay))))
    upper = lax.broadcasted_iota(jnp.int32, (rows, rows), 0) <= lax.broadcasted_iota(jnp.int32, (rows, rows), 1)
    sums = exact_dot(log_gamma, upper.astype(F32))
    beta = 1.0 / (1.0 + jnp.exp(-raw_gates[1]))
    at = 0
    for i, value in enumerate((sums, beta)):
        gates_ref[i * heads : i * heads + heads] = where_y(other, value[:heads], value[heads:])
        for term in three_terms(where_y(other, value[heads:], value[:heads])):
            pack_ref[rows : rows + heads, at : at + rows] = term
            at += rows
    copies.wait(2)


def early_kernel(q_ref, k_ref, v_ref, g_ref, cq_ref, ck_ref, cv_ref, doc_hbm,
                 own_edge_ref, late_ref, own_ref, weight_ref, own_gate_ref, down_ref, along_ref, doc_ref, sems):
    ctx = lax.axis_index("ctx")
    y = ctx % 2
    rows = q_ref.shape[0]
    copies = Copies(sems)
    copies.start(doc_hbm, doc_ref)
    at = 0
    for ref, weights in ((q_ref, cq_ref), (k_ref, ck_ref), (v_ref, cv_ref)):
        width = ref.shape[1] // 2
        here = pl.ds(at, width)
        copies.start(ref.at[pl.ds(rows - EDGE, EDGE), half_columns(ref, y)], own_edge_ref.at[:, here])
        copies.start(ref.at[:, half_columns(ref, y)], own_ref.at[:, here])
        copies.start(weights.at[:, half_columns(ref, y)], weight_ref.at[:, here])
        at += width
    key_width = q_ref.shape[1] // 2
    copies.start(q_ref.at[:, half_columns(q_ref, 1 - y)], late_ref.at[:, pl.ds(0, key_width)])
    copies.start(g_ref.at[:, half_columns(g_ref, 1 - y)], late_ref.at[:, pl.ds(key_width, g_ref.shape[1] // 2)])
    copies.start(g_ref.at[:, half_columns(g_ref, y)], own_gate_ref)
    copies.wait(0, 1)
    down_ref[...], along_ref[...] = document_counts(doc_ref, (ctx - y) * rows, 2 * rows, 128)
    copies.wait(1)


def conv_silu(halo, current, weight, keeps):
    rows = current.shape[0]
    padded = jnp.concatenate([halo.astype(F32)[EDGE - 8 :], current.astype(F32)], axis=0)
    margin = weight.shape[0] - 1
    summed = weight[margin : margin + 1] * padded[8:]
    for lag in range(1, margin + 1):
        summed = summed + weight[margin - lag : margin - lag + 1] * padded[8 - lag : 8 - lag + rows] * keeps[lag]
    return summed / (1.0 + jnp.exp(-summed))


def inverse_norms(vectors, axis):
    return lax.rsqrt(jnp.sum(vectors * vectors, axis=axis, keepdims=True) + 1e-6)


def odd_blocks(value, reach):
    return jnp.concatenate([value[at : at + reach] for at in range(reach, value.shape[0], 2 * reach)], axis=0)


def at_odd_blocks(value, reach):
    parts = []
    for at in range(0, value.shape[0], reach):
        parts += [jnp.zeros((reach, value.shape[1]), value.dtype), value[at : at + reach]]
    return jnp.concatenate(parts, axis=0)


def keep_masks(seg_down):
    seg = seg_down[8:]
    return [None] + [(seg_down[8 - lag : 8 - lag + seg.shape[0]] == seg).astype(F32) for lag in (1, 2, 3)]


def solve_terms(lower):
    rows = lower[0].shape[0]
    small, large = rows // 8, rows // 4
    row = lax.broadcasted_iota(jnp.int32, (rows, rows), 0)
    col = lax.broadcasted_iota(jnp.int32, (rows, rows), 1)
    power = [jnp.where(row // small == col // small, -x, 0.0) for x in lower]
    eye = (row == col).astype(F32)
    inverse = [eye + x for x in power]
    power = [x.astype(BF16) for x in power]
    power = [dot(x, x).astype(BF16) for x in power]
    reach = 4
    while reach < small:
        following = [dot(x, x).astype(BF16) for x in power]
        inverse = [x + dot(x, p) for x, p in zip(inverse, power)]
        power = following
        reach *= 2
    inverse = [x + dot(x, p) for x, p in zip(inverse, power)]
    here = (row // large == col // large) & (row // small != col // small)
    moved = [dot(odd_blocks(jnp.where(here, x, 0.0), small), i) for x, i in zip(lower, inverse)]
    moved = [dot(odd_blocks(i, small), at_odd_blocks(m, small)) for i, m in zip(inverse, moved)]
    inverse = [(i - at_odd_blocks(m, small)).astype(BF16) for i, m in zip(inverse, moved)]
    rest = [jnp.where(row // large == col // large, 0.0, -x) for x in lower]
    once = [dot(i, r).astype(BF16) for i, r in zip(inverse, rest)]
    return inverse, once


def block_terms(seg_down, seg_along, halo, k, v, weights, sums, beta):
    heads, rows = sums.shape
    key_heads = heads // 2
    seg = seg_down[8:]
    keeps = keep_masks(seg_down)
    before = seg_down[7:8]
    last = seg_down[rows + 7 : rows + 8]
    row = lax.broadcasted_iota(jnp.int32, (rows, rows), 0)
    col = lax.broadcasted_iota(jnp.int32, (rows, rows), 1)
    same = (seg == seg_along[0:1]) & (row >= col)
    stacked = jnp.concatenate([sums, beta, jnp.zeros((rows - 2 * heads, rows), F32)], axis=0)
    columns = stacked.T

    raw = [conv_silu(halo(1, g), k(g), weights(1, g), keeps) for g in range(key_heads)]
    grams = [dot_nt(key, key) for key in raw]
    raw_t = [key.T for key in raw]
    norms = [inverse_norms(key, 1) for key in raw]
    norms_t = [inverse_norms(key, 0) for key in raw_t]
    keys = [key * norm for key, norm in zip(raw, norms)]
    keys_t = [key * norm for key, norm in zip(raw_t, norms_t)]
    values = [conv_silu(halo(2, g), v(g), weights(2, g), keeps) for g in range(heads)]
    keys_t16 = [key.astype(BF16) for key in keys_t]

    lower, decays, right, start_keys, starts, ends, throughs = [], [], [], [], [], [], []
    for h in range(heads):
        g = h // 2
        down = jnp.broadcast_to(columns[:, h : h + 1], (rows, rows))
        beta_down = jnp.broadcast_to(columns[:, heads + h : heads + h + 1], (rows, rows))
        along = sums[h : h + 1]
        end = jnp.broadcast_to(columns[rows - 1 : rows, h : h + 1], (1, rows))
        decay = jnp.exp(jnp.where(same, down - along, -1e30))
        decays.append(decay)
        factor = jnp.where(row > col, beta_down * norms[g] * decay * norms_t[g], 0.0)
        lower.append(factor * grams[g])
        start = jnp.where(seg == before, jnp.exp(down), 0.0)
        starts.append(start)
        right.append(beta_down * values[h])
        start_keys.append((beta_down * start * keys[g]).astype(BF16))
        ends.append((keys_t[g] * jnp.where(seg_along[0:1] == last, jnp.exp(end - along), 0.0)).astype(BF16))
        throughs.append(jnp.where(last == before, jnp.exp(end), 0.0))

    return lower, right, start_keys, ends, throughs, decays, starts, keys_t16


def solved_with(inverse, once, right):
    result = [dot(i, r) for i, r in zip(inverse, right)]
    twice = [dot(m, m).astype(BF16) for m in once]
    result = [r + dot(m, r) for m, r in zip(once, result)]
    return [(r + dot(m, r)).astype(BF16) for m, r in zip(twice, result)], twice


def scaled_eye(scale):
    row = lax.broadcasted_iota(jnp.int32, (DK, DK), 0)
    col = lax.broadcasted_iota(jnp.int32, (DK, DK), 1)
    return jnp.where(row == col, scale, 0.0)


def query_terms(seg_down, halo, q, weights, decays, starts, keys_t):
    keeps = keep_masks(seg_down)
    queries = [conv_silu(halo(0, g), q(g), weights(0, g), keeps) for g in range(len(keys_t))]
    scores = [dot(query, key_t) for query, key_t in zip(queries, keys_t)]
    norms = [inverse_norms(query, 1) for query in queries]
    queries = [query * norm for query, norm in zip(queries, norms)]
    inside = [(scores[h // 2] * (norms[h // 2] * decays[h])).astype(BF16) for h in range(len(decays))]
    return inside, [queries[h // 2] * starts[h] for h in range(len(decays))]


def groups(heads):
    at = (0, heads // 2 * DK, heads * DK)
    return lambda which, g: slice(at[which] + g * 128, at[which] + g * 128 + 128)


def counts(down_ref, along_ref, block, rows):
    at = pl.multiple_of(block * rows, rows)
    return down_ref[pl.ds(at, rows + 8), :], along_ref[:, pl.ds(at, rows)]


def own_kernel(down_ref, along_ref, own_ref, weight_ref, gates_ref, halo_ref,
               state_ref, map_ref, out_ref, through_ref):
    rows = own_ref.shape[0]
    heads = gates_ref.shape[0] // 2
    columns = groups(heads)
    seg_down, seg_along = counts(down_ref, along_ref, lax.axis_index("ctx") % 2, rows)

    def halo(which, g):
        return halo_ref[:, columns(which, g)]

    def weights(which, g):
        return weight_ref[:, columns(which, g)]

    lower, right, start_keys, ends, throughs, decays, starts, keys_t = block_terms(
        seg_down,
        seg_along,
        halo,
        lambda g: own_ref[:, columns(1, g)],
        lambda g: own_ref[:, columns(2, g)],
        weights,
        gates_ref[0:heads],
        gates_ref[heads:],
    )
    inverse, once = solve_terms(lower)
    inside, start_queries = query_terms(
        seg_down, halo, lambda g: own_ref[:, columns(0, g)], weights, decays, starts, keys_t
    )
    both = [jnp.concatenate([r.astype(BF16), k], axis=1) for r, k in zip(right, start_keys)]
    solved, _ = solved_with(inverse, once, both)
    ended = [dot(e, s) for e, s in zip(ends, solved)]
    result = [dot(i, s) for i, s in zip(inside, solved)]
    for h in range(heads):
        state_ref[h] = ended[h][:, :DV]
        map_ref[h] = (scaled_eye(throughs[h]) - ended[h][:, DV:]).astype(BF16)
        out_ref[:, h * DV : h * DV + DV] = result[h][:, :DV]
        through_ref[:, h * DK : h * DK + DK] = (start_queries[h] - result[h][:, DV:]).astype(BF16)


def peer_halo(own_edge_ref, edge_ref, columns):
    y = lax.axis_index("ctx") % 2
    return lambda which, g: where_y(y, edge_ref[:, columns(which, g)], own_edge_ref[:, columns(which, g)])


def peer_kernel(down_ref, along_ref, pack_ref, own_edge_ref, edge_ref, weight_ref, own_state_ref, own_map_ref,
                state_ref, solved_ref, solver_ref, start_key_ref, ended_ref, passing_ref, decay_ref, start_ref, key_ref,
                pair_state_ref, *pair_map_ref):
    y = lax.axis_index("ctx") % 2
    rows = pack_ref.shape[0] - EDGE
    heads = own_state_ref.shape[0]
    columns = groups(heads)
    key_width = heads // 2 * DK
    gates = [
        sum(pack_ref[rows : rows + heads, (3 * part + i) * rows : (3 * part + i + 1) * rows].astype(F32) for i in range(3))
        for part in range(2)
    ]
    lower, right, start_keys, ends, throughs, decays, starts, keys_t = block_terms(
        *counts(down_ref, along_ref, 1 - y, rows),
        peer_halo(own_edge_ref, edge_ref, columns),
        lambda g: pack_ref[0:rows, g * DK : g * DK + DK],
        lambda g: pack_ref[0:rows, key_width + g * DV : key_width + g * DV + DV],
        lambda which, g: weight_ref[:, columns(which, g)],
        gates[0],
        gates[1],
    )
    entering = [where_y(y, jnp.zeros((DK, DV), F32), own_state_ref[h]) for h in range(heads)]
    right = [r - dot(k, e) for r, k, e in zip(right, start_keys, entering)]
    inverse, once = solve_terms(lower)
    solved, twice = solved_with(inverse, once, right)
    ended = [dot(e, s) for e, s in zip(ends, solved)]
    states = [t * e + s for t, e, s in zip(throughs, entering, ended)]
    moved = [dot(own_map_ref[h], states[h]) for h in range(heads)]
    for h in range(heads):
        pair_state_ref[h] = where_y(y, own_state_ref[h] + moved[h], states[h]).astype(BF16)
        state_ref[h] = states[h].astype(BF16)
    if pair_map_ref:
        solved_keys, _ = solved_with(inverse, once, start_keys)
        for h in range(heads):
            own_map = own_map_ref[h]
            peer_map = scaled_eye(throughs[h]) - dot(ends[h], solved_keys[h])
            pair_map_ref[0][h] = where_y(y, dot(own_map, peer_map), dot(peer_map, own_map)).astype(BF16)
    solver = (inverse, once, twice)
    for h in range(heads):
        solved_ref[h] = solved[h]
        for i in range(3):
            solver_ref[i * heads + h] = solver[i][h]
        start_key_ref[h] = start_keys[h]
        ended_ref[h] = ends[h]
        passing_ref[h : h + 1] = throughs[h]
        decay_ref[h] = decays[h]
        start_ref[h] = starts[h]
    for g in range(heads // 2):
        key_ref[g] = keys_t[g]


def passing_kernel(solver_ref, start_key_ref, ended_ref, passing_ref, weight_hbm, solved_ref, map_ref, weight_ref, sems):
    depth = weight_ref.shape[0]
    copies = Copies(sems)
    part = depth // PARTS
    for i in range(PARTS):
        from_row = pl.multiple_of(lax.axis_index("ctx") % 2 * depth + i * part, part)
        copies.start(weight_hbm.at[pl.ds(from_row, part), :], weight_ref.at[pl.ds(i * part, part), :])
    heads = start_key_ref.shape[0]
    every = range(heads)
    inverse, once, twice = ([solver_ref[i * heads + h] for h in every] for i in range(3))
    solved = [dot(inverse[h], start_key_ref[h]) for h in every]
    solved = [k + dot(m, k) for m, k in zip(once, solved)]
    solved = [(k + dot(m, k)).astype(BF16) for m, k in zip(twice, solved)]
    ended = [dot(ended_ref[h], solved[h]) for h in every]
    for h in every:
        solved_ref[h] = solved[h]
        map_ref[h] = (scaled_eye(passing_ref[h : h + 1]) - ended[h]).astype(BF16)
    copies.wait()


def local_kernel(own_state_ref, own_map_ref, own_out_ref, own_through_ref, state_ref, map_ref, solved_ref, solved_key_ref,
                 decay_ref, start_ref, key_ref, down_ref, along_ref, late_ref, own_edge_ref, edge_ref, conv_ref, gate_ref, gain_ref,
                 out_ref, through_ref, factor_ref):
    y = lax.axis_index("ctx") % 2
    rows = own_out_ref.shape[0]
    heads = own_state_ref.shape[0]
    columns = groups(heads)
    inside, start_queries = query_terms(
        counts(down_ref, along_ref, 1 - y, rows)[0],
        peer_halo(own_edge_ref, edge_ref, columns),
        lambda g: late_ref[:, g * DK : g * DK + DK],
        lambda which, g: conv_ref[:, columns(which, g)],
        [decay_ref[h] for h in range(heads)],
        [start_ref[h] for h in range(heads)],
        [key_ref[g] for g in range(heads // 2)],
    )
    every = range(heads)
    outs = [dot(inside[h], solved_ref[h]) for h in every]
    passed = [dot(inside[h], solved_key_ref[h]) for h in every]
    state_0 = [where_y(y, state_ref[h], own_state_ref[h].astype(BF16)) for h in every]
    own_throughs = [own_through_ref[:, h * DK : h * DK + DK] for h in every]
    extra = [dot(where_y(y, own_throughs[h], start_queries[h].astype(BF16)), state_0[h]) for h in every]
    throughs = [(start_queries[h] - passed[h]).astype(BF16) for h in every]
    moved = [
        dot(where_y(y, own_throughs[h], throughs[h]), where_y(y, map_ref[h], own_map_ref[h])).astype(BF16) for h in every
    ]
    for h in every:
        lanes = slice(h * DV, h * DV + DV)
        out_ref[0:rows, lanes] = own_out_ref[:, lanes] + where_y(y, extra[h], jnp.zeros_like(extra[h]))
        out_ref[rows:, lanes] = outs[h] + where_y(y, jnp.zeros_like(extra[h]), extra[h])
        through_ref[0:rows, lanes] = where_y(y, moved[h], own_throughs[h])
        through_ref[rows:, lanes] = where_y(y, throughs[h], moved[h])
    key_width = heads // 2 * DK
    for h in every:
        lanes = slice(h * DV, h * DV + DV)
        gates = (gate_ref[:, lanes], late_ref[:, key_width + h * DV : key_width + h * DV + DV])
        for b, gate in enumerate(gates):
            gate = gate.astype(F32)
            factor_ref[b * rows : b * rows + rows, lanes] = gain_ref[...] * (gate / (1.0 + jnp.exp(-gate)))


def feature_columns(weight_ref, other_core, other_x):
    head = lax.axis_index("head")
    core, x = head % 2, head // 2
    block = (x + other_x - 2 * x * other_x) * 2 + core + other_core - 2 * core * other_core
    width = weight_ref.shape[1] // lax.axis_size("head")
    return weight_ref[:, pl.ds(pl.multiple_of(block * width, width), width)]


def mix_kernel(out_ref, through_ref, even_ref, odd_ref, factor_ref, weight_ref, mixed_ref, send_ref):
    from_even = lax.axis_index("ctx") // 2 % 2
    heads = even_ref.shape[0]
    rows = out_ref.shape[0] // 2
    every = [slice(h * DV, h * DV + DV) for h in range(heads)]
    moved = [dot(through_ref[:, lanes], where_y(from_even, even_ref[h], odd_ref[h])) for h, lanes in enumerate(every)]
    for lanes, o in zip(every, moved):
        o = out_ref[:, lanes] + o
        scale = lax.rsqrt(jnp.mean(o * o, axis=-1, keepdims=True) + 1e-6)
        mixed_ref[:, lanes] = (o * scale * factor_ref[:, lanes]).astype(BF16)
    send_ref[...] = jnp.dot(mixed_ref[rows:, :], feature_columns(weight_ref, 1, 1), preferred_element_type=F32).astype(BF16)


QUARTERS = ((0, 0), (0, 1), (1, 0))


def project_kernel(mixed_ref, weight_ref, far_ref, send_ref, keep_ref):
    rows = send_ref.shape[1]
    far_ref[...] = jnp.dot(mixed_ref[rows:, :], feature_columns(weight_ref, 0, 1), preferred_element_type=F32).astype(BF16)
    for c, to_ref in ((0, send_ref), (1, keep_ref)):
        for i, (peer, far) in enumerate(QUARTERS):
            weights = feature_columns(weight_ref, 1 - c, far)
            product = jnp.dot(mixed_ref[peer * rows : peer * rows + rows, :], weights, preferred_element_type=F32)
            to_ref[i] = product.astype(BF16)


def core_sum_kernel(keep_ref, got_ref, xy_ref):
    xy_ref[...] = (keep_ref[...].astype(F32) + got_ref[...].astype(F32)).astype(BF16)


def core_sums_kernel(keep_ref, got_ref, mine_ref, x_ref, y_ref):
    for i, ref in enumerate((mine_ref, x_ref, y_ref)):
        ref[...] = (keep_ref[i].astype(F32) + got_ref[i].astype(F32)).astype(ref.dtype)


def last_kernel(mine_ref, x_ref, y_ref, xy_ref, out_ref):
    total = mine_ref[...] + x_ref[...].astype(F32) + (y_ref[...].astype(F32) + xy_ref[...].astype(F32))
    out_ref[...] = total.T.astype(BF16)


def call(kernel, outs, args, name, hbm=(), scratch=(), flops=0, moved=0):
    space = [pl.BlockSpec(memory_space=pltpu.HBM if i in hbm else pltpu.VMEM) for i in range(len(args))]
    args = [pltpu.with_memory_space_constraint(arg, pltpu.HBM) if i in hbm else arg for i, arg in enumerate(args)]
    return pl.pallas_call(
        kernel,
        out_shape=[jax.ShapeDtypeStruct(shape, kind) for shape, kind in outs],
        in_specs=space,
        out_specs=[pl.BlockSpec(memory_space=pltpu.VMEM)] * len(outs),
        scratch_shapes=list(scratch),
        compiler_params=pltpu.CompilerParams(vmem_limit_bytes=VMEM_LIMIT),
        cost_estimate=pl.CostEstimate(flops=flops, bytes_accessed=moved, transcendentals=0),
        name=name,
    )(*args)


def body(
    query_in,
    key_in,
    value_in,
    gate_in,
    conv_query,
    conv_key,
    conv_value,
    decay_in,
    beta_in,
    norm_gain,
    doc_lengths,
    out_weight,
):
    rows = query_in.shape[0]
    ctx_count, head_count = lax.axis_size("ctx"), lax.axis_size("head")
    heads = decay_in.shape[0] // 2
    key_width, value_width = key_in.shape[1] // 2, value_in.shape[1] // 2
    half_width = 2 * key_width + value_width
    width = out_weight.shape[1] // head_count
    longest = ctx_count * rows // 4
    hops = -(-(longest - 1) // (2 * rows))

    swap = [(i, i ^ 1) for i in range(ctx_count)]
    ahead_1 = [(i, (i + 1) % ctx_count) for i in range(ctx_count)]
    even_swap = [(i, i ^ 2) for i in range(ctx_count)]
    odd_swap = [
        (c * head_count + h, (((c + 2) ^ 2) - 2) * head_count + h if 2 <= c < ctx_count - 2 else c * head_count + (h ^ 1))
        for c in range(ctx_count)
        for h in range(head_count)
    ]
    far_ahead = [
        (c * head_count + h, (c + 2) % ctx_count * head_count + h if c % 2 else c * head_count + (h ^ 1))
        for c in range(ctx_count)
        for h in range(head_count)
    ]


    edge, pack, gates = call(
        pack_kernel,
        [((EDGE, half_width), BF16), ((rows + EDGE, key_width + value_width), BF16), ((2 * heads, rows), F32)],
        (query_in, key_in, value_in, decay_in, beta_in),
        "pack",
        hbm=range(5),
        scratch=(pltpu.VMEM((2,) + decay_in.shape, F32), pltpu.SemaphoreType.DMA((7,))),
    )
    own_edge, late, own, weights, own_gate, down, along = call(
        early_kernel,
        [
            ((EDGE, half_width), BF16),
            ((rows, key_width + value_width), BF16),
            ((rows, half_width), BF16),
            ((conv_query.shape[0], half_width), F32),
            ((rows, value_width), BF16),
            ((2 * rows + 8, 128), jnp.int32),
            ((8, 2 * rows), jnp.int32),
        ],
        (query_in, key_in, value_in, gate_in, conv_query, conv_key, conv_value, doc_lengths),
        "early",
        hbm=range(8),
        scratch=(pltpu.SMEM(doc_lengths.shape, jnp.int32), pltpu.SemaphoreType.DMA((13,))),
        flops=10_000_000_000,
        moved=2_000_000,
    )
    got_edge = lax.ppermute(edge, "ctx", ahead_1)
    got_pack = lax.ppermute(pack, "ctx", swap)
    got_far_edge = lax.ppermute(own_edge, ("ctx", "head"), far_ahead)

    square = (heads, DK, DV)
    own_state, own_map, own_out, own_through = call(
        own_kernel,
        [(square, F32), (square, BF16), ((rows, value_width), F32), ((rows, value_width), BF16)],
        (down, along, own, weights, gates, got_edge),
        "own_terms",
        flops=1_000_000,
        moved=4_000_000,
    )
    late, own_map = lax.optimization_barrier((late, own_map))
    got_late = lax.ppermute(late, "ctx", swap)
    peer = call(
        peer_kernel,
        [
            (square, BF16),
            ((heads, rows, DV), BF16),
            ((3 * heads, rows, rows), BF16),
            ((heads, rows, DK), BF16),
            ((heads, DK, rows), BF16),
            ((heads, rows), F32),
            ((heads, rows, rows), F32),
            ((heads, rows, DK), F32),
            ((heads // 2, DK, rows), BF16),
            (square, BF16),
        ]
        + ([(square, BF16)] if hops > 1 else []),
        (down, along, got_pack, own_edge, got_far_edge, weights, own_state, own_map),
        "peer_terms",
        flops=2_000_000_000,
        moved=4_000_000,
    )
    end = peer[9]
    def from_earlier(value):
        return lax.ppermute(value, "ctx", even_swap), lax.ppermute(value, ("ctx", "head"), odd_swap)

    entering = from_earlier(end)
    for _ in range(hops - 1):
        earlier = jnp.where(lax.axis_index("ctx") // 2 % 2 == 1, *entering)
        moved = jnp.einsum("hij,hjk->hik", peer[10], earlier, preferred_element_type=F32)
        moved = jnp.where(lax.axis_index("ctx") < 2, 0.0, moved)
        entering = from_earlier((end.astype(F32) + moved).astype(BF16))
    state, solved, solver, start_key, ended, passing, decay, start, key = peer[:9]
    solved_key, map_, weight = call(
        passing_kernel,
        [(square, BF16), (square, BF16), ((value_width, out_weight.shape[1]), BF16)],
        (solver, start_key, ended, passing, out_weight),
        "passing",
        hbm=(4,),
        scratch=(pltpu.SemaphoreType.DMA((PARTS,)),),
        flops=1_000_000_000,
        moved=4_000_000,
    )
    out, through, factor = call(
        local_kernel,
        [((2 * rows, value_width), F32), ((2 * rows, value_width), BF16), ((2 * rows, value_width), F32)],
        (own_state, own_map, own_out, own_through, state, map_, solved, solved_key, decay, start, key, down, along, got_late,
         own_edge, got_far_edge, weights, own_gate, norm_gain.reshape(1, DV)),
        "local_outputs",
        flops=1_000_000_000,
        moved=4_000_000,
    )
    cores = [(i, i ^ 1) for i in range(head_count)]
    mixed, send_far = call(
        mix_kernel,
        [((2 * rows, value_width), BF16), ((rows, width), BF16)],
        (out, through, *entering, factor, weight),
        "mix",
    )
    got_far = lax.ppermute(send_far, "head", cores)
    keep_far, send, keep = call(
        project_kernel,
        [((rows, width), BF16), ((3, rows, width), BF16), ((3, rows, width), BF16)],
        (mixed, weight),
        "project",
        flops=2_000_000_000,
        moved=4_000_000,
    )
    send, got_far = lax.optimization_barrier((send, got_far))
    got = lax.ppermute(send, "head", cores)
    (to_xy,) = call(core_sum_kernel, [((rows, width), BF16)], (keep_far, got_far), "core_sum_xy")
    mine, to_x, to_y = call(
        core_sums_kernel,
        [((rows, width), F32), ((rows, width), BF16), ((rows, width), BF16)],
        (keep, got),
        "core_sums",
    )
    both = [
        (c * head_count + h, (c ^ 1) * head_count + (h ^ 2)) for c in range(ctx_count) for h in range(head_count)
    ]
    got_xy = lax.ppermute(to_xy, ("ctx", "head"), both)
    got_x = lax.ppermute(to_x, "head", [(i, i ^ 2) for i in range(head_count)])
    got_y = lax.ppermute(to_y, "ctx", swap)
    (projected,) = call(
        last_kernel, [((width, rows), BF16)], (mine, got_x, got_y, got_xy), "last_sum"
    )
    return projected


def solution(mesh):
    return jax.shard_map(
        body,
        mesh=mesh,
        in_specs=(
            P("ctx", "head"),
            P("ctx", "head"),
            P("ctx", "head"),
            P("ctx", "head"),
            P(None, "head"),
            P(None, "head"),
            P(None, "head"),
            P("head", "ctx"),
            P("head", "ctx"),
            P(),
            P(),
            P("head", None),
        ),
        out_specs=P("head", "ctx"),
        check_vma=False,
    )
```

```python
import jax
import jax.numpy as jnp
from jax import lax
from jax.experimental import pallas as pl
from jax.experimental.pallas import tpu as pltpu
from jax.sharding import PartitionSpec as P

DK = 128
DV = 128
EDGE = 16
PARTS = 8
F32 = jnp.float32
BF16 = jnp.bfloat16
VMEM_LIMIT = 48 * 1024 * 1024


def dot(a, b):
    return jnp.dot(a.astype(BF16), b.astype(BF16), preferred_element_type=F32)


def dot_nt(a, b):
    dims = (((1,), (1,)), ((), ()))
    return lax.dot_general(a.astype(BF16), b.astype(BF16), dims, preferred_element_type=F32)


def exact_dot(a, b):
    return jnp.dot(a, b, precision=lax.Precision.HIGHEST, preferred_element_type=F32)


def where_y(flag, a, b):
    return jnp.where(flag == 1, a, b)


def document_counts(doc_ref, base, rows, lanes):
    down = lax.broadcasted_iota(jnp.int32, (rows + 8, lanes), 0) + (base - 8)
    along = lax.broadcasted_iota(jnp.int32, (8, rows), 1) + base
    docs = doc_ref.shape[0]

    def one(d, carried):
        start, count_down, count_along = carried
        count_down = count_down + (down >= start).astype(jnp.int32)
        count_along = count_along + (along >= start).astype(jnp.int32)
        return start + doc_ref[d], count_down, count_along

    state = (jnp.int32(0), jnp.zeros_like(down), jnp.zeros_like(along))
    if docs <= 16:
        for d in range(docs):
            state = one(d, state)
    else:
        state = lax.fori_loop(0, docs, one, state)
    return state[1], state[2]


def three_terms(value):
    high = value.astype(BF16)
    rest = value - high.astype(F32)
    middle = rest.astype(BF16)
    low = (rest - middle.astype(F32)).astype(BF16)
    return high, middle, low


class Copies:
    def __init__(self, sems):
        self.sems, self.started = sems, []

    def start(self, source, target):
        self.started.append(pltpu.make_async_copy(source, target, self.sems.at[len(self.started)]))
        self.started[-1].start()

    def wait(self, first=0, last=None):
        for one in self.started[first:last]:
            one.wait()


def half_columns(ref, which):
    width = ref.shape[1] // 2
    return pl.ds(pl.multiple_of(which * width, width), width)


def pack_kernel(q_ref, k_ref, v_ref, decay_ref, beta_ref, edge_ref, pack_ref, gates_ref, raw_gates, sems):
    other = 1 - lax.axis_index("ctx") % 2
    rows = q_ref.shape[0]
    heads = decay_ref.shape[0] // 2
    copies = Copies(sems)
    copies.start(decay_ref, raw_gates.at[0])
    copies.start(beta_ref, raw_gates.at[1])
    at = 0
    for ref in (q_ref, k_ref, v_ref):
        width = ref.shape[1] // 2
        copies.start(ref.at[pl.ds(rows - EDGE, EDGE), half_columns(ref, other)], edge_ref.at[:, pl.ds(at, width)])
        at += width
    at = 0
    for ref in (k_ref, v_ref):
        width = ref.shape[1] // 2
        copies.start(ref.at[:, half_columns(ref, other)], pack_ref.at[pl.ds(0, rows), pl.ds(at, width)])
        at += width
    pack_ref[rows : rows + EDGE, :] = jnp.zeros((EDGE, pack_ref.shape[1]), BF16)
    copies.wait(0, 2)
    decay = raw_gates[0]
    log_gamma = -(jnp.maximum(decay, 0.0) + jnp.log1p(jnp.exp(-jnp.abs(decay))))
    upper = lax.broadcasted_iota(jnp.int32, (rows, rows), 0) <= lax.broadcasted_iota(jnp.int32, (rows, rows), 1)
    sums = exact_dot(log_gamma, upper.astype(F32))
    beta = 1.0 / (1.0 + jnp.exp(-raw_gates[1]))
    at = 0
    for i, value in enumerate((sums, beta)):
        gates_ref[i * heads : i * heads + heads] = where_y(other, value[:heads], value[heads:])
        for term in three_terms(where_y(other, value[heads:], value[:heads])):
            pack_ref[rows : rows + heads, at : at + rows] = term
            at += rows
    copies.wait(2)


def early_kernel(q_ref, k_ref, v_ref, g_ref, cq_ref, ck_ref, cv_ref, doc_hbm,
                 own_edge_ref, late_ref, own_ref, weight_ref, own_gate_ref, down_ref, along_ref, doc_ref, sems):
    ctx = lax.axis_index("ctx")
    y = ctx % 2
    rows = q_ref.shape[0]
    copies = Copies(sems)
    copies.start(doc_hbm, doc_ref)
    at = 0
    for ref, weights in ((q_ref, cq_ref), (k_ref, ck_ref), (v_ref, cv_ref)):
        width = ref.shape[1] // 2
        here = pl.ds(at, width)
        copies.start(ref.at[pl.ds(rows - EDGE, EDGE), half_columns(ref, y)], own_edge_ref.at[:, here])
        copies.start(ref.at[:, half_columns(ref, y)], own_ref.at[:, here])
        copies.start(weights.at[:, half_columns(ref, y)], weight_ref.at[:, here])
        at += width
    key_width = q_ref.shape[1] // 2
    copies.start(q_ref.at[:, half_columns(q_ref, 1 - y)], late_ref.at[:, pl.ds(0, key_width)])
    copies.start(g_ref.at[:, half_columns(g_ref, 1 - y)], late_ref.at[:, pl.ds(key_width, g_ref.shape[1] // 2)])
    copies.start(g_ref.at[:, half_columns(g_ref, y)], own_gate_ref)
    copies.wait(0, 1)
    down_ref[...], along_ref[...] = document_counts(doc_ref, (ctx - y) * rows, 2 * rows, 128)
    copies.wait(1)


def conv_silu(halo, current, weight, keeps):
    rows = current.shape[0]
    padded = jnp.concatenate([halo.astype(F32)[EDGE - 8 :], current.astype(F32)], axis=0)
    margin = weight.shape[0] - 1
    summed = weight[margin : margin + 1] * padded[8:]
    for lag in range(1, margin + 1):
        summed = summed + weight[margin - lag : margin - lag + 1] * padded[8 - lag : 8 - lag + rows] * keeps[lag]
    return summed / (1.0 + jnp.exp(-summed))


def inverse_norms(vectors, axis):
    return lax.rsqrt(jnp.sum(vectors * vectors, axis=axis, keepdims=True) + 1e-6)


def odd_blocks(value, reach):
    return jnp.concatenate([value[at : at + reach] for at in range(reach, value.shape[0], 2 * reach)], axis=0)


def at_odd_blocks(value, reach):
    parts = []
    for at in range(0, value.shape[0], reach):
        parts += [jnp.zeros((reach, value.shape[1]), value.dtype), value[at : at + reach]]
    return jnp.concatenate(parts, axis=0)


def keep_masks(seg_down):
    seg = seg_down[8:]
    return [None] + [(seg_down[8 - lag : 8 - lag + seg.shape[0]] == seg).astype(F32) for lag in (1, 2, 3)]


def solve_terms(lower):
    rows = lower[0].shape[0]
    small, large = rows // 8, rows // 4
    row = lax.broadcasted_iota(jnp.int32, (rows, rows), 0)
    col = lax.broadcasted_iota(jnp.int32, (rows, rows), 1)
    power = [jnp.where(row // small == col // small, -x, 0.0) for x in lower]
    eye = (row == col).astype(F32)
    inverse = [eye + x for x in power]
    power = [x.astype(BF16) for x in power]
    power = [dot(x, x).astype(BF16) for x in power]
    reach = 4
    while reach < small:
        following = [dot(x, x).astype(BF16) for x in power]
        inverse = [x + dot(x, p) for x, p in zip(inverse, power)]
        power = following
        reach *= 2
    inverse = [x + dot(x, p) for x, p in zip(inverse, power)]
    here = (row // large == col // large) & (row // small != col // small)
    moved = [dot(odd_blocks(jnp.where(here, x, 0.0), small), i) for x, i in zip(lower, inverse)]
    moved = [dot(odd_blocks(i, small), at_odd_blocks(m, small)) for i, m in zip(inverse, moved)]
    inverse = [(i - at_odd_blocks(m, small)).astype(BF16) for i, m in zip(inverse, moved)]
    rest = [jnp.where(row // large == col // large, 0.0, -x) for x in lower]
    once = [dot(i, r).astype(BF16) for i, r in zip(inverse, rest)]
    return inverse, once


def block_terms(seg_down, seg_along, halo, k, v, weights, sums, beta):
    heads, rows = sums.shape
    key_heads = heads // 2
    seg = seg_down[8:]
    keeps = keep_masks(seg_down)
    before = seg_down[7:8]
    last = seg_down[rows + 7 : rows + 8]
    row = lax.broadcasted_iota(jnp.int32, (rows, rows), 0)
    col = lax.broadcasted_iota(jnp.int32, (rows, rows), 1)
    same = (seg == seg_along[0:1]) & (row >= col)
    stacked = jnp.concatenate([sums, beta, jnp.zeros((rows - 2 * heads, rows), F32)], axis=0)
    columns = stacked.T

    raw = [conv_silu(halo(1, g), k(g), weights(1, g), keeps) for g in range(key_heads)]
    grams = [dot_nt(key, key) for key in raw]
    raw_t = [key.T for key in raw]
    norms = [inverse_norms(key, 1) for key in raw]
    norms_t = [inverse_norms(key, 0) for key in raw_t]
    keys = [key * norm for key, norm in zip(raw, norms)]
    keys_t = [key * norm for key, norm in zip(raw_t, norms_t)]
    values = [conv_silu(halo(2, g), v(g), weights(2, g), keeps) for g in range(heads)]
    keys_t16 = [key.astype(BF16) for key in keys_t]

    lower, decays, right, start_keys, starts, ends, throughs = [], [], [], [], [], [], []
    for h in range(heads):
        g = h // 2
        down = jnp.broadcast_to(columns[:, h : h + 1], (rows, rows))
        beta_down = jnp.broadcast_to(columns[:, heads + h : heads + h + 1], (rows, rows))
        along = sums[h : h + 1]
        end = jnp.broadcast_to(columns[rows - 1 : rows, h : h + 1], (1, rows))
        decay = jnp.exp(jnp.where(same, down - along, -1e30))
        decays.append(decay)
        factor = jnp.where(row > col, beta_down * norms[g] * decay * norms_t[g], 0.0)
        lower.append(factor * grams[g])
        start = jnp.where(seg == before, jnp.exp(down), 0.0)
        starts.append(start)
        right.append(beta_down * values[h])
        start_keys.append((beta_down * start * keys[g]).astype(BF16))
        ends.append((keys_t[g] * jnp.where(seg_along[0:1] == last, jnp.exp(end - along), 0.0)).astype(BF16))
        throughs.append(jnp.where(last == before, jnp.exp(end), 0.0))

    return lower, right, start_keys, ends, throughs, decays, starts, keys_t16


def solved_with(inverse, once, right):
    result = [dot(i, r) for i, r in zip(inverse, right)]
    twice = [dot(m, m).astype(BF16) for m in once]
    result = [r + dot(m, r) for m, r in zip(once, result)]
    return [(r + dot(m, r)).astype(BF16) for m, r in zip(twice, result)], twice


def scaled_eye(scale):
    row = lax.broadcasted_iota(jnp.int32, (DK, DK), 0)
    col = lax.broadcasted_iota(jnp.int32, (DK, DK), 1)
    return jnp.where(row == col, scale, 0.0)


def query_terms(seg_down, halo, q, weights, decays, starts, keys_t):
    keeps = keep_masks(seg_down)
    queries = [conv_silu(halo(0, g), q(g), weights(0, g), keeps) for g in range(len(keys_t))]
    scores = [dot(query, key_t) for query, key_t in zip(queries, keys_t)]
    norms = [inverse_norms(query, 1) for query in queries]
    queries = [query * norm for query, norm in zip(queries, norms)]
    inside = [(scores[h // 2] * (norms[h // 2] * decays[h])).astype(BF16) for h in range(len(decays))]
    return inside, [queries[h // 2] * starts[h] for h in range(len(decays))]


def groups(heads):
    at = (0, heads // 2 * DK, heads * DK)
    return lambda which, g: slice(at[which] + g * 128, at[which] + g * 128 + 128)


def counts(down_ref, along_ref, block, rows):
    at = pl.multiple_of(block * rows, rows)
    return down_ref[pl.ds(at, rows + 8), :], along_ref[:, pl.ds(at, rows)]


def own_kernel(down_ref, along_ref, own_ref, weight_ref, gates_ref, halo_ref,
               state_ref, map_ref, solved_ref, decay_ref, start_ref, key_ref):
    rows = own_ref.shape[0]
    heads = gates_ref.shape[0] // 2
    columns = groups(heads)
    seg_down, seg_along = counts(down_ref, along_ref, lax.axis_index("ctx") % 2, rows)

    def halo(which, g):
        return halo_ref[:, columns(which, g)]

    def weights(which, g):
        return weight_ref[:, columns(which, g)]

    lower, right, start_keys, ends, throughs, decays, starts, keys_t = block_terms(
        seg_down,
        seg_along,
        halo,
        lambda g: own_ref[:, columns(1, g)],
        lambda g: own_ref[:, columns(2, g)],
        weights,
        gates_ref[0:heads],
        gates_ref[heads:],
    )
    inverse, once = solve_terms(lower)
    both = [jnp.concatenate([r.astype(BF16), k], axis=1) for r, k in zip(right, start_keys)]
    solved, _ = solved_with(inverse, once, both)
    ended = [dot(e, s) for e, s in zip(ends, solved)]
    for h in range(heads):
        state_ref[h] = ended[h][:, :DV]
        map_ref[h] = (scaled_eye(throughs[h]) - ended[h][:, DV:]).astype(BF16)
        solved_ref[h], decay_ref[h], start_ref[h] = solved[h], decays[h], starts[h]
    for g in range(heads // 2):
        key_ref[g] = keys_t[g]


def peer_halo(own_edge_ref, edge_ref, columns):
    y = lax.axis_index("ctx") % 2
    return lambda which, g: where_y(y, edge_ref[:, columns(which, g)], own_edge_ref[:, columns(which, g)])


def peer_kernel(down_ref, along_ref, pack_ref, own_edge_ref, edge_ref, weight_ref, own_state_ref, own_map_ref,
                state_ref, solved_ref, solver_ref, start_key_ref, ended_ref, passing_ref, decay_ref, start_ref, key_ref,
                pair_state_ref, *pair_map_ref):
    y = lax.axis_index("ctx") % 2
    rows = pack_ref.shape[0] - EDGE
    heads = own_state_ref.shape[0]
    columns = groups(heads)
    key_width = heads // 2 * DK
    gates = [
        sum(pack_ref[rows : rows + heads, (3 * part + i) * rows : (3 * part + i + 1) * rows].astype(F32) for i in range(3))
        for part in range(2)
    ]
    lower, right, start_keys, ends, throughs, decays, starts, keys_t = block_terms(
        *counts(down_ref, along_ref, 1 - y, rows),
        peer_halo(own_edge_ref, edge_ref, columns),
        lambda g: pack_ref[0:rows, g * DK : g * DK + DK],
        lambda g: pack_ref[0:rows, key_width + g * DV : key_width + g * DV + DV],
        lambda which, g: weight_ref[:, columns(which, g)],
        gates[0],
        gates[1],
    )
    entering = [where_y(y, jnp.zeros((DK, DV), F32), own_state_ref[h]) for h in range(heads)]
    right = [r - dot(k, e) for r, k, e in zip(right, start_keys, entering)]
    inverse, once = solve_terms(lower)
    solved, twice = solved_with(inverse, once, right)
    ended = [dot(e, s) for e, s in zip(ends, solved)]
    states = [t * e + s for t, e, s in zip(throughs, entering, ended)]
    moved = [dot(own_map_ref[h], states[h]) for h in range(heads)]
    for h in range(heads):
        pair_state_ref[h] = where_y(y, own_state_ref[h] + moved[h], states[h]).astype(BF16)
        state_ref[h] = states[h].astype(BF16)
    if pair_map_ref:
        solved_keys, _ = solved_with(inverse, once, start_keys)
        for h in range(heads):
            own_map = own_map_ref[h]
            peer_map = scaled_eye(throughs[h]) - dot(ends[h], solved_keys[h])
            pair_map_ref[0][h] = where_y(y, dot(own_map, peer_map), dot(peer_map, own_map)).astype(BF16)
    solver = (inverse, once, twice)
    for h in range(heads):
        solved_ref[h] = solved[h]
        for i in range(3):
            solver_ref[i * heads + h] = solver[i][h]
        start_key_ref[h] = start_keys[h]
        ended_ref[h] = ends[h]
        passing_ref[h : h + 1] = throughs[h]
        decay_ref[h] = decays[h]
        start_ref[h] = starts[h]
    for g in range(heads // 2):
        key_ref[g] = keys_t[g]


def passing_kernel(solver_ref, start_key_ref, ended_ref, passing_ref, own_solved_ref, decay_ref, start_ref, key_ref,
                   down_ref, along_ref, own_ref, halo_ref, conv_ref, weight_hbm,
                   solved_ref, map_ref, own_out_ref, own_through_ref, weight_ref, sems):
    depth = weight_ref.shape[0]
    copies = Copies(sems)
    part = depth // PARTS
    for i in range(PARTS):
        from_row = pl.multiple_of(lax.axis_index("ctx") % 2 * depth + i * part, part)
        copies.start(weight_hbm.at[pl.ds(from_row, part), :], weight_ref.at[pl.ds(i * part, part), :])
    heads = start_key_ref.shape[0]
    every = range(heads)
    inverse, once, twice = ([solver_ref[i * heads + h] for h in every] for i in range(3))
    solved = [dot(inverse[h], start_key_ref[h]) for h in every]
    solved = [k + dot(m, k) for m, k in zip(once, solved)]
    solved = [(k + dot(m, k)).astype(BF16) for m, k in zip(twice, solved)]
    ended = [dot(ended_ref[h], solved[h]) for h in every]
    columns = groups(heads)
    inside, start_queries = query_terms(
        counts(down_ref, along_ref, lax.axis_index("ctx") % 2, own_ref.shape[0])[0],
        lambda which, g: halo_ref[:, columns(which, g)],
        lambda g: own_ref[:, columns(0, g)],
        lambda which, g: conv_ref[:, columns(which, g)],
        [decay_ref[h] for h in every],
        [start_ref[h] for h in every],
        [key_ref[g] for g in range(heads // 2)],
    )
    result = [dot(inside[h], own_solved_ref[h]) for h in every]
    for h in every:
        own_out_ref[:, h * DV : h * DV + DV] = result[h][:, :DV]
        own_through_ref[:, h * DK : h * DK + DK] = (start_queries[h] - result[h][:, DV:]).astype(BF16)
        solved_ref[h] = solved[h]
        map_ref[h] = (scaled_eye(passing_ref[h : h + 1]) - ended[h]).astype(BF16)
    copies.wait()


def local_kernel(own_state_ref, own_map_ref, own_out_ref, own_through_ref, state_ref, map_ref, solved_ref, solved_key_ref,
                 decay_ref, start_ref, key_ref, down_ref, along_ref, late_ref, own_edge_ref, edge_ref, conv_ref, gate_ref, gain_ref,
                 out_ref, through_ref, factor_ref):
    y = lax.axis_index("ctx") % 2
    rows = own_out_ref.shape[0]
    heads = own_state_ref.shape[0]
    columns = groups(heads)
    inside, start_queries = query_terms(
        counts(down_ref, along_ref, 1 - y, rows)[0],
        peer_halo(own_edge_ref, edge_ref, columns),
        lambda g: late_ref[:, g * DK : g * DK + DK],
        lambda which, g: conv_ref[:, columns(which, g)],
        [decay_ref[h] for h in range(heads)],
        [start_ref[h] for h in range(heads)],
        [key_ref[g] for g in range(heads // 2)],
    )
    every = range(heads)
    outs = [dot(inside[h], solved_ref[h]) for h in every]
    passed = [dot(inside[h], solved_key_ref[h]) for h in every]
    state_0 = [where_y(y, state_ref[h], own_state_ref[h].astype(BF16)) for h in every]
    own_throughs = [own_through_ref[:, h * DK : h * DK + DK] for h in every]
    extra = [dot(where_y(y, own_throughs[h], start_queries[h].astype(BF16)), state_0[h]) for h in every]
    throughs = [(start_queries[h] - passed[h]).astype(BF16) for h in every]
    moved = [
        dot(where_y(y, own_throughs[h], throughs[h]), where_y(y, map_ref[h], own_map_ref[h])).astype(BF16) for h in every
    ]
    for h in every:
        lanes = slice(h * DV, h * DV + DV)
        out_ref[0:rows, lanes] = own_out_ref[:, lanes] + where_y(y, extra[h], jnp.zeros_like(extra[h]))
        out_ref[rows:, lanes] = outs[h] + where_y(y, jnp.zeros_like(extra[h]), extra[h])
        through_ref[0:rows, lanes] = where_y(y, moved[h], own_throughs[h])
        through_ref[rows:, lanes] = where_y(y, throughs[h], moved[h])
    key_width = heads // 2 * DK
    for h in every:
        lanes = slice(h * DV, h * DV + DV)
        gates = (gate_ref[:, lanes], late_ref[:, key_width + h * DV : key_width + h * DV + DV])
        for b, gate in enumerate(gates):
            gate = gate.astype(F32)
            factor_ref[b * rows : b * rows + rows, lanes] = gain_ref[...] * (gate / (1.0 + jnp.exp(-gate)))


def feature_columns(weight_ref, other_core, other_x):
    head = lax.axis_index("head")
    core, x = head % 2, head // 2
    block = (x + other_x - 2 * x * other_x) * 2 + core + other_core - 2 * core * other_core
    width = weight_ref.shape[1] // lax.axis_size("head")
    return weight_ref[:, pl.ds(pl.multiple_of(block * width, width), width)]


def mix_kernel(out_ref, through_ref, even_ref, odd_ref, factor_ref, weight_ref, mixed_ref, send_ref):
    from_even = lax.axis_index("ctx") // 2 % 2
    heads = even_ref.shape[0]
    rows = out_ref.shape[0] // 2
    every = [slice(h * DV, h * DV + DV) for h in range(heads)]
    moved = [dot(through_ref[:, lanes], where_y(from_even, even_ref[h], odd_ref[h])) for h, lanes in enumerate(every)]
    for lanes, o in zip(every, moved):
        o = out_ref[:, lanes] + o
        scale = lax.rsqrt(jnp.mean(o * o, axis=-1, keepdims=True) + 1e-6)
        mixed_ref[:, lanes] = (o * scale * factor_ref[:, lanes]).astype(BF16)
    send_ref[...] = jnp.dot(mixed_ref[rows:, :], feature_columns(weight_ref, 1, 1), preferred_element_type=F32).astype(BF16)


QUARTERS = ((0, 0), (0, 1), (1, 0))


def project_kernel(mixed_ref, weight_ref, far_ref, send_ref, keep_ref):
    rows = send_ref.shape[1]
    far_ref[...] = jnp.dot(mixed_ref[rows:, :], feature_columns(weight_ref, 0, 1), preferred_element_type=F32).astype(BF16)
    for c, to_ref in ((0, send_ref), (1, keep_ref)):
        for i, (peer, far) in enumerate(QUARTERS):
            weights = feature_columns(weight_ref, 1 - c, far)
            product = jnp.dot(mixed_ref[peer * rows : peer * rows + rows, :], weights, preferred_element_type=F32)
            to_ref[i] = product.astype(BF16)


def core_sum_kernel(keep_ref, got_ref, xy_ref):
    xy_ref[...] = (keep_ref[...].astype(F32) + got_ref[...].astype(F32)).astype(BF16)


def core_sums_kernel(keep_ref, got_ref, mine_ref, x_ref, y_ref):
    for i, ref in enumerate((mine_ref, x_ref, y_ref)):
        ref[...] = (keep_ref[i].astype(F32) + got_ref[i].astype(F32)).astype(ref.dtype)


def last_kernel(mine_ref, x_ref, y_ref, xy_ref, out_ref):
    total = mine_ref[...] + x_ref[...].astype(F32) + (y_ref[...].astype(F32) + xy_ref[...].astype(F32))
    out_ref[...] = total.T.astype(BF16)


def call(kernel, outs, args, name, hbm=(), scratch=(), flops=0, moved=0):
    space = [pl.BlockSpec(memory_space=pltpu.HBM if i in hbm else pltpu.VMEM) for i in range(len(args))]
    args = [pltpu.with_memory_space_constraint(arg, pltpu.HBM) if i in hbm else arg for i, arg in enumerate(args)]
    return pl.pallas_call(
        kernel,
        out_shape=[jax.ShapeDtypeStruct(shape, kind) for shape, kind in outs],
        in_specs=space,
        out_specs=[pl.BlockSpec(memory_space=pltpu.VMEM)] * len(outs),
        scratch_shapes=list(scratch),
        compiler_params=pltpu.CompilerParams(vmem_limit_bytes=VMEM_LIMIT),
        cost_estimate=pl.CostEstimate(flops=flops, bytes_accessed=moved, transcendentals=0),
        name=name,
    )(*args)


def body(
    query_in,
    key_in,
    value_in,
    gate_in,
    conv_query,
    conv_key,
    conv_value,
    decay_in,
    beta_in,
    norm_gain,
    doc_lengths,
    out_weight,
):
    rows = query_in.shape[0]
    ctx_count, head_count = lax.axis_size("ctx"), lax.axis_size("head")
    heads = decay_in.shape[0] // 2
    key_width, value_width = key_in.shape[1] // 2, value_in.shape[1] // 2
    half_width = 2 * key_width + value_width
    width = out_weight.shape[1] // head_count
    longest = ctx_count * rows // 4
    hops = -(-(longest - 1) // (2 * rows))

    swap = [(i, i ^ 1) for i in range(ctx_count)]
    ahead_1 = [(i, (i + 1) % ctx_count) for i in range(ctx_count)]
    even_swap = [(i, i ^ 2) for i in range(ctx_count)]
    odd_swap = [
        (c * head_count + h, (((c + 2) ^ 2) - 2) * head_count + h if 2 <= c < ctx_count - 2 else c * head_count + (h ^ 1))
        for c in range(ctx_count)
        for h in range(head_count)
    ]
    far_ahead = [
        (c * head_count + h, (c + 2) % ctx_count * head_count + h if c % 2 else c * head_count + (h ^ 1))
        for c in range(ctx_count)
        for h in range(head_count)
    ]


    edge, pack, gates = call(
        pack_kernel,
        [((EDGE, half_width), BF16), ((rows + EDGE, key_width + value_width), BF16), ((2 * heads, rows), F32)],
        (query_in, key_in, value_in, decay_in, beta_in),
        "pack",
        hbm=range(5),
        scratch=(pltpu.VMEM((2,) + decay_in.shape, F32), pltpu.SemaphoreType.DMA((7,))),
    )
    own_edge, late, own, weights, own_gate, down, along = call(
        early_kernel,
        [
            ((EDGE, half_width), BF16),
            ((rows, key_width + value_width), BF16),
            ((rows, half_width), BF16),
            ((conv_query.shape[0], half_width), F32),
            ((rows, value_width), BF16),
            ((2 * rows + 8, 128), jnp.int32),
            ((8, 2 * rows), jnp.int32),
        ],
        (query_in, key_in, value_in, gate_in, conv_query, conv_key, conv_value, doc_lengths),
        "early",
        hbm=range(8),
        scratch=(pltpu.SMEM(doc_lengths.shape, jnp.int32), pltpu.SemaphoreType.DMA((13,))),
        flops=10_000_000_000,
        moved=2_000_000,
    )
    got_edge = lax.ppermute(edge, "ctx", ahead_1)
    got_pack = lax.ppermute(pack, "ctx", swap)
    got_far_edge = lax.ppermute(own_edge, ("ctx", "head"), far_ahead)

    square = (heads, DK, DV)
    own_state, own_map, own_solved, own_decay, own_start, own_key = call(
        own_kernel,
        [
            (square, F32),
            (square, BF16),
            ((heads, rows, DK + DV), BF16),
            ((heads, rows, rows), F32),
            ((heads, rows, DK), F32),
            ((heads // 2, DK, rows), BF16),
        ],
        (down, along, own, weights, gates, got_edge),
        "own_terms",
        flops=1_000_000,
        moved=4_000_000,
    )
    late, own_map = lax.optimization_barrier((late, own_map))
    got_late = lax.ppermute(late, "ctx", swap)
    peer = call(
        peer_kernel,
        [
            (square, BF16),
            ((heads, rows, DV), BF16),
            ((3 * heads, rows, rows), BF16),
            ((heads, rows, DK), BF16),
            ((heads, DK, rows), BF16),
            ((heads, rows), F32),
            ((heads, rows, rows), F32),
            ((heads, rows, DK), F32),
            ((heads // 2, DK, rows), BF16),
            (square, BF16),
        ]
        + ([(square, BF16)] if hops > 1 else []),
        (down, along, got_pack, own_edge, got_far_edge, weights, own_state, own_map),
        "peer_terms",
        flops=2_000_000_000,
        moved=4_000_000,
    )
    end = peer[9]
    def from_earlier(value):
        return lax.ppermute(value, "ctx", even_swap), lax.ppermute(value, ("ctx", "head"), odd_swap)

    entering = from_earlier(end)
    for _ in range(hops - 1):
        earlier = jnp.where(lax.axis_index("ctx") // 2 % 2 == 1, *entering)
        moved = jnp.einsum("hij,hjk->hik", peer[10], earlier, preferred_element_type=F32)
        moved = jnp.where(lax.axis_index("ctx") < 2, 0.0, moved)
        entering = from_earlier((end.astype(F32) + moved).astype(BF16))
    state, solved, solver, start_key, ended, passing, decay, start, key = peer[:9]
    solved_key, map_, own_out, own_through, weight = call(
        passing_kernel,
        [
            (square, BF16),
            (square, BF16),
            ((rows, value_width), F32),
            ((rows, value_width), BF16),
            ((value_width, out_weight.shape[1]), BF16),
        ],
        (solver, start_key, ended, passing, own_solved, own_decay, own_start, own_key, down, along, own, got_edge, weights,
         out_weight),
        "passing",
        hbm=(13,),
        scratch=(pltpu.SemaphoreType.DMA((PARTS,)),),
        flops=1_000_000_000,
        moved=4_000_000,
    )
    out, through, factor = call(
        local_kernel,
        [((2 * rows, value_width), F32), ((2 * rows, value_width), BF16), ((2 * rows, value_width), F32)],
        (own_state, own_map, own_out, own_through, state, map_, solved, solved_key, decay, start, key, down, along, got_late,
         own_edge, got_far_edge, weights, own_gate, norm_gain.reshape(1, DV)),
        "local_outputs",
        flops=1_000_000_000,
        moved=4_000_000,
    )
    cores = [(i, i ^ 1) for i in range(head_count)]
    mixed, send_far = call(
        mix_kernel,
        [((2 * rows, value_width), BF16), ((rows, width), BF16)],
        (out, through, *entering, factor, weight),
        "mix",
    )
    got_far = lax.ppermute(send_far, "head", cores)
    keep_far, send, keep = call(
        project_kernel,
        [((rows, width), BF16), ((3, rows, width), BF16), ((3, rows, width), BF16)],
        (mixed, weight),
        "project",
        flops=2_000_000_000,
        moved=4_000_000,
    )
    send, got_far = lax.optimization_barrier((send, got_far))
    got = lax.ppermute(send, "head", cores)
    (to_xy,) = call(core_sum_kernel, [((rows, width), BF16)], (keep_far, got_far), "core_sum_xy")
    mine, to_x, to_y = call(
        core_sums_kernel,
        [((rows, width), F32), ((rows, width), BF16), ((rows, width), BF16)],
        (keep, got),
        "core_sums",
    )
    both = [
        (c * head_count + h, (c ^ 1) * head_count + (h ^ 2)) for c in range(ctx_count) for h in range(head_count)
    ]
    got_xy = lax.ppermute(to_xy, ("ctx", "head"), both)
    got_x = lax.ppermute(to_x, "head", [(i, i ^ 2) for i in range(head_count)])
    got_y = lax.ppermute(to_y, "ctx", swap)
    (projected,) = call(
        last_kernel, [((width, rows), BF16)], (mine, got_x, got_y, got_xy), "last_sum"
    )
    return projected


def solution(mesh):
    return jax.shard_map(
        body,
        mesh=mesh,
        in_specs=(
            P("ctx", "head"),
            P("ctx", "head"),
            P("ctx", "head"),
            P("ctx", "head"),
            P(None, "head"),
            P(None, "head"),
            P(None, "head"),
            P("head", "ctx"),
            P("head", "ctx"),
            P(),
            P(),
            P("head", None),
        ),
        out_specs=P("head", "ctx"),
        check_vma=False,
    )
```

```python
import jax
import jax.numpy as jnp
from jax import lax
from jax.experimental import pallas as pl
from jax.experimental.pallas import tpu as pltpu
from jax.sharding import PartitionSpec as P

DK = 128
DV = 128
EDGE = 16
GATE_ROWS = 8
PARTS = 8
F32 = jnp.float32
BF16 = jnp.bfloat16
VMEM_LIMIT = 48 * 1024 * 1024


def dot(a, b):
    return jnp.dot(a.astype(BF16), b.astype(BF16), preferred_element_type=F32)


def dot_nt(a, b):
    dims = (((1,), (1,)), ((), ()))
    return lax.dot_general(a.astype(BF16), b.astype(BF16), dims, preferred_element_type=F32)


def exact_dot(a, b):
    return jnp.dot(a, b, precision=lax.Precision.HIGHEST, preferred_element_type=F32)


def where_y(flag, a, b):
    return jnp.where(flag == 1, a, b)


def document_counts(doc_ref, base, rows, lanes):
    down = lax.broadcasted_iota(jnp.int32, (rows + 8, lanes), 0) + (base - 8)
    along = lax.broadcasted_iota(jnp.int32, (8, rows), 1) + base
    docs = doc_ref.shape[0]

    def one(d, carried):
        start, count_down, count_along = carried
        count_down = count_down + (down >= start).astype(jnp.int32)
        count_along = count_along + (along >= start).astype(jnp.int32)
        return start + doc_ref[d], count_down, count_along

    state = (jnp.int32(0), jnp.zeros_like(down), jnp.zeros_like(along))
    if docs <= 16:
        for d in range(docs):
            state = one(d, state)
    else:
        state = lax.fori_loop(0, docs, one, state)
    return state[1], state[2]


def three_terms(value):
    high = value.astype(BF16)
    rest = value - high.astype(F32)
    middle = rest.astype(BF16)
    low = (rest - middle.astype(F32)).astype(BF16)
    return high, middle, low


class Copies:
    def __init__(self, sems):
        self.sems, self.started = sems, []

    def start(self, source, target):
        self.started.append(pltpu.make_async_copy(source, target, self.sems.at[len(self.started)]))
        self.started[-1].start()

    def wait(self, first=0, last=None):
        for one in self.started[first:last]:
            one.wait()


def half_columns(ref, which):
    width = ref.shape[1] // 2
    return pl.ds(pl.multiple_of(which * width, width), width)


def pack_kernel(q_ref, k_ref, v_ref, decay_ref, beta_ref, edge_ref, pack_ref, gates_ref, raw_gates, sems):
    other = 1 - lax.axis_index("ctx") % 2
    rows = q_ref.shape[0]
    heads = decay_ref.shape[0] // 2
    copies = Copies(sems)
    copies.start(decay_ref, raw_gates.at[0])
    copies.start(beta_ref, raw_gates.at[1])
    at = 0
    for ref in (q_ref, k_ref, v_ref):
        width = ref.shape[1] // 2
        copies.start(ref.at[pl.ds(rows - EDGE, EDGE), half_columns(ref, other)], edge_ref.at[:, pl.ds(at, width)])
        at += width
    at = 0
    for ref in (k_ref, v_ref):
        width = ref.shape[1] // 2
        copies.start(ref.at[:, half_columns(ref, other)], pack_ref.at[pl.ds(0, rows), pl.ds(at, width)])
        at += width
    pack_ref[rows : rows + GATE_ROWS, :] = jnp.zeros((GATE_ROWS, pack_ref.shape[1]), BF16)
    copies.wait(0, 2)
    decay = raw_gates[0]
    log_gamma = -(jnp.maximum(decay, 0.0) + jnp.log1p(jnp.exp(-jnp.abs(decay))))
    upper = lax.broadcasted_iota(jnp.int32, (rows, rows), 0) <= lax.broadcasted_iota(jnp.int32, (rows, rows), 1)
    sums = exact_dot(log_gamma, upper.astype(F32))
    beta = 1.0 / (1.0 + jnp.exp(-raw_gates[1]))
    at = 0
    for i, value in enumerate((sums, beta)):
        gates_ref[i * heads : i * heads + heads] = where_y(other, value[:heads], value[heads:])
        for term in three_terms(where_y(other, value[heads:], value[:heads])):
            pack_ref[rows : rows + heads, at : at + rows] = term
            at += rows
    copies.wait(2)


def early_kernel(q_ref, k_ref, v_ref, g_ref, cq_ref, ck_ref, cv_ref, doc_hbm,
                 own_edge_ref, late_ref, own_ref, weight_ref, own_gate_ref, down_ref, along_ref, doc_ref, sems):
    ctx = lax.axis_index("ctx")
    y = ctx % 2
    rows = q_ref.shape[0]
    copies = Copies(sems)
    copies.start(doc_hbm, doc_ref)
    at = 0
    for ref, weights in ((q_ref, cq_ref), (k_ref, ck_ref), (v_ref, cv_ref)):
        width = ref.shape[1] // 2
        here = pl.ds(at, width)
        copies.start(ref.at[pl.ds(rows - EDGE, EDGE), half_columns(ref, y)], own_edge_ref.at[:, here])
        copies.start(ref.at[:, half_columns(ref, y)], own_ref.at[:, here])
        copies.start(weights.at[:, half_columns(ref, y)], weight_ref.at[:, here])
        at += width
    key_width = q_ref.shape[1] // 2
    copies.start(q_ref.at[:, half_columns(q_ref, 1 - y)], late_ref.at[:, pl.ds(0, key_width)])
    copies.start(g_ref.at[:, half_columns(g_ref, 1 - y)], late_ref.at[:, pl.ds(key_width, g_ref.shape[1] // 2)])
    copies.start(g_ref.at[:, half_columns(g_ref, y)], own_gate_ref)
    copies.wait(0, 1)
    down_ref[...], along_ref[...] = document_counts(doc_ref, (ctx - y) * rows, 2 * rows, 128)
    copies.wait(1)


def conv_silu(halo, current, weight, keeps):
    rows = current.shape[0]
    padded = jnp.concatenate([halo.astype(F32)[EDGE - 8 :], current.astype(F32)], axis=0)
    margin = weight.shape[0] - 1
    summed = weight[margin : margin + 1] * padded[8:]
    for lag in range(1, margin + 1):
        summed = summed + weight[margin - lag : margin - lag + 1] * padded[8 - lag : 8 - lag + rows] * keeps[lag]
    return summed / (1.0 + jnp.exp(-summed))


def inverse_norms(vectors, axis):
    return lax.rsqrt(jnp.sum(vectors * vectors, axis=axis, keepdims=True) + 1e-6)


def odd_blocks(value, reach):
    return jnp.concatenate([value[at : at + reach] for at in range(reach, value.shape[0], 2 * reach)], axis=0)


def at_odd_blocks(value, reach):
    parts = []
    for at in range(0, value.shape[0], reach):
        parts += [jnp.zeros((reach, value.shape[1]), value.dtype), value[at : at + reach]]
    return jnp.concatenate(parts, axis=0)


def keep_masks(seg_down):
    seg = seg_down[8:]
    return [None] + [(seg_down[8 - lag : 8 - lag + seg.shape[0]] == seg).astype(F32) for lag in (1, 2, 3)]


def solve_terms(lower):
    rows = lower[0].shape[0]
    small, large = rows // 8, rows // 4
    row = lax.broadcasted_iota(jnp.int32, (rows, rows), 0)
    col = lax.broadcasted_iota(jnp.int32, (rows, rows), 1)
    power = [jnp.where(row // small == col // small, -x, 0.0) for x in lower]
    eye = (row == col).astype(F32)
    inverse = [eye + x for x in power]
    power = [x.astype(BF16) for x in power]
    power = [dot(x, x).astype(BF16) for x in power]
    reach = 4
    while reach < small:
        following = [dot(x, x).astype(BF16) for x in power]
        inverse = [x + dot(x, p) for x, p in zip(inverse, power)]
        power = following
        reach *= 2
    inverse = [x + dot(x, p) for x, p in zip(inverse, power)]
    here = (row // large == col // large) & (row // small != col // small)
    moved = [dot(odd_blocks(jnp.where(here, x, 0.0), small), i) for x, i in zip(lower, inverse)]
    moved = [dot(odd_blocks(i, small), at_odd_blocks(m, small)) for i, m in zip(inverse, moved)]
    inverse = [(i - at_odd_blocks(m, small)).astype(BF16) for i, m in zip(inverse, moved)]
    rest = [jnp.where(row // large == col // large, 0.0, -x) for x in lower]
    once = [dot(i, r).astype(BF16) for i, r in zip(inverse, rest)]
    return inverse, once


def block_terms(seg_down, seg_along, halo, k, v, weights, sums, beta):
    heads, rows = sums.shape
    key_heads = heads // 2
    seg = seg_down[8:]
    keeps = keep_masks(seg_down)
    before = seg_down[7:8]
    last = seg_down[rows + 7 : rows + 8]
    row = lax.broadcasted_iota(jnp.int32, (rows, rows), 0)
    col = lax.broadcasted_iota(jnp.int32, (rows, rows), 1)
    same = (seg == seg_along[0:1]) & (row >= col)
    stacked = jnp.concatenate([sums, beta, jnp.zeros((rows - 2 * heads, rows), F32)], axis=0)
    columns = stacked.T

    raw = [conv_silu(halo(1, g), k(g), weights(1, g), keeps) for g in range(key_heads)]
    grams = [dot_nt(key, key) for key in raw]
    raw_t = [key.T for key in raw]
    norms = [inverse_norms(key, 1) for key in raw]
    norms_t = [inverse_norms(key, 0) for key in raw_t]
    keys = [key * norm for key, norm in zip(raw, norms)]
    keys_t = [key * norm for key, norm in zip(raw_t, norms_t)]
    values = [conv_silu(halo(2, g), v(g), weights(2, g), keeps) for g in range(heads)]
    keys_t16 = [key.astype(BF16) for key in keys_t]

    lower, decays, right, start_keys, starts, ends, throughs = [], [], [], [], [], [], []
    for h in range(heads):
        g = h // 2
        down = jnp.broadcast_to(columns[:, h : h + 1], (rows, rows))
        beta_down = jnp.broadcast_to(columns[:, heads + h : heads + h + 1], (rows, rows))
        along = sums[h : h + 1]
        end = jnp.broadcast_to(columns[rows - 1 : rows, h : h + 1], (1, rows))
        decay = jnp.exp(jnp.where(same, down - along, -1e30))
        decays.append(decay)
        factor = jnp.where(row > col, beta_down * norms[g] * decay * norms_t[g], 0.0)
        lower.append(factor * grams[g])
        start = jnp.where(seg == before, jnp.exp(down), 0.0)
        starts.append(start)
        right.append(beta_down * values[h])
        start_keys.append((beta_down * start * keys[g]).astype(BF16))
        ends.append((keys_t[g] * jnp.where(seg_along[0:1] == last, jnp.exp(end - along), 0.0)).astype(BF16))
        throughs.append(jnp.where(last == before, jnp.exp(end), 0.0))

    return lower, right, start_keys, ends, throughs, decays, starts, keys_t16


def solved_with(inverse, once, right):
    result = [dot(i, r) for i, r in zip(inverse, right)]
    twice = [dot(m, m).astype(BF16) for m in once]
    result = [r + dot(m, r) for m, r in zip(once, result)]
    return [(r + dot(m, r)).astype(BF16) for m, r in zip(twice, result)], twice


def scaled_eye(scale):
    row = lax.broadcasted_iota(jnp.int32, (DK, DK), 0)
    col = lax.broadcasted_iota(jnp.int32, (DK, DK), 1)
    return jnp.where(row == col, scale, 0.0)


def query_terms(seg_down, halo, q, weights, decays, starts, keys_t):
    keeps = keep_masks(seg_down)
    queries = [conv_silu(halo(0, g), q(g), weights(0, g), keeps) for g in range(len(keys_t))]
    scores = [dot(query, key_t) for query, key_t in zip(queries, keys_t)]
    norms = [inverse_norms(query, 1) for query in queries]
    queries = [query * norm for query, norm in zip(queries, norms)]
    inside = [(scores[h // 2] * (norms[h // 2] * decays[h])).astype(BF16) for h in range(len(decays))]
    return inside, [queries[h // 2] * starts[h] for h in range(len(decays))]


def groups(heads):
    at = (0, heads // 2 * DK, heads * DK)
    return lambda which, g: slice(at[which] + g * 128, at[which] + g * 128 + 128)


def counts(down_ref, along_ref, block, rows):
    at = pl.multiple_of(block * rows, rows)
    return down_ref[pl.ds(at, rows + 8), :], along_ref[:, pl.ds(at, rows)]


def own_kernel(down_ref, along_ref, own_ref, weight_ref, gates_ref, halo_ref,
               state_ref, map_ref, solved_ref, decay_ref, start_ref, key_ref):
    rows = own_ref.shape[0]
    heads = gates_ref.shape[0] // 2
    columns = groups(heads)
    seg_down, seg_along = counts(down_ref, along_ref, lax.axis_index("ctx") % 2, rows)

    def halo(which, g):
        return halo_ref[:, columns(which, g)]

    def weights(which, g):
        return weight_ref[:, columns(which, g)]

    lower, right, start_keys, ends, throughs, decays, starts, keys_t = block_terms(
        seg_down,
        seg_along,
        halo,
        lambda g: own_ref[:, columns(1, g)],
        lambda g: own_ref[:, columns(2, g)],
        weights,
        gates_ref[0:heads],
        gates_ref[heads:],
    )
    inverse, once = solve_terms(lower)
    both = [jnp.concatenate([r.astype(BF16), k], axis=1) for r, k in zip(right, start_keys)]
    solved, _ = solved_with(inverse, once, both)
    ended = [dot(e, s) for e, s in zip(ends, solved)]
    for h in range(heads):
        state_ref[h] = ended[h][:, :DV]
        map_ref[h] = (scaled_eye(throughs[h]) - ended[h][:, DV:]).astype(BF16)
        solved_ref[h], decay_ref[h], start_ref[h] = solved[h], decays[h], starts[h]
    for g in range(heads // 2):
        key_ref[g] = keys_t[g]


def peer_halo(own_edge_ref, edge_ref, columns):
    y = lax.axis_index("ctx") % 2
    return lambda which, g: where_y(y, edge_ref[:, columns(which, g)], own_edge_ref[:, columns(which, g)])


def peer_kernel(down_ref, along_ref, pack_ref, own_edge_ref, edge_ref, weight_ref, own_state_ref, own_map_ref,
                state_ref, solved_ref, solver_ref, start_key_ref, ended_ref, passing_ref, decay_ref, start_ref, key_ref,
                pair_state_ref, *pair_map_ref):
    y = lax.axis_index("ctx") % 2
    rows = pack_ref.shape[0] - GATE_ROWS
    heads = own_state_ref.shape[0]
    columns = groups(heads)
    key_width = heads // 2 * DK
    gates = [
        sum(pack_ref[rows : rows + heads, (3 * part + i) * rows : (3 * part + i + 1) * rows].astype(F32) for i in range(3))
        for part in range(2)
    ]
    lower, right, start_keys, ends, throughs, decays, starts, keys_t = block_terms(
        *counts(down_ref, along_ref, 1 - y, rows),
        peer_halo(own_edge_ref, edge_ref, columns),
        lambda g: pack_ref[0:rows, g * DK : g * DK + DK],
        lambda g: pack_ref[0:rows, key_width + g * DV : key_width + g * DV + DV],
        lambda which, g: weight_ref[:, columns(which, g)],
        gates[0],
        gates[1],
    )
    entering = [where_y(y, jnp.zeros((DK, DV), F32), own_state_ref[h]) for h in range(heads)]
    right = [r - dot(k, e) for r, k, e in zip(right, start_keys, entering)]
    inverse, once = solve_terms(lower)
    solved, twice = solved_with(inverse, once, right)
    ended = [dot(e, s) for e, s in zip(ends, solved)]
    states = [t * e + s for t, e, s in zip(throughs, entering, ended)]
    moved = [dot(own_map_ref[h], states[h]) for h in range(heads)]
    for h in range(heads):
        pair_state_ref[h] = where_y(y, own_state_ref[h] + moved[h], states[h]).astype(BF16)
        state_ref[h] = states[h].astype(BF16)
    if pair_map_ref:
        solved_keys, _ = solved_with(inverse, once, start_keys)
        for h in range(heads):
            own_map = own_map_ref[h]
            peer_map = scaled_eye(throughs[h]) - dot(ends[h], solved_keys[h])
            pair_map_ref[0][h] = where_y(y, dot(own_map, peer_map), dot(peer_map, own_map)).astype(BF16)
    solver = (inverse, once, twice)
    for h in range(heads):
        solved_ref[h] = solved[h]
        for i in range(3):
            solver_ref[i * heads + h] = solver[i][h]
        start_key_ref[h] = start_keys[h]
        ended_ref[h] = ends[h]
        passing_ref[h : h + 1] = throughs[h]
        decay_ref[h] = decays[h]
        start_ref[h] = starts[h]
    for g in range(heads // 2):
        key_ref[g] = keys_t[g]


def passing_kernel(solver_ref, start_key_ref, ended_ref, passing_ref, own_solved_ref, decay_ref, start_ref, key_ref,
                   down_ref, along_ref, own_ref, halo_ref, conv_ref, weight_hbm,
                   solved_ref, map_ref, own_out_ref, own_through_ref, weight_ref, sems):
    depth = weight_ref.shape[0]
    copies = Copies(sems)
    part = depth // PARTS
    for i in range(PARTS):
        from_row = pl.multiple_of(lax.axis_index("ctx") % 2 * depth + i * part, part)
        copies.start(weight_hbm.at[pl.ds(from_row, part), :], weight_ref.at[pl.ds(i * part, part), :])
    heads = start_key_ref.shape[0]
    every = range(heads)
    inverse, once, twice = ([solver_ref[i * heads + h] for h in every] for i in range(3))
    solved = [dot(inverse[h], start_key_ref[h]) for h in every]
    solved = [k + dot(m, k) for m, k in zip(once, solved)]
    solved = [(k + dot(m, k)).astype(BF16) for m, k in zip(twice, solved)]
    ended = [dot(ended_ref[h], solved[h]) for h in every]
    columns = groups(heads)
    inside, start_queries = query_terms(
        counts(down_ref, along_ref, lax.axis_index("ctx") % 2, own_ref.shape[0])[0],
        lambda which, g: halo_ref[:, columns(which, g)],
        lambda g: own_ref[:, columns(0, g)],
        lambda which, g: conv_ref[:, columns(which, g)],
        [decay_ref[h] for h in every],
        [start_ref[h] for h in every],
        [key_ref[g] for g in range(heads // 2)],
    )
    result = [dot(inside[h], own_solved_ref[h]) for h in every]
    for h in every:
        own_out_ref[:, h * DV : h * DV + DV] = result[h][:, :DV]
        own_through_ref[:, h * DK : h * DK + DK] = (start_queries[h] - result[h][:, DV:]).astype(BF16)
        solved_ref[h] = solved[h]
        map_ref[h] = (scaled_eye(passing_ref[h : h + 1]) - ended[h]).astype(BF16)
    copies.wait()


def local_kernel(own_state_ref, own_map_ref, own_out_ref, own_through_ref, state_ref, map_ref, solved_ref, solved_key_ref,
                 decay_ref, start_ref, key_ref, down_ref, along_ref, late_ref, own_edge_ref, edge_ref, conv_ref, gate_ref, gain_ref,
                 out_ref, through_ref, factor_ref):
    y = lax.axis_index("ctx") % 2
    rows = own_out_ref.shape[0]
    heads = own_state_ref.shape[0]
    columns = groups(heads)
    inside, start_queries = query_terms(
        counts(down_ref, along_ref, 1 - y, rows)[0],
        peer_halo(own_edge_ref, edge_ref, columns),
        lambda g: late_ref[:, g * DK : g * DK + DK],
        lambda which, g: conv_ref[:, columns(which, g)],
        [decay_ref[h] for h in range(heads)],
        [start_ref[h] for h in range(heads)],
        [key_ref[g] for g in range(heads // 2)],
    )
    every = range(heads)
    outs = [dot(inside[h], solved_ref[h]) for h in every]
    passed = [dot(inside[h], solved_key_ref[h]) for h in every]
    state_0 = [where_y(y, state_ref[h], own_state_ref[h].astype(BF16)) for h in every]
    own_throughs = [own_through_ref[:, h * DK : h * DK + DK] for h in every]
    extra = [dot(where_y(y, own_throughs[h], start_queries[h].astype(BF16)), state_0[h]) for h in every]
    throughs = [(start_queries[h] - passed[h]).astype(BF16) for h in every]
    moved = [
        dot(where_y(y, own_throughs[h], throughs[h]), where_y(y, map_ref[h], own_map_ref[h])).astype(BF16) for h in every
    ]
    for h in every:
        lanes = slice(h * DV, h * DV + DV)
        out_ref[0:rows, lanes] = own_out_ref[:, lanes] + where_y(y, extra[h], jnp.zeros_like(extra[h]))
        out_ref[rows:, lanes] = outs[h] + where_y(y, jnp.zeros_like(extra[h]), extra[h])
        through_ref[0:rows, lanes] = where_y(y, moved[h], own_throughs[h])
        through_ref[rows:, lanes] = where_y(y, throughs[h], moved[h])
    key_width = heads // 2 * DK
    for h in every:
        lanes = slice(h * DV, h * DV + DV)
        gates = (gate_ref[:, lanes], late_ref[:, key_width + h * DV : key_width + h * DV + DV])
        for b, gate in enumerate(gates):
            gate = gate.astype(F32)
            factor_ref[b * rows : b * rows + rows, lanes] = gain_ref[...] * (gate / (1.0 + jnp.exp(-gate)))


def feature_columns(weight_ref, other_core, other_x):
    head = lax.axis_index("head")
    core, x = head % 2, head // 2
    block = (x + other_x - 2 * x * other_x) * 2 + core + other_core - 2 * core * other_core
    width = weight_ref.shape[1] // lax.axis_size("head")
    return weight_ref[:, pl.ds(pl.multiple_of(block * width, width), width)]


def mix_kernel(out_ref, through_ref, even_ref, odd_ref, factor_ref, weight_ref, mixed_ref, send_ref):
    from_even = lax.axis_index("ctx") // 2 % 2
    heads = even_ref.shape[0]
    rows = out_ref.shape[0] // 2
    every = [slice(h * DV, h * DV + DV) for h in range(heads)]
    moved = [dot(through_ref[:, lanes], where_y(from_even, even_ref[h], odd_ref[h])) for h, lanes in enumerate(every)]
    for lanes, o in zip(every, moved):
        o = out_ref[:, lanes] + o
        scale = lax.rsqrt(jnp.mean(o * o, axis=-1, keepdims=True) + 1e-6)
        mixed_ref[:, lanes] = (o * scale * factor_ref[:, lanes]).astype(BF16)
    send_ref[...] = jnp.dot(mixed_ref[rows:, :], feature_columns(weight_ref, 1, 1), preferred_element_type=F32).astype(BF16)


QUARTERS = ((0, 0), (0, 1), (1, 0))


def project_kernel(mixed_ref, weight_ref, far_ref, send_ref, keep_ref):
    rows = send_ref.shape[1]
    far_ref[...] = jnp.dot(mixed_ref[rows:, :], feature_columns(weight_ref, 0, 1), preferred_element_type=F32).astype(BF16)
    for c, to_ref in ((0, send_ref), (1, keep_ref)):
        for i, (peer, far) in enumerate(QUARTERS):
            weights = feature_columns(weight_ref, 1 - c, far)
            product = jnp.dot(mixed_ref[peer * rows : peer * rows + rows, :], weights, preferred_element_type=F32)
            to_ref[i] = product.astype(BF16)


def core_sum_kernel(keep_ref, got_ref, xy_ref):
    xy_ref[...] = (keep_ref[...].astype(F32) + got_ref[...].astype(F32)).astype(BF16)


def core_sums_kernel(keep_ref, got_ref, mine_ref, x_ref, y_ref):
    for i, ref in enumerate((mine_ref, x_ref, y_ref)):
        ref[...] = (keep_ref[i].astype(F32) + got_ref[i].astype(F32)).astype(ref.dtype)


def last_kernel(mine_ref, x_ref, y_ref, xy_ref, out_ref):
    total = mine_ref[...] + x_ref[...].astype(F32) + (y_ref[...].astype(F32) + xy_ref[...].astype(F32))
    out_ref[...] = total.T.astype(BF16)


def call(kernel, outs, args, name, hbm=(), scratch=(), flops=0, moved=0):
    space = [pl.BlockSpec(memory_space=pltpu.HBM if i in hbm else pltpu.VMEM) for i in range(len(args))]
    args = [pltpu.with_memory_space_constraint(arg, pltpu.HBM) if i in hbm else arg for i, arg in enumerate(args)]
    return pl.pallas_call(
        kernel,
        out_shape=[jax.ShapeDtypeStruct(shape, kind) for shape, kind in outs],
        in_specs=space,
        out_specs=[pl.BlockSpec(memory_space=pltpu.VMEM)] * len(outs),
        scratch_shapes=list(scratch),
        compiler_params=pltpu.CompilerParams(vmem_limit_bytes=VMEM_LIMIT),
        cost_estimate=pl.CostEstimate(flops=flops, bytes_accessed=moved, transcendentals=0),
        name=name,
    )(*args)


def body(
    query_in,
    key_in,
    value_in,
    gate_in,
    conv_query,
    conv_key,
    conv_value,
    decay_in,
    beta_in,
    norm_gain,
    doc_lengths,
    out_weight,
):
    rows = query_in.shape[0]
    ctx_count, head_count = lax.axis_size("ctx"), lax.axis_size("head")
    heads = decay_in.shape[0] // 2
    key_width, value_width = key_in.shape[1] // 2, value_in.shape[1] // 2
    half_width = 2 * key_width + value_width
    width = out_weight.shape[1] // head_count
    longest = ctx_count * rows // 4
    hops = -(-(longest - 1) // (2 * rows))

    swap = [(i, i ^ 1) for i in range(ctx_count)]
    ahead_1 = [(i, (i + 1) % ctx_count) for i in range(ctx_count)]
    even_swap = [(i, i ^ 2) for i in range(ctx_count)]
    odd_swap = [
        (c * head_count + h, (((c + 2) ^ 2) - 2) * head_count + h if 2 <= c < ctx_count - 2 else c * head_count + (h ^ 1))
        for c in range(ctx_count)
        for h in range(head_count)
    ]
    far_ahead = [
        (c * head_count + h, (c + 2) % ctx_count * head_count + h if c % 2 else c * head_count + (h ^ 1))
        for c in range(ctx_count)
        for h in range(head_count)
    ]


    edge, pack, gates = call(
        pack_kernel,
        [((EDGE, half_width), BF16), ((rows + GATE_ROWS, key_width + value_width), BF16), ((2 * heads, rows), F32)],
        (query_in, key_in, value_in, decay_in, beta_in),
        "pack",
        hbm=range(5),
        scratch=(pltpu.VMEM((2,) + decay_in.shape, F32), pltpu.SemaphoreType.DMA((7,))),
    )
    own_edge, late, own, weights, own_gate, down, along = call(
        early_kernel,
        [
            ((EDGE, half_width), BF16),
            ((rows, key_width + value_width), BF16),
            ((rows, half_width), BF16),
            ((conv_query.shape[0], half_width), F32),
            ((rows, value_width), BF16),
            ((2 * rows + 8, 128), jnp.int32),
            ((8, 2 * rows), jnp.int32),
        ],
        (query_in, key_in, value_in, gate_in, conv_query, conv_key, conv_value, doc_lengths),
        "early",
        hbm=range(8),
        scratch=(pltpu.SMEM(doc_lengths.shape, jnp.int32), pltpu.SemaphoreType.DMA((13,))),
        flops=10_000_000_000,
        moved=2_000_000,
    )
    got_edge = lax.ppermute(edge, "ctx", ahead_1)
    got_pack = lax.ppermute(pack, "ctx", swap)
    got_far_edge = lax.ppermute(own_edge, ("ctx", "head"), far_ahead)

    square = (heads, DK, DV)
    own_state, own_map, own_solved, own_decay, own_start, own_key = call(
        own_kernel,
        [
            (square, F32),
            (square, BF16),
            ((heads, rows, DK + DV), BF16),
            ((heads, rows, rows), F32),
            ((heads, rows, DK), F32),
            ((heads // 2, DK, rows), BF16),
        ],
        (down, along, own, weights, gates, got_edge),
        "own_terms",
        flops=1_000_000,
        moved=4_000_000,
    )
    late, own_map = lax.optimization_barrier((late, own_map))
    got_late = lax.ppermute(late, "ctx", swap)
    peer = call(
        peer_kernel,
        [
            (square, BF16),
            ((heads, rows, DV), BF16),
            ((3 * heads, rows, rows), BF16),
            ((heads, rows, DK), BF16),
            ((heads, DK, rows), BF16),
            ((heads, rows), F32),
            ((heads, rows, rows), F32),
            ((heads, rows, DK), F32),
            ((heads // 2, DK, rows), BF16),
            (square, BF16),
        ]
        + ([(square, BF16)] if hops > 1 else []),
        (down, along, got_pack, own_edge, got_far_edge, weights, own_state, own_map),
        "peer_terms",
        flops=2_000_000_000,
        moved=4_000_000,
    )
    end = peer[9]
    def from_earlier(value):
        return lax.ppermute(value, "ctx", even_swap), lax.ppermute(value, ("ctx", "head"), odd_swap)

    entering = from_earlier(end)
    for _ in range(hops - 1):
        earlier = jnp.where(lax.axis_index("ctx") // 2 % 2 == 1, *entering)
        moved = jnp.einsum("hij,hjk->hik", peer[10], earlier, preferred_element_type=F32)
        moved = jnp.where(lax.axis_index("ctx") < 2, 0.0, moved)
        entering = from_earlier((end.astype(F32) + moved).astype(BF16))
    state, solved, solver, start_key, ended, passing, decay, start, key = peer[:9]
    solved_key, map_, own_out, own_through, weight = call(
        passing_kernel,
        [
            (square, BF16),
            (square, BF16),
            ((rows, value_width), F32),
            ((rows, value_width), BF16),
            ((value_width, out_weight.shape[1]), BF16),
        ],
        (solver, start_key, ended, passing, own_solved, own_decay, own_start, own_key, down, along, own, got_edge, weights,
         out_weight),
        "passing",
        hbm=(13,),
        scratch=(pltpu.SemaphoreType.DMA((PARTS,)),),
        flops=1_000_000_000,
        moved=4_000_000,
    )
    out, through, factor = call(
        local_kernel,
        [((2 * rows, value_width), F32), ((2 * rows, value_width), BF16), ((2 * rows, value_width), F32)],
        (own_state, own_map, own_out, own_through, state, map_, solved, solved_key, decay, start, key, down, along, got_late,
         own_edge, got_far_edge, weights, own_gate, norm_gain.reshape(1, DV)),
        "local_outputs",
        flops=1_000_000_000,
        moved=4_000_000,
    )
    cores = [(i, i ^ 1) for i in range(head_count)]
    mixed, send_far = call(
        mix_kernel,
        [((2 * rows, value_width), BF16), ((rows, width), BF16)],
        (out, through, *entering, factor, weight),
        "mix",
    )
    got_far = lax.ppermute(send_far, "head", cores)
    keep_far, send, keep = call(
        project_kernel,
        [((rows, width), BF16), ((3, rows, width), BF16), ((3, rows, width), BF16)],
        (mixed, weight),
        "project",
        flops=2_000_000_000,
        moved=4_000_000,
    )
    send, got_far = lax.optimization_barrier((send, got_far))
    got = lax.ppermute(send, "head", cores)
    (to_xy,) = call(core_sum_kernel, [((rows, width), BF16)], (keep_far, got_far), "core_sum_xy")
    mine, to_x, to_y = call(
        core_sums_kernel,
        [((rows, width), F32), ((rows, width), BF16), ((rows, width), BF16)],
        (keep, got),
        "core_sums",
    )
    both = [
        (c * head_count + h, (c ^ 1) * head_count + (h ^ 2)) for c in range(ctx_count) for h in range(head_count)
    ]
    got_xy = lax.ppermute(to_xy, ("ctx", "head"), both)
    got_x = lax.ppermute(to_x, "head", [(i, i ^ 2) for i in range(head_count)])
    got_y = lax.ppermute(to_y, "ctx", swap)
    (projected,) = call(
        last_kernel, [((width, rows), BF16)], (mine, got_x, got_y, got_xy), "last_sum"
    )
    return projected


def solution(mesh):
    return jax.shard_map(
        body,
        mesh=mesh,
        in_specs=(
            P("ctx", "head"),
            P("ctx", "head"),
            P("ctx", "head"),
            P("ctx", "head"),
            P(None, "head"),
            P(None, "head"),
            P(None, "head"),
            P("head", "ctx"),
            P("head", "ctx"),
            P(),
            P(),
            P("head", None),
        ),
        out_specs=P("head", "ctx"),
        check_vma=False,
    )
```
